32 devices in a mesh: rep: 16 (over z, y, core), grp: 2 (over x).
Axes of the slice: x: 2, y: 2, z: 4, core: 2. Of those that a mesh axis runs over, the one named last changes fastest.
Arguments:
- clips: bfloat16 [48, 1568, 1024], P('rep', 'grp'), may hold values from -6 to 6
- clip_count: int32 [16], P('rep'), may hold values from 2 to 3, as said below
- cotangent: bfloat16 [48, 1568, 1024], P('rep', 'grp'), may hold values from -6 to 6
- norm_gain: bfloat16 [2, 1024], P(None, 'grp'), may hold values from 0.099609375 to 1.8984375
- bias_d: bfloat16 [6, 1024], P(None, 'grp'), may hold values from -1.1953125 to 1.1953125
- bias_ff: bfloat16 [4096], P('grp'), may hold values from -1.796875 to 1.796875
- w_qkv: bfloat16 [1024, 3072], P('grp'), may hold values from -0.25 to 0.25
- w_o: bfloat16 [1024, 1024], P('grp'), may hold values from -0.5 to 0.5
- w_up: bfloat16 [1024, 4096], P('grp'), may hold values from -0.1875 to 0.1875
- w_down: bfloat16 [4096, 1024], P('grp'), may hold values from -0.09375 to 0.09375
Outputs:
- block_out: bfloat16 [48, 1568, 1024], P('rep', 'grp')
- input_grad: float32 [48, 1568, 1024], P('rep', 'grp')
- grad_gain: float32 [2, 1024], P(None, 'grp')
- grad_bias: float32 [6, 1024], P(None, 'grp')
- grad_bias_ff: float32 [4096], P('grp')
- grad_qkv: float32 [1024, 3072], P('grp', 'rep')
- grad_o: float32 [1024, 1024], P('grp', 'rep')
- grad_up: float32 [1024, 4096], P('grp', 'rep')
- grad_down: float32 [4096, 1024], P('grp', 'rep')
The draws below stay inside these ranges and needn't reach their ends.
Inputs may be any that keep to these rules, and one draw needn't show every extreme that they name: Group g's live clips are its slots 0 to clip_count[g] - 1.
All inputs are finite; a program needn't handle non-finite values.
Results may differ from the reference program's by a relative error of at most 0.012.
The reference program's roundings to bfloat16 on the way count: a program that leaves them out, or rounds other values in their place, can miss the bound.
Values may be sent and summed in bfloat16 or wider, within the bound.
No kernel may reach another device: no remote copies, remote signals or barrier semaphores. Data moves between devices by JAX's collectives and lax.ppermute only.
A program may use at most 568 MiB of HBM per device.

```python
import jax
import jax.numpy as jnp
from jax import lax

D = 1024
H = 16
HD = 64
FF = 4096
SEQ = 1568
SLOTS = 3
GROUPS = 16
CLIPS = 48


def draw_clip_count(key, part):
    key = jax.random.fold_in(key, 7)
    first, second = jax.random.split(key)
    counts = jax.random.randint(first, (GROUPS,), SLOTS - 1, SLOTS + 1).astype(jnp.int32)
    order = jax.random.permutation(second, GROUPS)
    counts = counts.at[order[0]].set(SLOTS).at[order[1]].set(SLOTS - 1)
    return counts.astype(jnp.int32)


def levels(key, extent, cuts, low, top_value):
    loudness = 1.0
    for dim, parts in cuts:
        steps = jax.random.uniform(jax.random.fold_in(jax.random.fold_in(key, 6), dim), (parts,), jnp.float32, low / len(cuts), top_value / len(cuts))
        loudness = loudness * jnp.repeat(jnp.exp(steps), extent[dim] // parts).reshape((-1,) + (1,) * (len(extent) - 1 - dim))
    return loudness


def bell_draw(own_key, extent, deviation, reach, shards=(), kind=jnp.bfloat16):
    values = jax.random.normal(own_key, extent, jnp.float32) * deviation
    if len(shards) > 0:
        values = levels(own_key, extent, shards, -0.22, 0.18) * values
    return jnp.clip(values, min=-reach, max=reach).astype(kind)


def setup_inputs(seed: int = 0) -> dict:
    key_list = jax.random.split(jax.random.key(seed), 11)
    clips = bell_draw(key_list[0], (CLIPS, SEQ, D), 1.0, 6.0, ((0, 16), (1, 2)))
    clip_count = draw_clip_count(jax.random.fold_in(key_list[10], 71), 0)
    cotangent = bell_draw(key_list[2], (CLIPS, SEQ, D), 1.0, 6.0, ((0, 16), (1, 2)))
    norm_gain = jnp.clip(1.0 + 0.18 * jax.random.normal(key_list[3], (2, D), jnp.float32), 0.099609375, 1.8984375).astype(jnp.bfloat16)
    bias_d = bell_draw(key_list[4], (6, D), 0.2, 1.1953125, ((1, 2),))
    bias_ff = bell_draw(key_list[5], (FF,), 0.3, 1.796875, ((0, 2),))
    w_qkv = bell_draw(key_list[6], (D, 3 * D), (D // 2) ** -0.5, 0.25, ((0, 2),))
    w_o = bell_draw(key_list[7], (D, D), (D // 8) ** -0.5, 0.5, ((0, 2),))
    w_up = bell_draw(key_list[8], (D, FF), D ** -0.5, 0.1875, ((0, 2),))
    w_down = bell_draw(key_list[9], (FF, D), FF ** -0.5, 0.09375, ((0, 2),))
    return dict(clips=clips, clip_count=clip_count, cotangent=cotangent, norm_gain=norm_gain, bias_d=bias_d, bias_ff=bias_ff, w_qkv=w_qkv, w_o=w_o, w_up=w_up, w_down=w_down)


EPSILON = 1e-06
PRECISE = lax.Precision.HIGHEST

@jax.custom_vjp
def low(v):
    return lax.optimization_barrier(v.astype(jnp.bfloat16)).astype(jnp.float32)

@jax.custom_vjp
def low_back(v):
    return v

def low_keep(v):
    return (low(v), None)

def low_pass(kept, grad):
    return (grad,)

def back_keep(v):
    return (v, None)

def back_low(kept, grad):
    return (low(grad),)
low.defvjp(low_keep, low_pass)
low_back.defvjp(back_keep, back_low)

def product(left, right):
    return jnp.dot(left, right, precision=PRECISE, preferred_element_type=jnp.float32)

def layer_norm(values, gain, shift):
    centred = values - lax.optimization_barrier(jnp.mean(values, -1, keepdims=True))
    spread = lax.optimization_barrier(jnp.mean(centred * centred, -1, keepdims=True))
    return centred * lax.rsqrt(spread + EPSILON) * gain + shift

def block_forward(inputs, gains, biases, bias_ff, w_qkv, w_o, w_up, w_down):
    length = inputs.shape[0]
    model_width = inputs.shape[1]
    normed = low(layer_norm(inputs, gains[0], biases[0]))
    shift = jnp.concatenate([biases[1], jnp.zeros_like(biases[1]), biases[2]])
    qkv = low_back(low(product(normed, w_qkv) + shift))
    query = qkv[:, :model_width].reshape(length, H, HD)
    keys = qkv[:, model_width:2 * model_width].reshape(length, H, HD)
    values = qkv[:, 2 * model_width:].reshape(length, H, HD)
    scores = low_back(jnp.einsum('qhd,khd->hqk', query, keys, precision=PRECISE) * HD ** (-0.5))
    probs = jax.nn.softmax(scores, axis=-1)
    context = jnp.einsum('hqk,khd->qhd', low(probs), values, precision=PRECISE).reshape(length, model_width)
    context = low_back(low(context))
    hidden = inputs + low_back(product(context, w_o) + biases[3])
    normed2 = low(layer_norm(hidden, gains[1], biases[4]))
    pre = low_back(product(normed2, w_up) + bias_ff)
    active = low(jax.nn.gelu(pre, approximate=False))
    return hidden + low_back(product(active, w_down) + biases[5])

def reference(clips, clip_count, cotangent, norm_gain, bias_d, bias_ff, w_qkv, w_o, w_up, w_down):
    params = tuple((p.astype(jnp.float32) for p in (norm_gain, bias_d, bias_ff, w_qkv, w_o, w_up, w_down)))
    slots = jnp.arange(SLOTS, dtype=jnp.int32)
    live = (slots[None, :] < clip_count[:, None]).reshape(CLIPS).astype(jnp.float32)

    def scan_step(totals, item):
        inputs, incoming, weight = item
        result, pull = jax.vjp(block_forward, inputs.astype(jnp.float32), *params)
        grads = pull(incoming.astype(jnp.float32) * weight)
        totals = tuple((total + grad for total, grad in zip(totals, grads[1:])))
        return (totals, ((result * weight).astype(jnp.bfloat16), grads[0]))
    zeros = tuple((jnp.zeros_like(p) for p in params))
    totals, (outputs, input_grad) = lax.scan(scan_step, zeros, (clips, cotangent, live))
    return (outputs, input_grad) + totals
```

```python
import functools

import jax
import jax.numpy as jnp
from jax import lax
from jax.experimental import pallas as pl
from jax.experimental.pallas import tpu as pltpu
from jax.sharding import Mesh
from jax.sharding import PartitionSpec as P

H = 16
HD = 64
EPSILON = 1e-06

F32 = jnp.float32
BF = jnp.bfloat16
LOG2E = 1.4426950408889634
SCALE = HD ** -0.5
BQ = 512
TK = 224
LIMIT = 70.0


def dot(a, b, dims):
    return lax.dot_general(a, b, (dims, ((), ())), preferred_element_type=F32)


def nt(a, b):
    return dot(a, b, ((1,), (1,)))


def nn(a, b):
    return dot(a, b, ((1,), (0,)))


def tn(a, b):
    return dot(a, b, ((0,), (0,)))


def pair_mask(a):
    lane = lax.broadcasted_iota(jnp.int32, (1, 128), 1)
    return (lane < HD) if a == 0 else (lane >= HD)

def norm_peak(x, np_):
    inner = x.shape[1]
    r = lax.broadcasted_iota(jnp.int32, (inner, 128), 0)
    c = lax.broadcasted_iota(jnp.int32, (inner, 128), 1)
    ones = jnp.where(r // HD == c, 1.0, 0.0).astype(BF)
    xf = x.astype(F32)
    return jnp.max(nn((xf * xf).astype(BF), ones), axis=0, keepdims=True)

def attend_kernel(own, rec, oo, orr, ro, rr, p_out, prem_out, q_s, k_s, vt_s, o_s, r_s, fast, *, nb, np_, rem):
    half = own.shape[0]
    inner = own.shape[1] // 3
    full = 2 * half
    t = pl.program_id(0)
    last = np_ * nb

    @pl.when(t == 0)
    def _():
        q_s[:half] = own[:, :inner]
        q_s[half:] = rec[:, :inner]
        k_s[:half] = own[:, inner:2 * inner]
        k_s[half:] = rec[:, inner:2 * inner]
        row = lax.broadcasted_iota(jnp.int32, (128, 1), 0)
        for p in range(np_):
            cols = slice(2 * inner + p * 128, 2 * inner + (p + 1) * 128)
            vt = jnp.concatenate([own[:, cols], rec[:, cols]], axis=0).T
            for a in range(2):
                mine = (row < HD) if a == 0 else (row >= HD)
                vt_s[2 * p + a] = jnp.where(mine, vt, 1.0).astype(BF)
        peak = jnp.max(norm_peak(q_s[...], np_) * norm_peak(k_s[...], np_))
        fast[0] = (peak * (1.1 * SCALE * SCALE) < LIMIT * LIMIT).astype(jnp.int32)

    def store(o, rows, cols):
        oa, ob = o
        ra = 1.0 / oa[HD:]
        rb = 1.0 / ob[:HD]
        o_s[rows, cols] = jnp.concatenate([oa[:HD] * ra, ob[HD:] * rb], axis=0).T.astype(BF)
        r_s[rows, cols] = jnp.concatenate([ra, rb], axis=0).T

    def main(quick):
        p = t // nb
        b = t % nb
        rows = pl.ds(pl.multiple_of(b * BQ, BQ), BQ)
        cols = pl.ds(pl.multiple_of(p * 128, 128), 128)
        q = q_s[rows, cols]
        def weights(a):
            qa = jnp.where(pair_mask(a), q, 0.0).astype(BF)
            if quick:
                for j in range(full // TK):
                    tile = slice(j * TK, (j + 1) * TK)
                    s = nt(k_s[tile, cols], qa)
                    p_out[0, a, tile] = jnp.exp2(s * (LOG2E * SCALE)).astype(BF)
            else:
                s = nt(k_s[:, cols], qa)
                m = jnp.max(s, axis=0, keepdims=True)
                p_out[0, a] = jnp.exp2((s - m) * (LOG2E * SCALE)).astype(BF)
        weights(0)
        weights(1)
        oa = nn(vt_s[2 * p], p_out[0, 0])
        ob = nn(vt_s[2 * p + 1], p_out[0, 1])
        store((oa, ob), rows, cols)

    @pl.when((t < last) & (fast[0] == 1))
    def _():
        main(True)

    @pl.when((t < last) & (fast[0] == 0))
    def _():
        main(False)

    @pl.when(t == last)
    def _():
        if rem:
            lane = lax.broadcasted_iota(jnp.int32, (1, 256), 1)
            for u in range(np_ // 2):
                q = q_s[nb * BQ:, u * 256:(u + 1) * 256]
                qd = jnp.concatenate([jnp.where(lane // HD == h, q, 0.0).astype(BF) for h in range(4)], axis=0)
                s = nt(k_s[:, u * 256:(u + 1) * 256], qd)
                m = jnp.max(s, axis=0, keepdims=True)
                prem_out[u] = jnp.exp2((s - m) * (LOG2E * SCALE)).astype(BF)
                for v in range(2):
                    oa = nn(vt_s[4 * u + 2 * v], prem_out[u])
                    ob = nn(vt_s[4 * u + 2 * v + 1], prem_out[u])
                    ra = 1.0 / oa[HD:]
                    rb = 1.0 / ob[:HD]
                    x = jnp.concatenate([oa[:HD] * ra, ob[HD:] * rb], axis=0).T
                    r = jnp.concatenate([ra, rb], axis=0).T
                    ha, hb = 2 * v, 2 * v + 1
                    pick = lambda y: jnp.where(pair_mask(0), y[ha * rem:(ha + 1) * rem], y[hb * rem:(hb + 1) * rem])
                    cols = slice((2 * u + v) * 128, (2 * u + v + 1) * 128)
                    o_s[nb * BQ:, cols] = pick(x).astype(BF)
                    r_s[nb * BQ:, cols] = pick(r)
        oo[...] = o_s[:half]
        orr[...] = o_s[half:]
        ro[...] = r_s[:half]
        rr[...] = r_s[half:]

def attend(own, rec):
    half, w = own.shape
    inner = w // 3
    np_ = inner // 128
    full = 2 * half
    nb = full // BQ
    rem = full - nb * BQ
    last = np_ * nb
    whole = lambda shape: pl.BlockSpec(shape, lambda t: (0,) * len(shape))
    return pl.pallas_call(
        functools.partial(attend_kernel, nb=nb, np_=np_, rem=rem),
        grid=(last + 1,),
        in_specs=[whole((half, w))] * 2,
        out_specs=[whole((half, inner))] * 4 + [pl.BlockSpec((1, 2, full, BQ), lambda t: (jnp.minimum(t, last - 1), 0, 0, 0)), whole((np_ // 2, full, 4 * rem))],
        out_shape=[jax.ShapeDtypeStruct((half, inner), BF)] * 2 + [jax.ShapeDtypeStruct((half, inner), F32)] * 2
        + [jax.ShapeDtypeStruct((last, 2, full, BQ), BF), jax.ShapeDtypeStruct((np_ // 2, full, 4 * rem), BF)],
        scratch_shapes=[
            pltpu.VMEM((full, inner), BF), pltpu.VMEM((full, inner), BF), pltpu.VMEM((2 * np_, 128, full), BF),
            pltpu.VMEM((full, inner), BF), pltpu.VMEM((full, inner), F32), pltpu.SMEM((1,), jnp.int32)],
        compiler_params=pltpu.CompilerParams(vmem_limit_bytes=60 * 1024 * 1024),
    )(own, rec)


def attend_back_kernel(own, rec, do_o, do_r, o_o, o_r, r_o, r_r, e, erem, out_o, out_r,
               q_s, k_s, v_s, kt_s, do_s, pr_s, ds_s, dq_s, dk_s, dv_s, *, nb, np_, rem):
    half = own.shape[0]
    inner = own.shape[1] // 3
    full = 2 * half
    t = pl.program_id(0)
    last = np_ * nb

    @pl.when(t == 0)
    def _():
        for lo, src, d, o, r in ((0, own, do_o, o_o, r_o), (half, rec, do_r, o_r, r_r)):
            rows = slice(lo, lo + half)
            q_s[rows] = src[:, :inner]
            k_s[rows] = src[:, inner:2 * inner]
            v_s[rows] = src[:, 2 * inner:]
            dn = (d[...].astype(F32) * r[...]).astype(BF)
            do_s[rows] = dn
            pr_s[rows] = dn.astype(F32) * o[...].astype(F32)
        for p in range(np_):
            kt_s[p * 128:(p + 1) * 128] = k_s[:, p * 128:(p + 1) * 128].T
        dk_s[...] = jnp.zeros_like(dk_s)
        dv_s[...] = jnp.zeros_like(dv_s)

    @pl.when(t < last)
    def _():
        p = t // nb
        b = t % nb
        rows = pl.ds(pl.multiple_of(b * BQ, BQ), BQ)
        cols = pl.ds(pl.multiple_of(p * 128, 128), 128)
        q = q_s[rows, cols]
        dn = do_s[rows, cols]
        prod = pr_s[rows, cols].T
        qs, dns = [], []
        for a in range(2):
            qs.append(jnp.where(pair_mask(a), q, 0.0).astype(BF))
            dns.append(jnp.where(pair_mask(a), dn, 0.0).astype(BF))
        for a in range(2):
            delta = jnp.sum(prod[a * HD:(a + 1) * HD], axis=0, keepdims=True)
            for j in range(full // TK):
                tile = slice(j * TK, (j + 1) * TK)
                dp = nt(v_s[tile, cols], dns[a])
                ds_s[a, tile] = (e[0, a, tile].astype(F32) * (dp - delta)).astype(BF)
        for j in range(full // TK):
            tile = slice(j * TK, (j + 1) * TK)
            dv_s[tile, cols] += nn(e[0, 0, tile], dns[0]) + nn(e[0, 1, tile], dns[1])
        dqt = []
        for a in range(2):
            dqt.append(nn(kt_s[pl.ds(pl.multiple_of(p * 128, 128), 128)], ds_s[a])[a * HD:(a + 1) * HD])
        dq_s[rows, cols] = (jnp.concatenate(dqt, axis=0) * SCALE).T.astype(BF)
        for j in range(full // TK):
            tile = slice(j * TK, (j + 1) * TK)
            dk_s[tile, cols] += nn(ds_s[0, tile], qs[0]) + nn(ds_s[1, tile], qs[1])

    @pl.when(t == last)
    def _():
        if rem:
            lane = lax.broadcasted_iota(jnp.int32, (1, 256), 1)
            def spread(x):
                return jnp.concatenate([jnp.where(lane // HD == h, x, 0.0).astype(x.dtype) for h in range(4)], axis=0)
            for u in range(np_ // 2):
                cols = slice(u * 256, (u + 1) * 256)
                qd = spread(q_s[nb * BQ:, cols])
                dd = spread(do_s[nb * BQ:, cols])
                delta = jnp.sum(spread(pr_s[nb * BQ:, cols]).T, axis=0, keepdims=True)
                dp = nt(v_s[:, cols], dd)
                ds = (erem[u].astype(F32) * (dp - delta)).astype(BF)
                dv_s[:, cols] += nn(erem[u], dd)
                dk_s[:, cols] += nn(ds, qd)
                x = nn(kt_s[cols], ds).T * SCALE
                dq = x[:rem]
                for h in range(1, 4):
                    dq = jnp.where(lane // HD == h, x[h * rem:(h + 1) * rem], dq)
                dq_s[nb * BQ:, cols] = dq.astype(BF)
        for lo, dst in ((0, out_o), (half, out_r)):
            rows = slice(lo, lo + half)
            dst[:, :inner] = dq_s[rows]
            dst[:, inner:2 * inner] = (dk_s[rows] * SCALE).astype(BF)
            dst[:, 2 * inner:] = dv_s[rows].astype(BF)

def attend_back(own, rec, do_o, do_r, o_o, o_r, r_o, r_r, e, erem):
    half, w = own.shape
    inner = w // 3
    np_ = inner // 128
    full = 2 * half
    nb = full // BQ
    rem = full - nb * BQ
    last = np_ * nb
    whole = lambda shape, **kw: pl.BlockSpec(shape, lambda t: (0,) * len(shape), **kw)
    one = dict(pipeline_mode=pl.Buffered(1))
    return pl.pallas_call(
        functools.partial(attend_back_kernel, nb=nb, np_=np_, rem=rem),
        grid=(last + 1,),
        in_specs=[whole((half, w), **one)] * 2 + [whole((half, inner), **one)] * 6
        + [pl.BlockSpec((1, 2, full, BQ), lambda t: (jnp.minimum(t, last - 1), 0, 0, 0)), whole(erem.shape, **one)],
        out_specs=[whole((half, w), **one)] * 2,
        out_shape=[jax.ShapeDtypeStruct((half, w), BF)] * 2,
        scratch_shapes=[
            pltpu.VMEM((full, inner), BF), pltpu.VMEM((full, inner), BF), pltpu.VMEM((full, inner), BF),
            pltpu.VMEM((inner, full), BF), pltpu.VMEM((full, inner), BF), pltpu.VMEM((full, inner), F32),
            pltpu.VMEM((2, full, BQ), BF), pltpu.VMEM((full, inner), BF),
            pltpu.VMEM((full, inner), F32), pltpu.VMEM((full, inner), F32)],
        compiler_params=pltpu.CompilerParams(vmem_limit_bytes=62 * 1024 * 1024),
    )(own, rec, do_o, do_r, o_o, o_r, r_o, r_r, e, erem)


def matmul(left, right):
    return jnp.dot(left, right, preferred_element_type=jnp.float32)


def layer_norm(values, gain, shift):
    centred = values - jnp.mean(values, -1, keepdims=True)
    spread = jnp.mean(centred * centred, -1, keepdims=True)
    inverse = lax.rsqrt(spread + EPSILON)
    scaled = centred * inverse
    return (scaled, inverse, scaled * gain + shift)


def norm_back(scaled, inverse, gain, incoming):
    weighted = incoming * gain
    first = jnp.mean(weighted, -1, keepdims=True)
    second = jnp.mean(weighted * scaled, -1, keepdims=True)
    return inverse * (weighted - first - scaled * second)


def fetch_weights(shards):
    return (
        lax.all_gather(shards[0], "grp", axis=0, tiled=True),
        lax.all_gather(shards[1], "grp", axis=0, tiled=True),
        lax.all_gather(shards[2], "grp", axis=0, tiled=True),
        lax.all_gather(shards[3], "grp", axis=0, tiled=True),
        lax.all_gather(shards[4], "grp", axis=1, tiled=True),
        lax.all_gather(shards[5], "grp", axis=1, tiled=True),
        lax.all_gather(shards[6], "grp", axis=0, tiled=True),
    )


def shard_grads(weight_grads):
    return (
        lax.psum_scatter(weight_grads[0], "grp", scatter_dimension=1, tiled=True),
        lax.psum_scatter(weight_grads[1], "grp", scatter_dimension=1, tiled=True),
        lax.psum_scatter(weight_grads[2], "grp", scatter_dimension=0, tiled=True),
        lax.psum_scatter(weight_grads[3], "grp", scatter_dimension=0, tiled=True),
        lax.psum_scatter(weight_grads[4], "grp", scatter_dimension=0, tiled=True),
        lax.psum_scatter(weight_grads[5], "grp", scatter_dimension=0, tiled=True),
        lax.psum_scatter(weight_grads[6], "grp", scatter_dimension=0, tiled=True),
    )


def raw_scores(query, keys):
    rows = query.shape[0]
    length = keys.shape[0]
    return jnp.einsum(
        "qhd,khd->hqk",
        query.reshape(rows, H, HD),
        keys.reshape(length, H, HD),
        preferred_element_type=jnp.float32,
    ) * HD ** (-0.5)


def score_probs(query, keys):
    return jax.nn.softmax(raw_scores(query, keys), axis=-1)


def forward_pass(row_block, gathered):
    qkv_weight, out_weight, up_weight, down_weight, gains, biases, hidden_bias = gathered
    gain_f = gains.astype(jnp.float32)
    bias_f = biases.astype(jnp.float32)
    rows = row_block.shape[0]
    model_width = row_block.shape[1]
    inputs = row_block.astype(jnp.float32)
    scaled1, inverse1, normed = layer_norm(inputs, gain_f[0], bias_f[0])
    normed = normed.astype(jnp.bfloat16)
    shift = jnp.concatenate([bias_f[1], jnp.zeros_like(bias_f[1]), bias_f[2]])
    qkv = (matmul(normed, qkv_weight) + shift).astype(jnp.bfloat16)
    query = qkv[:, :model_width]
    key_part = qkv[:, model_width : 2 * model_width]
    value_part = qkv[:, 2 * model_width :]
    keys, values = (
        lax.all_gather(key_part, "grp", axis=0, tiled=True),
        lax.all_gather(value_part, "grp", axis=0, tiled=True),
    )
    length = keys.shape[0]
    probs = score_probs(query, keys)
    context = (
        jnp.einsum(
            "hqk,khd->qhd",
            probs.astype(jnp.bfloat16),
            values.reshape(length, H, HD),
            preferred_element_type=jnp.float32,
        )
        .reshape(rows, model_width)
        .astype(jnp.bfloat16)
    )
    hidden = inputs + matmul(context, out_weight) + bias_f[3]
    scaled2, inverse2, normed2 = layer_norm(hidden, gain_f[1], bias_f[4])
    normed2 = normed2.astype(jnp.bfloat16)
    pre = matmul(normed2, up_weight) + hidden_bias.astype(jnp.float32)
    active = jax.nn.gelu(pre, approximate=False).astype(jnp.bfloat16)
    result = hidden + matmul(active, down_weight) + bias_f[5]
    saved = (
        scaled1,
        inverse1,
        normed,
        query,
        keys,
        values,
        context,
        scaled2,
        inverse2,
        normed2,
        pre,
        active,
    )
    return (result, saved)


def backward_pass(incoming, weight, saved, gathered):
    qkv_weight, out_weight, up_weight, down_weight, gains, biases, hidden_bias = gathered
    gain_f = gains.astype(jnp.float32)
    (
        scaled1,
        inverse1,
        normed,
        query,
        keys,
        values,
        context,
        scaled2,
        inverse2,
        normed2,
        pre,
        active,
    ) = saved
    rows = query.shape[0]
    model_width = query.shape[1]
    length = keys.shape[0]
    d_out = incoming * weight.astype(jnp.bfloat16)
    d_out_f = d_out.astype(jnp.float32)
    grad_down = jnp.einsum("rf,rd->fd", active, d_out, preferred_element_type=jnp.float32)
    grad_b2 = jnp.sum(d_out_f, 0)
    d_act = jnp.einsum("rd,fd->rf", d_out, down_weight, preferred_element_type=jnp.float32)
    unused, gelu_pull = jax.vjp(lambda inputs: jax.nn.gelu(inputs, approximate=False), pre)
    d_pre = gelu_pull(d_act)[0].astype(jnp.bfloat16)
    grad_up = jnp.einsum("rd,rf->df", normed2, d_pre, preferred_element_type=jnp.float32)
    grad_hidden_bias = jnp.sum(d_pre.astype(jnp.float32), 0)
    d_norm2 = jnp.einsum("rf,df->rd", d_pre, up_weight, preferred_element_type=jnp.float32)
    d_hidden = d_out_f + norm_back(scaled2, inverse2, gain_f[1], d_norm2)
    grad_g2 = jnp.sum(d_norm2 * scaled2, 0)
    grad_beta2 = jnp.sum(d_norm2, 0)
    d_branch = d_hidden.astype(jnp.bfloat16)
    grad_out = jnp.einsum("rd,re->de", context, d_branch, preferred_element_type=jnp.float32)
    grad_bo = jnp.sum(d_branch.astype(jnp.float32), 0)
    d_context = jnp.einsum(
        "re,de->rd", d_branch, out_weight, preferred_element_type=jnp.float32
    ).astype(jnp.bfloat16)
    scores = raw_scores(query, keys)
    probs = jax.nn.softmax(scores, axis=-1)
    context_heads = d_context.reshape(rows, H, HD)
    d_probs = jnp.einsum(
        "qhd,khd->hqk",
        context_heads,
        values.reshape(length, H, HD),
        preferred_element_type=jnp.float32,
    )
    delta = jnp.sum(probs * d_probs, -1)
    d_scores = (probs * (d_probs - delta[..., None])).astype(jnp.bfloat16)
    d_query = (
        jnp.einsum(
            "hqk,khd->qhd",
            d_scores,
            keys.reshape(length, H, HD),
            preferred_element_type=jnp.float32,
        )
        * HD ** (-0.5)
    ).reshape(rows, model_width)
    d_value = jnp.einsum(
        "hqk,qhd->khd",
        probs.astype(jnp.bfloat16),
        context_heads,
        preferred_element_type=jnp.float32,
    ).reshape(length, model_width)
    d_key = (
        jnp.einsum(
            "hqk,qhd->khd", d_scores, query.reshape(rows, H, HD), preferred_element_type=jnp.float32
        )
        * HD ** (-0.5)
    ).reshape(length, model_width)
    d_key, d_value = (
        lax.psum_scatter(d_key, "grp", scatter_dimension=0, tiled=True),
        lax.psum_scatter(d_value, "grp", scatter_dimension=0, tiled=True),
    )
    d_qkv = jnp.concatenate(
        [d_query.astype(jnp.bfloat16), d_key.astype(jnp.bfloat16), d_value.astype(jnp.bfloat16)], 1
    )
    grad_qkv = jnp.einsum("rd,re->de", normed, d_qkv, preferred_element_type=jnp.float32)
    d_qkv_f = d_qkv.astype(jnp.float32)
    grad_bq = jnp.sum(d_qkv_f[:, :model_width], 0)
    grad_bv = jnp.sum(d_qkv_f[:, 2 * model_width :], 0)
    d_norm1 = jnp.einsum("re,de->rd", d_qkv, qkv_weight, preferred_element_type=jnp.float32)
    row_grad = d_hidden + norm_back(scaled1, inverse1, gain_f[0], d_norm1)
    grad_g1 = jnp.sum(d_norm1 * scaled1, 0)
    grad_beta1 = jnp.sum(d_norm1, 0)
    grad_gains = jnp.stack([grad_g1, grad_g2])
    grad_biases = jnp.stack([grad_beta1, grad_bq, grad_bv, grad_bo, grad_beta2, grad_b2])
    weight_grads = (
        grad_gains,
        grad_biases,
        grad_hidden_bias,
        grad_qkv,
        grad_out,
        grad_up,
        grad_down,
    )
    return (row_grad, weight_grads)


def plain_body(clips, clip_count, cotangent, norm_gain, bias_d, bias_ff, w_qkv, w_o, w_up, w_down):
    shards = (w_qkv, w_o, w_up, w_down, norm_gain, bias_d, bias_ff)
    number = clips.shape[0]
    outputs = []
    records = []
    actives = []
    for slot_index in range(number):
        gathered = fetch_weights(shards)
        active = (clip_count[0] > slot_index).astype(jnp.float32)
        result, saved = forward_pass(clips[slot_index], gathered)
        outputs.append((result * active).astype(jnp.bfloat16))
        records.append(saved)
        actives.append(active)
    row_grads = [None] * number
    totals = None
    for slot_index in reversed(range(number)):
        gathered = fetch_weights(shards)
        row_grad, weight_grads = backward_pass(
            cotangent[slot_index], actives[slot_index], records[slot_index], gathered
        )
        row_grads[slot_index] = row_grad
        totals = (
            weight_grads
            if totals is None
            else jax.tree.map(lambda left, right: left + right, totals, weight_grads)
        )
    totals = shard_grads(totals)
    small_sums = lax.psum((totals[0], totals[1], totals[2]), "rep")
    matrix_sums = (
        lax.psum_scatter(totals[3], "rep", scatter_dimension=1, tiled=True),
        lax.psum_scatter(totals[4], "rep", scatter_dimension=1, tiled=True),
        lax.psum_scatter(totals[5], "rep", scatter_dimension=1, tiled=True),
        lax.psum_scatter(totals[6], "rep", scatter_dimension=1, tiled=True),
    )
    return (jnp.stack(outputs), jnp.stack(row_grads)) + tuple(small_sums) + tuple(matrix_sums)


def swap_core(x):
    return lax.ppermute(x, "core", ((0, 1), (1, 0)))


def swap_owner(x, sizes):
    outer = sizes["outer"]
    pairs = []
    for k in range(outer):
        pairs += [(4 * k, 4 * k), (4 * k + 1, 4 * k + 2), (4 * k + 2, 4 * k + 1), (4 * k + 3, 4 * k + 3)]
    return lax.ppermute(x, ("outer", "core", "grp"), pairs)


def two_halves(x, core, axis=0):
    size = x.shape[axis] // 2
    return (
        lax.dynamic_slice_in_dim(x, core * size, size, axis),
        lax.dynamic_slice_in_dim(x, (1 - core) * size, size, axis),
    )


def join_halves(mine, other, core, axis=0):
    first = jnp.where(core == 0, mine, other)
    second = jnp.where(core == 0, other, mine)
    return jnp.concatenate([first, second], axis)


def scatter_blocks(grad, sizes):
    outer = sizes["outer"]
    rows, cols = grad.shape
    x = grad.astype(BF).reshape(2, rows // 2, 2 * outer, cols // (2 * outer)).transpose(2, 0, 1, 3)
    x = x.reshape(2 * outer * 2, rows // 2, cols // (2 * outer))
    return lax.psum_scatter(x, ("outer", "core", "grp"), scatter_dimension=0, tiled=True)[0].astype(F32)


def gather_rows(shard):
    core = lax.axis_index("core")
    part = shard.shape[0] // 2
    piece = lax.dynamic_slice_in_dim(shard, core * part, part, 0)
    return lax.all_gather(piece, ("grp", "core"), axis=0, tiled=True)


def body(sizes, clips, clip_count, cotangent, norm_gain, bias_d, bias_ff, w_qkv, w_o, w_up, w_down):
    core = lax.axis_index("core")
    slots, half, width = clips.shape
    inner = width // 2
    qkv_weight = gather_rows(w_qkv)
    gains = lax.all_gather(norm_gain, "grp", axis=1, tiled=True).astype(F32)
    biases = lax.all_gather(bias_d, "grp", axis=1, tiled=True).astype(F32)
    bias_hidden = lax.all_gather(bias_ff, "grp", axis=0, tiled=True).astype(F32)
    count = swap_owner(clip_count, sizes)[0]
    out_weight = gather_rows(w_o)
    up_weight = gather_rows(w_up)
    down_weight = gather_rows(w_down)

    qkv_parts = [two_halves(qkv_weight[:, i * width : (i + 1) * width], core, 1) for i in range(3)]
    qkv_mine = jnp.concatenate([part[0] for part in qkv_parts], 1)
    qkv_other = jnp.concatenate([part[1] for part in qkv_parts], 1)
    zero = jnp.zeros((inner,), F32)
    q_shift = two_halves(biases[1], core)
    v_shift = two_halves(biases[2], core)
    shift_mine = jnp.concatenate([q_shift[0], zero, v_shift[0]])
    shift_other = jnp.concatenate([q_shift[1], zero, v_shift[1]])
    out_mine, out_other = two_halves(out_weight, core)

    inputs, normed, scaled1, inverse1 = [], [], [], []
    saved, context_mine, context_other = [], [], []
    for s in range(slots):
        block = swap_owner(clips[s], sizes).astype(F32)
        scaled, inverse, norm = layer_norm(block, gains[0], biases[0])
        norm = norm.astype(BF)
        other = (nn(norm, qkv_other) + shift_other).astype(BF)
        received = swap_core(other)
        mine = (nn(norm, qkv_mine) + shift_mine).astype(BF)
        here, there, r_here, r_there, weights, weights_rem = attend(mine, received)
        context_mine.append(here)
        context_other.append(swap_core(there))
        saved.append((mine, received, here, there, r_here, r_there, weights, weights_rem))
        inputs.append(block)
        normed.append(norm)
        scaled1.append(scaled)
        inverse1.append(inverse)
    live = jnp.repeat((count > jnp.arange(slots)).astype(F32), half)[:, None]
    cot = jnp.concatenate([swap_owner(cotangent[s], sizes) for s in range(slots)])
    inputs = jnp.concatenate(inputs)
    normed = jnp.concatenate(normed)
    scaled1 = jnp.concatenate(scaled1)
    inverse1 = jnp.concatenate(inverse1)
    context_mine = jnp.concatenate(context_mine)
    context_other = jnp.concatenate(context_other)

    hidden = inputs + nn(context_mine, out_mine) + nn(context_other, out_other) + biases[3]
    scaled2, inverse2, normed2 = layer_norm(hidden, gains[1], biases[4])
    normed2 = normed2.astype(BF)
    pre = nn(normed2, up_weight) + bias_hidden
    active = jax.nn.gelu(pre, approximate=False).astype(BF)
    result = ((hidden + nn(active, down_weight) + biases[5]) * live).astype(BF)
    block_out = jnp.stack([swap_owner(result[s * half : (s + 1) * half], sizes) for s in range(slots)])

    d_out = cot * live.astype(BF)
    d_out_f = d_out.astype(F32)
    grad_down = scatter_blocks(tn(active, d_out), sizes)
    grad_b2 = jnp.sum(d_out_f, 0)
    d_act = nt(d_out, down_weight)
    unused, gelu_pull = jax.vjp(lambda x: jax.nn.gelu(x, approximate=False), pre)
    d_pre = gelu_pull(d_act)[0].astype(BF)
    grad_up = scatter_blocks(tn(normed2, d_pre), sizes)
    grad_bias_hidden = jnp.sum(d_pre.astype(F32), 0)
    d_norm2 = nt(d_pre, up_weight)
    d_hidden = d_out_f + norm_back(scaled2, inverse2, gains[1], d_norm2)
    grad_g2 = jnp.sum(d_norm2 * scaled2, 0)
    grad_beta2 = jnp.sum(d_norm2, 0)
    d_branch = d_hidden.astype(BF)
    grad_bo = jnp.sum(d_branch.astype(F32), 0)
    d_context_other = swap_core(nt(d_branch, out_other).astype(BF))
    d_context_mine = nt(d_branch, out_mine).astype(BF)
    grad_out = scatter_blocks(
        join_halves(tn(context_mine, d_branch), tn(context_other, d_branch), core), sizes
    )

    d_mine, d_other = [], []
    for s in range(slots):
        rows = slice(s * half, (s + 1) * half)
        mine, received, here, there, r_here, r_there, weights, weights_rem = saved[s]
        d_here, d_there = attend_back(
            mine, received, d_context_mine[rows], d_context_other[rows], here, there, r_here, r_there, weights, weights_rem
        )
        d_mine.append(d_here)
        d_other.append(swap_core(d_there))
    d_mine = jnp.concatenate(d_mine)
    d_other = jnp.concatenate(d_other)
    d_norm1 = nt(d_mine, qkv_mine) + nt(d_other, qkv_other)
    grad_mine = tn(normed, d_mine)
    grad_other = tn(normed, d_other)
    grad_qkv = scatter_blocks(
        jnp.concatenate(
            [
                join_halves(grad_mine[:, i * inner : (i + 1) * inner], grad_other[:, i * inner : (i + 1) * inner], core, 1)
                for i in range(3)
            ],
            1,
        ),
        sizes,
    )
    sum_mine = jnp.sum(d_mine.astype(F32), 0)
    sum_other = jnp.sum(d_other.astype(F32), 0)
    grad_bq = join_halves(sum_mine[:inner], sum_other[:inner], core)
    grad_bv = join_halves(sum_mine[2 * inner :], sum_other[2 * inner :], core)
    row_grad = (d_hidden + norm_back(scaled1, inverse1, gains[0], d_norm1)).astype(BF)
    grad_g1 = jnp.sum(d_norm1 * scaled1, 0)
    grad_beta1 = jnp.sum(d_norm1, 0)
    input_grad = jnp.stack(
        [swap_owner(row_grad[s * half : (s + 1) * half], sizes).astype(F32) for s in range(slots)]
    )
    small = jnp.concatenate(
        [
            jnp.stack([grad_g1, grad_g2, grad_beta1, grad_bq, grad_bv, grad_bo, grad_beta2, grad_b2]),
            grad_bias_hidden.reshape(4, width),
        ]
    )
    small = lax.psum(small, ("outer", "core", "grp"))
    x = lax.axis_index("grp")
    columns = lax.dynamic_slice_in_dim(small[:8], x * inner, inner, 1)
    hidden_part = lax.dynamic_slice_in_dim(small[8:], 2 * x, 2, 0).reshape(-1)
    return (block_out, input_grad, columns[:2], columns[2:], hidden_part, grad_qkv, grad_out, grad_up, grad_down)


def solution(mesh):
    in_specs = (
        P("rep", "grp", None),
        P("rep"),
        P("rep", "grp", None),
        P(None, "grp"),
        P(None, "grp"),
        P("grp"),
        P("grp", None),
        P("grp", None),
        P("grp", None),
        P("grp", None),
    )
    out_specs = (
        P("rep", "grp", None),
        P("rep", "grp", None),
        P(None, "grp"),
        P(None, "grp"),
        P("grp"),
        P("grp", "rep"),
        P("grp", "rep"),
        P("grp", "rep"),
        P("grp", "rep"),
    )
    if mesh.shape["grp"] != 2:
        return jax.shard_map(plain_body, mesh=mesh, in_specs=in_specs, out_specs=out_specs, check_vma=False)
    outer = mesh.shape["rep"] // 2
    split = Mesh(mesh.devices.reshape(outer, 2, 2), ("outer", "core", "grp"))
    rep = lambda spec: P(*[("outer", "core") if axis == "rep" else axis for axis in spec])
    return jax.shard_map(
        functools.partial(body, {"outer": outer}),
        mesh=split,
        in_specs=tuple(rep(spec) for spec in in_specs),
        out_specs=tuple(rep(spec) for spec in out_specs),
        check_vma=False,
    )
```

```python
import functools

import jax
import jax.numpy as jnp
from jax import lax
from jax.experimental import pallas as pl
from jax.experimental.pallas import tpu as pltpu
from jax.sharding import Mesh
from jax.sharding import PartitionSpec as P

H = 16
HD = 64
EPSILON = 1e-06

F32 = jnp.float32
BF = jnp.bfloat16
LOG2E = 1.4426950408889634
SCALE = HD ** -0.5
AXES = ("z", "mid", "core", "grp")
BQ = 512
TK = 224
COST = 0.4
LIMIT = 70.0


def dot(a, b, dims):
    return lax.dot_general(a, b, (dims, ((), ())), preferred_element_type=F32)


def nt(a, b):
    return dot(a, b, ((1,), (1,)))


def nn(a, b):
    return dot(a, b, ((1,), (0,)))


def tn(a, b):
    return dot(a, b, ((0,), (0,)))


def pair_mask(a):
    lane = lax.broadcasted_iota(jnp.int32, (1, 128), 1)
    return (lane < HD) if a == 0 else (lane >= HD)

def norm_peak(x, np_):
    inner = x.shape[1]
    r = lax.broadcasted_iota(jnp.int32, (inner, 128), 0)
    c = lax.broadcasted_iota(jnp.int32, (inner, 128), 1)
    ones = jnp.where(r // HD == c, 1.0, 0.0).astype(BF)
    xf = x.astype(F32)
    return jnp.max(nn((xf * xf).astype(BF), ones), axis=0, keepdims=True)

def attend_kernel(own, rec, oo, orr, ro, rr, p_out, prem_out, q_s, k_s, vt_s, o_s, r_s, fast, *, nb, np_, rem):
    half = own.shape[0]
    inner = own.shape[1] // 3
    full = 2 * half
    t = pl.program_id(0)
    last = np_ * nb

    @pl.when(t == 0)
    def _():
        q_s[:half] = own[:, :inner]
        q_s[half:] = rec[:, :inner]
        k_s[:half] = own[:, inner:2 * inner]
        k_s[half:] = rec[:, inner:2 * inner]
        row = lax.broadcasted_iota(jnp.int32, (128, 1), 0)
        for p in range(np_):
            cols = slice(2 * inner + p * 128, 2 * inner + (p + 1) * 128)
            vt = jnp.concatenate([own[:, cols], rec[:, cols]], axis=0).T
            for a in range(2):
                mine = (row < HD) if a == 0 else (row >= HD)
                vt_s[2 * p + a] = jnp.where(mine, vt, 1.0).astype(BF)
        peak = jnp.max(norm_peak(q_s[...], np_) * norm_peak(k_s[...], np_))
        fast[0] = (peak * (1.1 * SCALE * SCALE) < LIMIT * LIMIT).astype(jnp.int32)

    def store(o, rows, cols):
        oa, ob = o
        ra = 1.0 / oa[HD:]
        rb = 1.0 / ob[:HD]
        o_s[rows, cols] = jnp.concatenate([oa[:HD] * ra, ob[HD:] * rb], axis=0).T.astype(BF)
        r_s[rows, cols] = jnp.concatenate([ra, rb], axis=0).T

    def main(quick):
        p = t // nb
        b = t % nb
        rows = pl.ds(pl.multiple_of(b * BQ, BQ), BQ)
        cols = pl.ds(pl.multiple_of(p * 128, 128), 128)
        q = q_s[rows, cols]
        def weights(a):
            qa = jnp.where(pair_mask(a), q, 0.0).astype(BF)
            if quick:
                for j in range(full // TK):
                    tile = slice(j * TK, (j + 1) * TK)
                    s = nt(k_s[tile, cols], qa)
                    p_out[0, a, tile] = jnp.exp2(s * (LOG2E * SCALE)).astype(BF)
            else:
                s = nt(k_s[:, cols], qa)
                m = jnp.max(s, axis=0, keepdims=True)
                p_out[0, a] = jnp.exp2((s - m) * (LOG2E * SCALE)).astype(BF)
        weights(0)
        weights(1)
        oa = nn(vt_s[2 * p], p_out[0, 0])
        ob = nn(vt_s[2 * p + 1], p_out[0, 1])
        store((oa, ob), rows, cols)

    @pl.when((t < last) & (fast[0] == 1))
    def _():
        main(True)

    @pl.when((t < last) & (fast[0] == 0))
    def _():
        main(False)

    @pl.when(t == last)
    def _():
        if rem:
            lane = lax.broadcasted_iota(jnp.int32, (1, 256), 1)
            for u in range(np_ // 2):
                q = q_s[nb * BQ:, u * 256:(u + 1) * 256]
                qd = jnp.concatenate([jnp.where(lane // HD == h, q, 0.0).astype(BF) for h in range(4)], axis=0)
                s = nt(k_s[:, u * 256:(u + 1) * 256], qd)
                m = jnp.max(s, axis=0, keepdims=True)
                prem_out[u] = jnp.exp2((s - m) * (LOG2E * SCALE)).astype(BF)
                for v in range(2):
                    oa = nn(vt_s[4 * u + 2 * v], prem_out[u])
                    ob = nn(vt_s[4 * u + 2 * v + 1], prem_out[u])
                    ra = 1.0 / oa[HD:]
                    rb = 1.0 / ob[:HD]
                    x = jnp.concatenate([oa[:HD] * ra, ob[HD:] * rb], axis=0).T
                    r = jnp.concatenate([ra, rb], axis=0).T
                    ha, hb = 2 * v, 2 * v + 1
                    pick = lambda y: jnp.where(pair_mask(0), y[ha * rem:(ha + 1) * rem], y[hb * rem:(hb + 1) * rem])
                    cols = slice((2 * u + v) * 128, (2 * u + v + 1) * 128)
                    o_s[nb * BQ:, cols] = pick(x).astype(BF)
                    r_s[nb * BQ:, cols] = pick(r)
        oo[...] = o_s[:half]
        orr[...] = o_s[half:]
        ro[...] = r_s[:half]
        rr[...] = r_s[half:]

def attend(own, rec):
    half, w = own.shape
    inner = w // 3
    np_ = inner // 128
    full = 2 * half
    nb = full // BQ
    rem = full - nb * BQ
    last = np_ * nb
    whole = lambda shape: pl.BlockSpec(shape, lambda t: (0,) * len(shape))
    return pl.pallas_call(
        functools.partial(attend_kernel, nb=nb, np_=np_, rem=rem),
        grid=(last + 1,),
        in_specs=[whole((half, w))] * 2,
        out_specs=[whole((half, inner))] * 4 + [pl.BlockSpec((1, 2, full, BQ), lambda t: (jnp.minimum(t, last - 1), 0, 0, 0)), whole((np_ // 2, full, 4 * rem))],
        out_shape=[jax.ShapeDtypeStruct((half, inner), BF)] * 2 + [jax.ShapeDtypeStruct((half, inner), F32)] * 2
        + [jax.ShapeDtypeStruct((last, 2, full, BQ), BF), jax.ShapeDtypeStruct((np_ // 2, full, 4 * rem), BF)],
        scratch_shapes=[
            pltpu.VMEM((full, inner), BF), pltpu.VMEM((full, inner), BF), pltpu.VMEM((2 * np_, 128, full), BF),
            pltpu.VMEM((full, inner), BF), pltpu.VMEM((full, inner), F32), pltpu.SMEM((1,), jnp.int32)],
        cost_estimate=pl.CostEstimate(flops=int(3.5e10 * COST), bytes_accessed=0, transcendentals=0),
        compiler_params=pltpu.CompilerParams(vmem_limit_bytes=60 * 1024 * 1024),
    )(own, rec)


def attend_back_kernel(own, rec, do_o, do_r, o_o, o_r, r_o, r_r, e, erem, out_o, out_r,
               q_s, k_s, v_s, kt_s, do_s, pr_s, ds_s, dq_s, dk_s, dv_s, *, nb, np_, rem):
    half = own.shape[0]
    inner = own.shape[1] // 3
    full = 2 * half
    t = pl.program_id(0)
    last = np_ * nb

    @pl.when(t == 0)
    def _():
        for lo, src, d, o, r in ((0, own, do_o, o_o, r_o), (half, rec, do_r, o_r, r_r)):
            rows = slice(lo, lo + half)
            q_s[rows] = src[:, :inner]
            k_s[rows] = src[:, inner:2 * inner]
            v_s[rows] = src[:, 2 * inner:]
            dn = (d[...].astype(F32) * r[...]).astype(BF)
            do_s[rows] = dn
            pr_s[rows] = dn.astype(F32) * o[...].astype(F32)
        for p in range(np_):
            kt_s[p * 128:(p + 1) * 128] = k_s[:, p * 128:(p + 1) * 128].T
        dk_s[...] = jnp.zeros_like(dk_s)
        dv_s[...] = jnp.zeros_like(dv_s)

    @pl.when(t < last)
    def _():
        p = t // nb
        b = t % nb
        rows = pl.ds(pl.multiple_of(b * BQ, BQ), BQ)
        cols = pl.ds(pl.multiple_of(p * 128, 128), 128)
        q = q_s[rows, cols]
        dn = do_s[rows, cols]
        prod = pr_s[rows, cols].T
        qs, dns = [], []
        for a in range(2):
            qs.append(jnp.where(pair_mask(a), q, 0.0).astype(BF))
            dns.append(jnp.where(pair_mask(a), dn, 0.0).astype(BF))
        for a in range(2):
            delta = jnp.sum(prod[a * HD:(a + 1) * HD], axis=0, keepdims=True)
            for j in range(full // TK):
                tile = slice(j * TK, (j + 1) * TK)
                dp = nt(v_s[tile, cols], dns[a])
                ds_s[a, tile] = (e[0, a, tile].astype(F32) * (dp - delta)).astype(BF)
        for j in range(full // TK):
            tile = slice(j * TK, (j + 1) * TK)
            dv_s[tile, cols] += nn(e[0, 0, tile], dns[0]) + nn(e[0, 1, tile], dns[1])
        dqt = []
        for a in range(2):
            dqt.append(nn(kt_s[pl.ds(pl.multiple_of(p * 128, 128), 128)], ds_s[a])[a * HD:(a + 1) * HD])
        dq_s[rows, cols] = (jnp.concatenate(dqt, axis=0) * SCALE).T.astype(BF)
        for j in range(full // TK):
            tile = slice(j * TK, (j + 1) * TK)
            dk_s[tile, cols] += nn(ds_s[0, tile], qs[0]) + nn(ds_s[1, tile], qs[1])

    @pl.when(t == last)
    def _():
        if rem:
            lane = lax.broadcasted_iota(jnp.int32, (1, 256), 1)
            def spread(x):
                return jnp.concatenate([jnp.where(lane // HD == h, x, 0.0).astype(x.dtype) for h in range(4)], axis=0)
            for u in range(np_ // 2):
                cols = slice(u * 256, (u + 1) * 256)
                qd = spread(q_s[nb * BQ:, cols])
                dd = spread(do_s[nb * BQ:, cols])
                delta = jnp.sum(spread(pr_s[nb * BQ:, cols]).T, axis=0, keepdims=True)
                dp = nt(v_s[:, cols], dd)
                ds = (erem[u].astype(F32) * (dp - delta)).astype(BF)
                dv_s[:, cols] += nn(erem[u], dd)
                dk_s[:, cols] += nn(ds, qd)
                x = nn(kt_s[cols], ds).T * SCALE
                dq = x[:rem]
                for h in range(1, 4):
                    dq = jnp.where(lane // HD == h, x[h * rem:(h + 1) * rem], dq)
                dq_s[nb * BQ:, cols] = dq.astype(BF)
        for lo, dst in ((0, out_o), (half, out_r)):
            rows = slice(lo, lo + half)
            dst[:, :inner] = dq_s[rows]
            dst[:, inner:2 * inner] = (dk_s[rows] * SCALE).astype(BF)
            dst[:, 2 * inner:] = dv_s[rows].astype(BF)

def attend_back(slot, own, rec, do_o, do_r, o_o, o_r, r_o, r_r, e, erem):
    half, w = own.shape
    inner = w // 3
    np_ = inner // 128
    full = 2 * half
    nb = full // BQ
    rem = full - nb * BQ
    last = np_ * nb
    whole = lambda shape, **kw: pl.BlockSpec(shape, lambda t: (0,) * len(shape), **kw)
    one = dict(pipeline_mode=pl.Buffered(1))
    return pl.pallas_call(
        functools.partial(attend_back_kernel, nb=nb, np_=np_, rem=rem),
        grid=(last + 1,),
        in_specs=[whole((half, w), **one)] * 2
        + [whole((half, inner), **one), pl.BlockSpec((None, half, inner), lambda t: (slot, 0, 0), **one)]
        + [whole((half, inner), **one)] * 4
        + [pl.BlockSpec((1, 2, full, BQ), lambda t: (jnp.minimum(t, last - 1), 0, 0, 0)), whole(erem.shape, **one)],
        out_specs=[whole((half, w), **one)] * 2,
        out_shape=[jax.ShapeDtypeStruct((half, w), BF)] * 2,
        scratch_shapes=[
            pltpu.VMEM((full, inner), BF), pltpu.VMEM((full, inner), BF), pltpu.VMEM((full, inner), BF),
            pltpu.VMEM((inner, full), BF), pltpu.VMEM((full, inner), BF), pltpu.VMEM((full, inner), F32),
            pltpu.VMEM((2, full, BQ), BF), pltpu.VMEM((full, inner), BF),
            pltpu.VMEM((full, inner), F32), pltpu.VMEM((full, inner), F32)],
        cost_estimate=pl.CostEstimate(flops=int(6e10 * COST), bytes_accessed=0, transcendentals=0),
        compiler_params=pltpu.CompilerParams(vmem_limit_bytes=62 * 1024 * 1024),
    )(own, rec, do_o, do_r, o_o, o_r, r_o, r_r, e, erem)


def matmul(left, right):
    return jnp.dot(left, right, preferred_element_type=jnp.float32)


def layer_norm(values, gain, shift):
    centred = values - jnp.mean(values, -1, keepdims=True)
    spread = jnp.mean(centred * centred, -1, keepdims=True)
    inverse = lax.rsqrt(spread + EPSILON)
    scaled = centred * inverse
    return (scaled, inverse, scaled * gain + shift)


def norm_back(scaled, inverse, gain, incoming):
    weighted = incoming * gain
    first = jnp.mean(weighted, -1, keepdims=True)
    second = jnp.mean(weighted * scaled, -1, keepdims=True)
    return inverse * (weighted - first - scaled * second)


def fetch_weights(shards):
    return (
        lax.all_gather(shards[0], "grp", axis=0, tiled=True),
        lax.all_gather(shards[1], "grp", axis=0, tiled=True),
        lax.all_gather(shards[2], "grp", axis=0, tiled=True),
        lax.all_gather(shards[3], "grp", axis=0, tiled=True),
        lax.all_gather(shards[4], "grp", axis=1, tiled=True),
        lax.all_gather(shards[5], "grp", axis=1, tiled=True),
        lax.all_gather(shards[6], "grp", axis=0, tiled=True),
    )


def shard_grads(weight_grads):
    return (
        lax.psum_scatter(weight_grads[0], "grp", scatter_dimension=1, tiled=True),
        lax.psum_scatter(weight_grads[1], "grp", scatter_dimension=1, tiled=True),
        lax.psum_scatter(weight_grads[2], "grp", scatter_dimension=0, tiled=True),
        lax.psum_scatter(weight_grads[3], "grp", scatter_dimension=0, tiled=True),
        lax.psum_scatter(weight_grads[4], "grp", scatter_dimension=0, tiled=True),
        lax.psum_scatter(weight_grads[5], "grp", scatter_dimension=0, tiled=True),
        lax.psum_scatter(weight_grads[6], "grp", scatter_dimension=0, tiled=True),
    )


def raw_scores(query, keys):
    rows = query.shape[0]
    length = keys.shape[0]
    return jnp.einsum(
        "qhd,khd->hqk",
        query.reshape(rows, H, HD),
        keys.reshape(length, H, HD),
        preferred_element_type=jnp.float32,
    ) * HD ** (-0.5)


def score_probs(query, keys):
    return jax.nn.softmax(raw_scores(query, keys), axis=-1)


def forward_pass(row_block, gathered):
    qkv_weight, out_weight, up_weight, down_weight, gains, biases, hidden_bias = gathered
    gain_f = gains.astype(jnp.float32)
    bias_f = biases.astype(jnp.float32)
    rows = row_block.shape[0]
    model_width = row_block.shape[1]
    inputs = row_block.astype(jnp.float32)
    scaled1, inverse1, normed = layer_norm(inputs, gain_f[0], bias_f[0])
    normed = normed.astype(jnp.bfloat16)
    shift = jnp.concatenate([bias_f[1], jnp.zeros_like(bias_f[1]), bias_f[2]])
    qkv = (matmul(normed, qkv_weight) + shift).astype(jnp.bfloat16)
    query = qkv[:, :model_width]
    key_part = qkv[:, model_width : 2 * model_width]
    value_part = qkv[:, 2 * model_width :]
    keys, values = (
        lax.all_gather(key_part, "grp", axis=0, tiled=True),
        lax.all_gather(value_part, "grp", axis=0, tiled=True),
    )
    length = keys.shape[0]
    probs = score_probs(query, keys)
    context = (
        jnp.einsum(
            "hqk,khd->qhd",
            probs.astype(jnp.bfloat16),
            values.reshape(length, H, HD),
            preferred_element_type=jnp.float32,
        )
        .reshape(rows, model_width)
        .astype(jnp.bfloat16)
    )
    hidden = inputs + matmul(context, out_weight) + bias_f[3]
    scaled2, inverse2, normed2 = layer_norm(hidden, gain_f[1], bias_f[4])
    normed2 = normed2.astype(jnp.bfloat16)
    pre = matmul(normed2, up_weight) + hidden_bias.astype(jnp.float32)
    active = jax.nn.gelu(pre, approximate=False).astype(jnp.bfloat16)
    result = hidden + matmul(active, down_weight) + bias_f[5]
    saved = (
        scaled1,
        inverse1,
        normed,
        query,
        keys,
        values,
        context,
        scaled2,
        inverse2,
        normed2,
        pre,
        active,
    )
    return (result, saved)


def backward_pass(incoming, weight, saved, gathered):
    qkv_weight, out_weight, up_weight, down_weight, gains, biases, hidden_bias = gathered
    gain_f = gains.astype(jnp.float32)
    (
        scaled1,
        inverse1,
        normed,
        query,
        keys,
        values,
        context,
        scaled2,
        inverse2,
        normed2,
        pre,
        active,
    ) = saved
    rows = query.shape[0]
    model_width = query.shape[1]
    length = keys.shape[0]
    d_out = incoming * weight.astype(jnp.bfloat16)
    d_out_f = d_out.astype(jnp.float32)
    grad_down = jnp.einsum("rf,rd->fd", active, d_out, preferred_element_type=jnp.float32)
    grad_b2 = jnp.sum(d_out_f, 0)
    d_act = jnp.einsum("rd,fd->rf", d_out, down_weight, preferred_element_type=jnp.float32)
    unused, gelu_pull = jax.vjp(lambda inputs: jax.nn.gelu(inputs, approximate=False), pre)
    d_pre = gelu_pull(d_act)[0].astype(jnp.bfloat16)
    grad_up = jnp.einsum("rd,rf->df", normed2, d_pre, preferred_element_type=jnp.float32)
    grad_hidden_bias = jnp.sum(d_pre.astype(jnp.float32), 0)
    d_norm2 = jnp.einsum("rf,df->rd", d_pre, up_weight, preferred_element_type=jnp.float32)
    d_hidden = d_out_f + norm_back(scaled2, inverse2, gain_f[1], d_norm2)
    grad_g2 = jnp.sum(d_norm2 * scaled2, 0)
    grad_beta2 = jnp.sum(d_norm2, 0)
    d_branch = d_hidden.astype(jnp.bfloat16)
    grad_out = jnp.einsum("rd,re->de", context, d_branch, preferred_element_type=jnp.float32)
    grad_bo = jnp.sum(d_branch.astype(jnp.float32), 0)
    d_context = jnp.einsum(
        "re,de->rd", d_branch, out_weight, preferred_element_type=jnp.float32
    ).astype(jnp.bfloat16)
    scores = raw_scores(query, keys)
    probs = jax.nn.softmax(scores, axis=-1)
    context_heads = d_context.reshape(rows, H, HD)
    d_probs = jnp.einsum(
        "qhd,khd->hqk",
        context_heads,
        values.reshape(length, H, HD),
        preferred_element_type=jnp.float32,
    )
    delta = jnp.sum(probs * d_probs, -1)
    d_scores = (probs * (d_probs - delta[..., None])).astype(jnp.bfloat16)
    d_query = (
        jnp.einsum(
            "hqk,khd->qhd",
            d_scores,
            keys.reshape(length, H, HD),
            preferred_element_type=jnp.float32,
        )
        * HD ** (-0.5)
    ).reshape(rows, model_width)
    d_value = jnp.einsum(
        "hqk,qhd->khd",
        probs.astype(jnp.bfloat16),
        context_heads,
        preferred_element_type=jnp.float32,
    ).reshape(length, model_width)
    d_key = (
        jnp.einsum(
            "hqk,qhd->khd", d_scores, query.reshape(rows, H, HD), preferred_element_type=jnp.float32
        )
        * HD ** (-0.5)
    ).reshape(length, model_width)
    d_key, d_value = (
        lax.psum_scatter(d_key, "grp", scatter_dimension=0, tiled=True),
        lax.psum_scatter(d_value, "grp", scatter_dimension=0, tiled=True),
    )
    d_qkv = jnp.concatenate(
        [d_query.astype(jnp.bfloat16), d_key.astype(jnp.bfloat16), d_value.astype(jnp.bfloat16)], 1
    )
    grad_qkv = jnp.einsum("rd,re->de", normed, d_qkv, preferred_element_type=jnp.float32)
    d_qkv_f = d_qkv.astype(jnp.float32)
    grad_bq = jnp.sum(d_qkv_f[:, :model_width], 0)
    grad_bv = jnp.sum(d_qkv_f[:, 2 * model_width :], 0)
    d_norm1 = jnp.einsum("re,de->rd", d_qkv, qkv_weight, preferred_element_type=jnp.float32)
    row_grad = d_hidden + norm_back(scaled1, inverse1, gain_f[0], d_norm1)
    grad_g1 = jnp.sum(d_norm1 * scaled1, 0)
    grad_beta1 = jnp.sum(d_norm1, 0)
    grad_gains = jnp.stack([grad_g1, grad_g2])
    grad_biases = jnp.stack([grad_beta1, grad_bq, grad_bv, grad_bo, grad_beta2, grad_b2])
    weight_grads = (
        grad_gains,
        grad_biases,
        grad_hidden_bias,
        grad_qkv,
        grad_out,
        grad_up,
        grad_down,
    )
    return (row_grad, weight_grads)


def plain_body(clips, clip_count, cotangent, norm_gain, bias_d, bias_ff, w_qkv, w_o, w_up, w_down):
    shards = (w_qkv, w_o, w_up, w_down, norm_gain, bias_d, bias_ff)
    number = clips.shape[0]
    outputs = []
    records = []
    actives = []
    for slot_index in range(number):
        gathered = fetch_weights(shards)
        active = (clip_count[0] > slot_index).astype(jnp.float32)
        result, saved = forward_pass(clips[slot_index], gathered)
        outputs.append((result * active).astype(jnp.bfloat16))
        records.append(saved)
        actives.append(active)
    row_grads = [None] * number
    totals = None
    for slot_index in reversed(range(number)):
        gathered = fetch_weights(shards)
        row_grad, weight_grads = backward_pass(
            cotangent[slot_index], actives[slot_index], records[slot_index], gathered
        )
        row_grads[slot_index] = row_grad
        totals = (
            weight_grads
            if totals is None
            else jax.tree.map(lambda left, right: left + right, totals, weight_grads)
        )
    totals = shard_grads(totals)
    small_sums = lax.psum((totals[0], totals[1], totals[2]), "rep")
    matrix_sums = (
        lax.psum_scatter(totals[3], "rep", scatter_dimension=1, tiled=True),
        lax.psum_scatter(totals[4], "rep", scatter_dimension=1, tiled=True),
        lax.psum_scatter(totals[5], "rep", scatter_dimension=1, tiled=True),
        lax.psum_scatter(totals[6], "rep", scatter_dimension=1, tiled=True),
    )
    return (jnp.stack(outputs), jnp.stack(row_grads)) + tuple(small_sums) + tuple(matrix_sums)


def row_stats(values):
    centred = values - jnp.mean(values, -1, keepdims=True)
    inverse = lax.rsqrt(jnp.mean(centred * centred, -1, keepdims=True) + EPSILON)
    return centred * inverse, inverse


def whole(shape, **kw):
    return pl.BlockSpec(shape, lambda *_: (0,) * len(shape), **kw)


def call(kernel, ids, grid, in_specs, out_specs, out_shape, args, scratch=(), flops=0, limit=60, aliases=()):
    return pl.pallas_call(
        kernel,
        grid_spec=pltpu.PrefetchScalarGridSpec(
            num_scalar_prefetch=1, grid=grid, in_specs=in_specs, out_specs=out_specs, scratch_shapes=list(scratch)
        ),
        out_shape=out_shape,
        cost_estimate=pl.CostEstimate(flops=int(flops * COST), bytes_accessed=0, transcendentals=0),
        input_output_aliases=dict(aliases),
        compiler_params=pltpu.CompilerParams(vmem_limit_bytes=limit * 1024 * 1024),
    )(ids, *args)


def slot_of(shape, s):
    return pl.BlockSpec((None,) + shape, lambda *_: (s,) + (0,) * len(shape))


def piece_places(ids):
    y, core = ids[4], ids[0]
    return (2 * y + core, 2 * (1 - y) + core, 2 * y + 1 - core, 2 * (1 - y) + 1 - core)


def lay_pieces(ids, target, pieces):
    size = target.shape[0] // len(pieces)
    for piece, place in zip(pieces, piece_places(ids)):
        target[pl.ds(pl.multiple_of(place * size, size), size)] = piece[...]


def by_rows(ids, x, near, far):
    size = near.shape[0]
    own = pl.ds(pl.multiple_of(ids[3] * size, size), size)
    across = pl.ds(pl.multiple_of((1 - ids[3]) * size, size), size)
    return nn(x[:, own], near[...]) + nn(x[:, across], far[...])


def project_other_kernel(ids, mine, got, gain, shift, near, p0, p1, p2, p3, bias, block, normed, out, far_s):
    @pl.when(pl.program_id(0) == 0)
    def _():
        x = jnp.where(ids[1] == 1, got[...], mine[...])
        block[...] = x
        hat, unused = row_stats(x.astype(F32))
        normed[...] = (hat * gain[...] + shift[...]).astype(BF)

    lay_pieces(ids, far_s, (p0, p1, p2, p3))
    out[...] = (by_rows(ids, normed, near, far_s) + bias[...]).astype(BF)


def project_other(ids, mine, mine_slot, got, got_slot, gain, shift, near, far, bias):
    rows, width = mine.shape[1:]
    inner = width // 2
    columns = lambda i, ids: (0, 2 * i + 1 - ids[0])
    return call(
        project_other_kernel,
        ids,
        (3,),
        [
            slot_of((rows, width), mine_slot),
            slot_of((rows, width), got_slot),
            whole((1, width)),
            whole((1, width)),
            pl.BlockSpec((inner, inner), columns),
        ]
        + [pl.BlockSpec((inner // 4, inner), columns)] * 4
        + [pl.BlockSpec((1, inner), columns)],
        [whole((rows, width)), whole((rows, width)), pl.BlockSpec((rows, inner), lambda i, ids: (0, i))],
        [
            jax.ShapeDtypeStruct((rows, width), BF),
            jax.ShapeDtypeStruct((rows, width), BF),
            jax.ShapeDtypeStruct((rows, 3 * inner), BF),
        ],
        (mine, got, gain, shift, near, *far, bias),
        scratch=[pltpu.VMEM((inner, inner), BF)],
        flops=2 * rows * width * 3 * inner,
    )


def project_mine_kernel(ids, normed, near, p0, p1, p2, p3, bias, out, far_s):
    lay_pieces(ids, far_s, (p0, p1, p2, p3))
    out[...] = (by_rows(ids, normed, near, far_s) + bias[...]).astype(BF)


def project_mine(ids, normed, near, far, bias):
    rows, width = normed.shape
    inner = width // 2
    columns = lambda i, ids: (0, 2 * i + ids[0])
    return call(
        project_mine_kernel,
        ids,
        (3,),
        [whole((rows, width)), pl.BlockSpec((inner, inner), columns)]
        + [pl.BlockSpec((inner // 4, inner), columns)] * 4
        + [pl.BlockSpec((1, inner), columns)],
        pl.BlockSpec((rows, inner), lambda i, ids: (0, i)),
        jax.ShapeDtypeStruct((rows, 3 * inner), BF),
        (normed, near, *far, bias),
        scratch=[pltpu.VMEM((inner, inner), BF)],
        flops=2 * rows * width * 3 * inner,
    )


def feed_kernel(
    ids, block, ctx_mine, ctx_other, cot_mine, cot_got, out_near, o0, o1, o2, o3, up_near, u0, u1, u2, u3,
    down_near, d0, d1, d2, d3, gain, biases, bias_hidden, *rest,
):
    (
        active, d_pre, normed2, d_out, result, d_hidden, d_branch, d_ctx_mine, d_ctx_other, sums, sum_hidden,
        hidden_s, total_s, d_norm_s, up_far, w_down,
    ) = rest[-16:]
    j = pl.program_id(0)
    half = pl.num_programs(0) // 2
    inner = ctx_mine.shape[1]
    live = ids[2].astype(F32)
    own = pl.ds(pl.multiple_of(ids[3] * inner, inner), inner)
    across = pl.ds(pl.multiple_of((1 - ids[3]) * inner, inner), inner)
    lay_pieces(ids, up_far, (u0, u1, u2, u3))

    out_far = w_down.at[:inner]

    straight = ids[0] == ids[3]

    @pl.when(j == 0)
    def _():
        lay_pieces(ids, out_far, (o0, o1, o2, o3))
        w_mine = jnp.where(straight, out_near[...], out_far[...])
        w_other = jnp.where(straight, out_far[...], out_near[...])
        hidden = block[...].astype(F32) + (nn(ctx_mine[...], w_mine) + nn(ctx_other[...], w_other))
        hidden = hidden + biases[3:4]
        hidden_s[...] = hidden
        hat, unused = row_stats(hidden)
        normed2[...] = (hat * gain[1:2] + biases[4:5]).astype(BF)
        d = (jnp.where(ids[1] == 1, cot_got[...], cot_mine[...]).astype(F32) * live).astype(BF)
        d_out[...] = d

    @pl.when(j < half)
    def _():
        w_down[...] = down_near[...]

    @pl.when(j >= half)
    def _():
        here = ids[4] == j - half
        size = d0.shape[0]
        w_down[pl.ds(pl.multiple_of(ids[0] * size, size), size)] = jnp.where(here, d0[...], d1[...])
        w_down[pl.ds(pl.multiple_of((1 - ids[0]) * size, size), size)] = jnp.where(here, d2[...], d3[...])

    pre = by_rows(ids, normed2, up_near, up_far) + bias_hidden[...]
    phi = 0.5 + 0.5 * lax.erf(pre * 0.7071067811865476)
    act = (pre * phi).astype(BF)
    active[...] = act
    slope = phi + pre * (jnp.exp2(pre * pre * (-0.5 * LOG2E)) * 0.3989422804014327)
    dp = nt(d_out[...], w_down[...]) * slope
    sum_hidden[...] = jnp.broadcast_to(jnp.sum(dp.astype(BF).astype(F32), 0, keepdims=True), sum_hidden.shape)
    dp = dp.astype(BF)
    d_pre[...] = dp
    forward = nn(act, w_down[...])
    back = nt(dp, up_near[...])
    back_far = nt(dp, up_far[...])

    @pl.when(j == 0)
    def _():
        total_s[...] = forward
        d_norm_s[:, own] = back
        d_norm_s[:, across] = back_far

    @pl.when(j > 0)
    def _():
        total_s[...] += forward
        d_norm_s[:, own] += back
        d_norm_s[:, across] += back_far

    @pl.when(j == pl.num_programs(0) - 1)
    def _():
        hidden = hidden_s[...]
        result[...] = ((hidden + total_s[...] + biases[5:6]) * live).astype(BF)
        hat, inverse = row_stats(hidden)
        d_norm = d_norm_s[...]
        weighted = d_norm * gain[1:2]
        first = jnp.mean(weighted, -1, keepdims=True)
        second = jnp.mean(weighted * hat, -1, keepdims=True)
        d = d_out[...].astype(F32)
        d_hid = d + inverse * (weighted - first - hat * second)
        d_hidden[...] = d_hid
        branch = d_hid.astype(BF)
        d_branch[...] = branch
        sums[...] = jnp.concatenate(
            [
                jnp.sum(d_norm * hat, 0, keepdims=True),
                jnp.sum(d_norm, 0, keepdims=True),
                jnp.sum(branch.astype(F32), 0, keepdims=True),
                jnp.sum(d, 0, keepdims=True),
                jnp.zeros((4, d.shape[1]), F32),
            ],
            0,
        )
        lay_pieces(ids, out_far, (o0, o1, o2, o3))
        w_mine = jnp.where(straight, out_near[...], out_far[...])
        w_other = jnp.where(straight, out_far[...], out_near[...])
        d_ctx_mine[...] = nt(branch, w_mine).astype(BF)
        d_ctx_other[...] = nt(branch, w_other).astype(BF)


def feed(ids, slot, slots, block, ctx_mine, ctx_other, cot_mine, cot_got, w_out, w_up, w_down, far, far_down, gain, biases, bias_hidden, before):
    rows, width = block.shape
    inner = width // 2
    ff = w_up.shape[1]
    chunk = width
    steps = ff // chunk
    one = dict(pipeline_mode=pl.Buffered(1))
    full = whole((rows, width), **one)
    part = whole((rows, inner), **one)
    place = lambda j, ids: (0, (ids[3] * (steps // 2) + j) % steps)
    columns = pl.BlockSpec((rows, chunk), place)
    one_slot = lambda shape: pl.BlockSpec((None,) + shape, lambda *_: (slot, 0, 0), **one)
    wide = jax.ShapeDtypeStruct((rows, width), BF)
    args = (
        block, ctx_mine, ctx_other, cot_mine, cot_got, w_out, *far, w_up, *far, w_down, *far_down, gain, biases, bias_hidden,
    )
    return call(
        feed_kernel,
        ids,
        (steps,),
        [full, part, part, one_slot((rows, width)), one_slot((rows, width)), whole((inner, width), **one)]
        + [pl.BlockSpec((inner // 4, width), lambda j, ids: (steps, 0), **one)] * 4
        + [pl.BlockSpec((inner, chunk), place)]
        + [pl.BlockSpec((inner // 4, chunk), lambda j, ids: (place(j, ids)[1], 0))] * 4
        + [pl.BlockSpec((chunk, width), lambda j, ids: (jnp.minimum(j, steps // 2 - 1), 0), **one)]
        + [whole((ff // 8, width), **one)] * 4
        + [whole(gain.shape), whole(biases.shape), pl.BlockSpec((1, chunk), place)]
        + [pl.BlockSpec(memory_space=pl.ANY)] * len(before),
        [
            columns, columns, full, full, full, full, full, part, one_slot((rows, inner)),
            whole((8, width)),
            pl.BlockSpec((8, chunk), place),
        ],
        [
            jax.ShapeDtypeStruct((rows, ff), BF), jax.ShapeDtypeStruct((rows, ff), BF),
            wide, wide, wide, jax.ShapeDtypeStruct((rows, width), F32), wide,
            jax.ShapeDtypeStruct((rows, inner), BF), jax.ShapeDtypeStruct((slots, rows, inner), BF),
            jax.ShapeDtypeStruct((8, width), F32), jax.ShapeDtypeStruct((8, ff), F32),
        ],
        args + tuple(before),
        scratch=[pltpu.VMEM((rows, width), F32)] * 3
        + [pltpu.VMEM((inner, chunk), BF), pltpu.VMEM((chunk, width), BF)],
        flops=2 * rows * width * (4 * ff + 2 * width),
        limit=62,
        aliases=[(1 + len(args), 8)] if before else (),
    )


def outer_sum(left, right):
    total = None
    for a, b in zip(left, right):
        term = tn(a, b)
        total = term if total is None else total + term
    return total


def put_block(ids, outs, rec, piece, x, y, z, rows):
    place = 2 * (x != ids[3]).astype(jnp.int32) + (y != ids[4]).astype(jnp.int32)
    if rec is None:
        outs[0][place, z, rows] = piece.astype(BF)
        return
    for i, out in enumerate(outs):

        @pl.when(place == i)
        def _(i=i, out=out):
            out[z, rows] = (piece + rec[i, z, rows].astype(F32)).astype(BF)


def split_refs(refs, counts):
    parts, at = [], 0
    for count in counts:
        parts.append(refs[at : at + count])
        at += count
    rest = refs[at:]
    return parts + ([None, rest] if len(rest) == 1 else [rest[0], rest[-4:]])


def grad_down_kernel(ids, *refs, slots):
    left, right, rec, outs = split_refs(refs, (slots, slots))
    step = pl.program_id(0)
    x = jnp.where(step == 0, 1 - ids[3], ids[3])
    total = outer_sum([a[...] for a in left], [b[...] for b in right])
    chips, rows, cols = outs[0].shape[-3:]
    parts = total.shape[1] // cols
    rows = rows // parts
    for z in range(chips):
        for y in range(2):
            at = (2 * z + y) * rows
            for part in range(parts):
                piece = total[at : at + rows, part * cols : (part + 1) * cols]
                put_block(ids, outs, rec, piece, x, jnp.int32(y), z, slice(part * rows, (part + 1) * rows))


def grad_up_kernel(ids, *refs, slots):
    left, first, last, rec, outs = split_refs(refs, (slots, slots, slots))
    z = pl.program_id(0)
    right = [jnp.concatenate([a[...], b[...]], 1) for a, b in zip(first, last)]
    total = outer_sum([a[...] for a in left], right)
    rows, cols = outs[0].shape[-2:]
    for x in range(2):
        for y in range(2):
            piece = total[y * rows : (y + 1) * rows, x * cols : (x + 1) * cols]
            put_block(ids, outs, rec, piece, jnp.int32(x), jnp.int32(y), z, slice(0, rows))


def grad_out_kernel(ids, *refs, slots):
    left, mine, other, rec, outs = split_refs(refs, (slots, slots, slots))
    right = [jnp.concatenate([a[...], b[...]], 1) for a, b in zip(mine, other)]
    total = outer_sum([a[...] for a in left], right)
    chips, rows, cols = outs[0].shape[-3:]
    for near in range(2):
        x = ids[0] if near == 0 else 1 - ids[0]
        for z in range(chips):
            for y in range(2):
                at = (2 * z + y) * rows
                piece = total[at : at + rows, near * cols : (near + 1) * cols]
                put_block(ids, outs, rec, piece, x, jnp.int32(y), z, slice(0, rows))


def grad_qkv_kernel(ids, *refs, slots, steps):
    mine, other, first, last, rec, outs = split_refs(refs, (slots, slots, slots, slots))
    right = [jnp.concatenate([a[...], b[...]], 1) for a, b in zip(first, last)]
    near = outer_sum([a[...] for a in mine], right)
    far = outer_sum([a[...] for a in other], right)
    total = jnp.concatenate([jnp.where(ids[0] == 0, near, far), jnp.where(ids[0] == 0, far, near)])
    chips, rows, cols = outs[0].shape[-3:]
    span = total.shape[0]
    for step in range(steps):

        @pl.when(pl.program_id(0) == step)
        def _(step=step):
            for block in range(2 * chips):
                begin = max(block * rows, step * span)
                end = min((block + 1) * rows, (step + 1) * span)
                if begin >= end:
                    continue
                for x in range(2):
                    piece = total[begin - step * span : end - step * span, x * cols : (x + 1) * cols]
                    put_block(
                        ids, outs, rec, piece, jnp.int32(x), jnp.int32(block % 2), block // 2,
                        slice(begin - block * rows, end - block * rows),
                    )


def grad_call(kernel, ids, grid, groups, shape, rec, flops, joint=None, **kw):
    specs, args = [], []
    for arrays, block, index in groups:
        specs += [pl.BlockSpec(block, index)] * len(arrays)
        args += arrays
    if rec is None:
        out_specs, out_shapes, aliases = whole(shape, pipeline_mode=pl.Buffered(1)), jax.ShapeDtypeStruct(shape, BF), ()
    else:
        specs.append(whole(shape, pipeline_mode=pl.Buffered(1)))
        args.append(rec)
        all_rows, at, arrays = joint
        out_specs = [pl.BlockSpec(shape[1:], lambda *_: (0, at, 0), pipeline_mode=pl.Buffered(1))] * 4
        out_shapes = [jax.ShapeDtypeStruct((shape[1], all_rows, shape[3]), BF)] * 4
        aliases = [(1 + len(args) + i, i) for i in range(len(arrays))]
        specs += [pl.BlockSpec(memory_space=pl.ANY)] * len(arrays)
        args += arrays
    return call(
        functools.partial(kernel, slots=len(groups[0][0]), **kw),
        ids, grid, specs, out_specs, out_shapes, tuple(args), flops=flops, aliases=aliases,
    )


def column_half(ids, rec):
    return 1 - ids[0] if rec is None else ids[0]


def grad_down_part(ids, chips, d_out, active, rec, joint=None):
    rows, width = d_out[0].shape
    ff = active[0].shape[1]
    cols = ff // 4
    parts = 4 * cols // width
    block = lambda i, ids: (0, 2 * jnp.where(i == 0, 1 - ids[3], ids[3]) + column_half(ids, rec))
    groups = [(d_out, (rows, width), lambda i, ids: (0, 0)), (active, (rows, cols), block)]
    flops = 2 * len(d_out) * rows * width * 2 * cols
    shape = (4, chips, parts * width // (2 * chips), cols // parts)
    return grad_call(grad_down_kernel, ids, (2,), groups, shape, rec, flops, joint)


def grad_up_part(ids, chips, d_pre, normed, rec, joint=None):
    rows, width = normed[0].shape
    ff = d_pre[0].shape[1]
    cols = width // 4
    groups = [
        (d_pre, (rows, ff // chips), lambda i, ids: (0, i)),
        (normed, (rows, cols), lambda i, ids: (0, column_half(ids, rec))),
        (normed, (rows, cols), lambda i, ids: (0, 2 + column_half(ids, rec))),
    ]
    flops = 2 * len(d_pre) * rows * ff * 2 * cols
    return grad_call(grad_up_kernel, ids, (chips,), groups, (4, chips, ff // (2 * chips), cols), rec, flops, joint)


def grad_out_part(ids, chips, d_branch, mine, other, rec, joint=None):
    rows, width = d_branch[0].shape
    cols = width // 4
    half = lambda i, ids: (0, column_half(ids, rec))
    groups = [(d_branch, (rows, width), lambda i, ids: (0, 0)), (mine, (rows, cols), half), (other, (rows, cols), half)]
    flops = 2 * len(d_branch) * rows * width * 2 * cols
    return grad_call(grad_out_kernel, ids, (1,), groups, (4, chips, width // (2 * chips), cols), rec, flops, joint)


def grad_qkv_part(ids, chips, mine, other, normed, rec, joint=None):
    rows, width = normed[0].shape
    cols = width // 4
    columns = lambda i, ids: (0, i)
    groups = [
        (mine, (rows, width // 2), columns),
        (other, (rows, width // 2), columns),
        (normed, (rows, cols), lambda i, ids: (0, column_half(ids, rec))),
        (normed, (rows, cols), lambda i, ids: (0, 2 + column_half(ids, rec))),
    ]
    flops = 2 * len(mine) * rows * 3 * width * 2 * cols
    return grad_call(
        grad_qkv_kernel, ids, (3,), groups, (4, chips, 3 * width // (2 * chips), cols), rec, flops, joint, steps=3
    )


def add_kernel(ids, *refs):
    refs[-1][...] = sum(term[...].astype(F32) for term in refs[:-1]).astype(BF)


def add_chips(ids, terms, chips, rows):
    cols = terms[0].shape[1]
    return call(
        add_kernel,
        ids,
        (chips,),
        [pl.BlockSpec((rows, cols), lambda i, ids: (ids[5] ^ i, 0))] * len(terms),
        pl.BlockSpec((None, rows, cols), lambda i, ids: (i, 0, 0)),
        jax.ShapeDtypeStruct((chips, rows, cols), BF),
        tuple(terms),
    )


def finish_kernel(
    ids, d_mine, d_other, mine_near, m0, m1, m2, m3, other_near, o0, o1, o2, o3, block, d_hidden, gain,
    row_grad, sums, sum_mine, sum_other, total_s, mine_far, other_far,
):
    i = pl.program_id(0)
    size = mine_near.shape[0]
    lay_pieces(ids, mine_far, (m0, m1, m2, m3))
    lay_pieces(ids, other_far, (o0, o1, o2, o3))
    own = pl.ds(pl.multiple_of(ids[3] * size, size), size)
    across = pl.ds(pl.multiple_of((1 - ids[3]) * size, size), size)
    term = nt(d_mine[...], mine_near[...]) + nt(d_other[...], other_near[...])
    term_far = nt(d_mine[...], mine_far[...]) + nt(d_other[...], other_far[...])
    sum_mine[...] = jnp.broadcast_to(jnp.sum(d_mine[...].astype(F32), 0, keepdims=True), sum_mine.shape)
    sum_other[...] = jnp.broadcast_to(jnp.sum(d_other[...].astype(F32), 0, keepdims=True), sum_other.shape)

    @pl.when(i == 0)
    def _():
        total_s[:, own] = term
        total_s[:, across] = term_far

    @pl.when(i > 0)
    def _():
        total_s[:, own] += term
        total_s[:, across] += term_far

    @pl.when(i == pl.num_programs(0) - 1)
    def _():
        hat, inverse = row_stats(block[...].astype(F32))
        d_norm = total_s[...]
        weighted = d_norm * gain[0:1]
        first = jnp.mean(weighted, -1, keepdims=True)
        second = jnp.mean(weighted * hat, -1, keepdims=True)
        row_grad[...] = (d_hidden[...] + inverse * (weighted - first - hat * second)).astype(BF)
        sums[...] = jnp.concatenate(
            [jnp.sum(d_norm * hat, 0, keepdims=True), jnp.sum(d_norm, 0, keepdims=True), jnp.zeros((6, d_norm.shape[1]), F32)], 0
        )


def finish(ids, d_mine, d_other, near, far, block, d_hidden, gain):
    rows, width = block.shape
    inner = width // 2
    full = whole((rows, width))
    part = pl.BlockSpec((rows, inner), lambda i, ids: (0, i))
    row = pl.BlockSpec((8, inner), lambda i, ids: (0, i))
    mine = lambda i, ids: (0, 2 * i + ids[0])
    other = lambda i, ids: (0, 2 * i + 1 - ids[0])
    return call(
        finish_kernel,
        ids,
        (3,),
        [
            part, part,
            pl.BlockSpec((inner, inner), mine), *[pl.BlockSpec((inner // 4, inner), mine)] * 4,
            pl.BlockSpec((inner, inner), other), *[pl.BlockSpec((inner // 4, inner), other)] * 4,
            full, full, whole(gain.shape),
        ],
        [full, whole((8, width)), row, row],
        [
            jax.ShapeDtypeStruct((rows, width), BF), jax.ShapeDtypeStruct((8, width), F32),
            jax.ShapeDtypeStruct((8, 3 * inner), F32), jax.ShapeDtypeStruct((8, 3 * inner), F32),
        ],
        (d_mine, d_other, near, *far, near, *far, block, d_hidden, gain),
        scratch=[pltpu.VMEM((rows, width), F32)] + [pltpu.VMEM((inner, inner), BF)] * 2,
        flops=2 * rows * width * 3 * width,
    )


def swap_axis(x, axis, step=1):
    size = lax.axis_size(axis)
    return lax.ppermute(x, axis, [(i, i ^ step) for i in range(size)])


def swap_across(x):
    return lax.ppermute(x, ("mid", "grp"), [(0, 3), (1, 2), (2, 1), (3, 0)])


def swap_owner(x, chips):
    pairs = []
    for k in range(2 * chips):
        pairs += [(4 * k + 1, 4 * k + 2), (4 * k + 2, 4 * k + 1)]
    return lax.ppermute(x, AXES, pairs)


def after(values, first):
    return lax.optimization_barrier((values, first))[0]


def in_order(index, mine, other, axis=0):
    return jnp.concatenate([jnp.where(index == 0, mine, other), jnp.where(index == 0, other, mine)], axis)


def own_half(x, index, axis=0):
    size = x.shape[axis] // 2
    return lax.dynamic_slice_in_dim(x, index * size, size, axis)


def send_piece(piece):
    return swap_axis(piece, "grp")


def own_piece(shard):
    place = 2 * lax.axis_index("mid") + lax.axis_index("core")
    part = shard.shape[0] // 4
    return lax.dynamic_slice_in_dim(shard, place * part, part, 0)


def as_lines(x, cols):
    parts = []
    for _ in range(3):
        part = lax.reduce_precision(x, 8, 7)
        parts.append(part.astype(BF))
        x = x - part
    return jnp.concatenate(parts).reshape(-1, cols)


def from_lines(lines, shape):
    return lines.astype(F32).reshape((3,) + shape).sum(0)


def send_sums(part):
    return [part[0], swap_axis(part[1], "mid"), swap_axis(part[2], "grp"), swap_across(part[3])]


def send_chips(part):
    return [part[0]] + [swap_axis(part[i], "z", i) for i in range(1, lax.axis_size("z"))]


def settle(total, parts, core):
    mine = jnp.concatenate([lax.dynamic_index_in_dim(part, core, 0, False) for part in parts])
    other = jnp.concatenate([lax.dynamic_index_in_dim(part, 1 - core, 0, False) for part in parts])
    return mine, swap_axis(other, "core")


def body(chips, clips, clip_count, cotangent, norm_gain, bias_d, bias_ff, w_qkv, w_o, w_up, w_down):
    core, x, y, z = (lax.axis_index(axis) for axis in ("core", "grp", "mid", "z"))
    slots, half, width = clips.shape
    inner = width // 2
    ff = w_up.shape[1]
    swap = (core != x).astype(jnp.int32)

    qkv_piece = own_piece(w_qkv)
    small = jnp.concatenate([norm_gain.reshape(-1), bias_d.reshape(-1), bias_ff]).reshape(-1, 128)
    qkv_0 = send_piece(qkv_piece)
    got_small = swap_axis(after(small, qkv_piece), "grp")
    got_first = swap_owner(after(clips[:1], qkv_piece), chips)
    other_count = swap_axis(clip_count, "core")
    qkv_1 = swap_axis(qkv_0, "mid")
    qkv_2 = swap_axis(qkv_0, "core")
    got_rest = swap_owner(after(clips[1:], qkv_0), chips)
    piece = own_piece(w_up).reshape(-1, ff // width, width).transpose(1, 0, 2).reshape(-1, width)
    piece = jnp.concatenate([piece, own_piece(w_o)])
    down_piece = own_piece(w_down)
    qkv_3 = swap_axis(qkv_1, "core")
    qkv_far = (qkv_0, qkv_1, qkv_2, qkv_3)
    far_0 = send_piece(after(piece, qkv_1))
    down_0 = send_piece(after(down_piece, qkv_1))

    pair = in_order(x, small[None], got_small[None]).reshape(2, -1).astype(F32)
    gains = pair[:, : 2 * inner].reshape(2, 2, inner).transpose(1, 0, 2).reshape(2, width)
    biases = pair[:, 2 * inner : 8 * inner].reshape(2, 6, inner).transpose(1, 0, 2).reshape(6, width)
    bias_hidden = pair[:, 8 * inner :].reshape(1, -1)
    count = jnp.where(swap == 1, other_count, clip_count)[0]
    qkv_bias = jnp.concatenate([biases[1], jnp.zeros_like(biases[1]), biases[2]])[None]
    ids = [jnp.stack([core, swap, (count > s).astype(jnp.int32), x, y, z]).astype(jnp.int32) for s in range(slots)]

    blocks, normed, saved, ctx_mine, ctx_other = [], [], [], [], []
    for s in range(slots):
        got, slot = (got_first, 0) if s == 0 else (got_rest, s - 1)
        block, norm, other = project_other(ids[s], clips, s, got, slot, gains[0:1], biases[0:1], w_qkv, qkv_far, qkv_bias)
        received = swap_axis(other, "core")
        mine = project_mine(ids[s], norm, w_qkv, qkv_far, qkv_bias)
        if s == 0:
            mine = after(mine, (piece, down_piece))
        elif s == 2:
            mine = after(mine, (far_2, far_3))
        here, there, r_here, r_there, weights, weights_rem = attend(mine, received)
        saved.append((mine, received, here, there, r_here, r_there, weights, weights_rem))
        ctx_mine.append(here)
        ctx_other.append(swap_axis(there, "core"))
        blocks.append(block)
        normed.append(norm)
        if s == 0:
            far_0 = after(far_0, here)
            far_1 = swap_axis(far_0, "mid")
            far_2 = swap_axis(far_0, "core")
            got_rest = after(got_rest, (here, far_0))
        elif s == 1:
            far_1 = after(far_1, here)
            far_3 = swap_axis(far_1, "core")
            down_0 = after(down_0, here)
            down_1 = swap_axis(down_0, "mid")
            got_cot = swap_owner(after(cotangent, down_0), chips)
            got_rest = after(got_rest, (here, far_1, down_0))
        elif s == 2:
            down_2 = swap_axis(after(down_0, here), "core")
            down_1 = after(down_1, here)
            down_3 = swap_axis(down_1, "core")
    far = (far_0, far_1, far_2, far_3)
    far_down = (down_0, down_1, down_2, down_3)

    fed, got_result = [], []
    before = ()
    for s in range(slots):
        fed.append(
            feed(
                ids[s], s, slots, blocks[s], ctx_mine[s], ctx_other[s], cotangent, got_cot, w_o, w_up, w_down, far, far_down,
                gains, biases, bias_hidden, before,
            )
        )
        before = (fed[-1][8],)
        got_result.append(swap_owner(fed[-1][4], chips))
    active, d_pre, normed2, d_out, result, d_hidden, d_branch, d_ctx_mine, d_ctx_other, sums2, sums_hidden = map(list, zip(*fed))
    d_ctx_got = swap_axis(d_ctx_other[-1], "core")

    sent_down = grad_down_part(ids[0], chips, d_out, active, None)
    sent_up = grad_up_part(ids[0], chips, d_pre, normed2, None)
    sent_out = grad_out_part(ids[0], chips, d_branch, ctx_mine, ctx_other, None)
    rows_down, rows_up, rows_out = (part.shape[2] for part in (sent_down, sent_up, sent_out))
    rows = rows_down + rows_up + rows_out
    joint = grad_down_part(ids[0], chips, d_out, active, swap_axis(sent_down, "core"), (rows, 0, []))
    joint = grad_up_part(
        ids[0], chips, d_pre, normed2, swap_axis(sent_up, "core"), (rows, rows_down // rows_up, joint)
    )
    joint = grad_out_part(
        ids[0], chips, d_branch, ctx_mine, ctx_other, swap_axis(sent_out, "core"),
        (rows, (rows_down + rows_up) // rows_out, joint),
    )
    cols = joint[0].shape[-1]
    sums = send_sums([part.reshape(-1, cols) for part in joint])
    early = jnp.concatenate([sum(sums2)[:4], sum(sums_hidden)[0].reshape(-1, width)])

    d_mine, d_other, row_grads, sums1, sums_mine, sums_other = [], [], [], [], [], []

    def complete(s, first):
        row_grad, sum1, sum_mine, sum_other = finish(
            ids[s], d_mine[s], after(d_other[s], first), w_qkv, qkv_far, blocks[s], d_hidden[s], gains
        )
        row_grads.append(jnp.where(swap == 1, swap_owner(row_grad, chips), row_grad).astype(F32))
        sums1.append(sum1)
        sums_mine.append(sum_mine[0])
        sums_other.append(sum_other[0])
        return row_grad

    outs = jnp.stack([jnp.where(swap == 1, got_result[s], result[s]) for s in range(slots)])
    gate = (joint, outs)
    for s in range(slots):
        mine, received, here, there, r_here, r_there, weights, weights_rem = saved[s]
        d_here, d_there = attend_back(
            s, mine, received, after(d_ctx_mine[s], gate), d_ctx_got, here, there, r_here, r_there, weights, weights_rem
        )
        d_mine.append(d_here)
        d_other.append(swap_axis(d_there, "core"))
        gate = (d_here,)
        if s == 0:
            sums[3] = after(sums[3], d_here)
            gate = (d_here, sums[3])
        elif s == 1:
            sums = add_chips(ids[0], after(sums, d_here), chips, rows)
            gate = sums
            terms = send_chips(sums)
        if s > 0:
            gate = (gate, complete(s - 1, d_here))
    terms = after(terms, gate)
    sent_qkv = grad_qkv_part(ids[0], chips, d_mine, after(d_other, (gate, terms)), normed, None)
    row_grad = complete(slots - 1, sent_qkv)
    part_qkv = grad_qkv_part(
        ids[0], chips, d_mine, d_other, normed, after(swap_axis(sent_qkv, "core"), row_grad),
        (sent_qkv.shape[2], 0, []),
    )
    total1 = sum(sums1)
    total_mine, total_other = sum(sums_mine), sum(sums_other)
    grad_bq = in_order(core, total_mine[:inner], total_other[:inner])
    grad_bv = in_order(core, total_mine[2 * inner :], total_other[2 * inner :])
    lines = jnp.concatenate(
        [jnp.stack([total1[0], early[0], total1[1], grad_bq, grad_bv, early[2], early[1], early[3]]), early[4:]]
    )
    lines = lines + swap_axis(lines, "core")
    shape = lines.shape
    under = as_lines(lines, cols)
    qkv_rows = part_qkv[0].shape[1]
    qkv_terms = send_sums([jnp.concatenate([part.reshape(-1, cols), under]) for part in part_qkv])

    total = sum(term.astype(F32) for term in after(terms, part_qkv))
    chunks = rows_down // rows_out
    down = total[:rows_down].reshape(chunks, 2, -1, cols).transpose(1, 0, 2, 3).reshape(2, -1, cols)
    up = total[rows_down : rows_down + rows_up].reshape(2, -1, cols)
    out = total[rows_down + rows_up :].reshape(2, -1, cols)
    mine, other = settle(total, (down, up, out), core)
    whole_rows = in_order(core, mine, other, 1)
    n_down, n_up = rows_down // 2, rows_up // 2
    own_down = in_order(core, mine[:n_down].reshape(chunks, -1, cols), other[:n_down].reshape(chunks, -1, cols))
    grad_down = own_down.transpose(0, 2, 1).reshape(2 * chunks * cols, -1)
    grad_up = whole_rows[n_down : n_down + n_up].T
    grad_out = whole_rows[n_down + n_up :].T

    sums = add_chips(ids[0], qkv_terms, chips, qkv_rows)
    lines = sum(from_lines(term[chips * qkv_rows :], shape) for term in qkv_terms)
    under = as_lines(lines, cols)
    qkv_terms = send_chips([jnp.concatenate([sums[i], under]) for i in range(chips)])
    lines = sum(from_lines(term[qkv_rows:], shape) for term in qkv_terms)
    columns = own_half(lines[:8], x, 1)
    hidden_part = own_half(lines[8:], x).reshape(-1)
    total = sum(term[:qkv_rows].astype(F32) for term in qkv_terms)
    mine, other = settle(total, (total.reshape(2, -1, cols),), core)
    grad_qkv = in_order(core, mine, other, 1).T
    return (outs, jnp.stack(row_grads), columns[:2], columns[2:], hidden_part, grad_qkv, grad_out, grad_up, grad_down)


def solution(mesh):
    in_specs = (
        P("rep", "grp", None),
        P("rep"),
        P("rep", "grp", None),
        P(None, "grp"),
        P(None, "grp"),
        P("grp"),
        P("grp", None),
        P("grp", None),
        P("grp", None),
        P("grp", None),
    )
    out_specs = (
        P("rep", "grp", None),
        P("rep", "grp", None),
        P(None, "grp"),
        P(None, "grp"),
        P("grp"),
        P("grp", "rep"),
        P("grp", "rep"),
        P("grp", "rep"),
        P("grp", "rep"),
    )
    if mesh.shape["grp"] != 2 or mesh.shape["rep"] != 16:
        return jax.shard_map(plain_body, mesh=mesh, in_specs=in_specs, out_specs=out_specs, check_vma=False)
    chips = mesh.shape["rep"] // 4
    split = Mesh(mesh.devices.reshape(chips, 2, 2, 2), AXES)
    rep = lambda spec: P(*[AXES[:3] if axis == "rep" else axis for axis in spec])
    return jax.shard_map(
        functools.partial(body, chips),
        mesh=split,
        in_specs=tuple(rep(spec) for spec in in_specs),
        out_specs=tuple(rep(spec) for spec in out_specs),
        check_vma=False,
    )
```

```python
import functools

import jax
import jax.numpy as jnp
from jax import lax
from jax.experimental import pallas as pl
from jax.experimental.pallas import tpu as pltpu
from jax.sharding import Mesh
from jax.sharding import PartitionSpec as P

H = 16
HD = 64
EPSILON = 1e-06

F32 = jnp.float32
BF = jnp.bfloat16
LOG2E = 1.4426950408889634
SCALE = HD ** -0.5
AXES = ("z", "mid", "core", "grp")
BQ = 512
TK = 224
COST = 5 * 10**10
LIMIT = 70.0


def dot(a, b, dims):
    return lax.dot_general(a, b, (dims, ((), ())), preferred_element_type=F32)


def nt(a, b):
    return dot(a, b, ((1,), (1,)))


def nn(a, b):
    return dot(a, b, ((1,), (0,)))


def tn(a, b):
    return dot(a, b, ((0,), (0,)))


def pair_mask(a):
    lane = lax.broadcasted_iota(jnp.int32, (1, 128), 1)
    return (lane < HD) if a == 0 else (lane >= HD)

def norm_peak(x, np_):
    inner = x.shape[1]
    r = lax.broadcasted_iota(jnp.int32, (inner, 128), 0)
    c = lax.broadcasted_iota(jnp.int32, (inner, 128), 1)
    ones = jnp.where(r // HD == c, 1.0, 0.0).astype(BF)
    xf = x.astype(F32)
    return jnp.max(nn((xf * xf).astype(BF), ones), axis=0, keepdims=True)

def attend_kernel(own, rec, oo, orr, ro, rr, p_out, prem_out, q_s, k_s, vt_s, o_s, r_s, fast, *, nb, np_, rem):
    half = own.shape[0]
    inner = own.shape[1] // 3
    full = 2 * half
    t = pl.program_id(0)
    last = np_ * nb

    @pl.when(t == 0)
    def _():
        q_s[:half] = own[:, :inner]
        q_s[half:] = rec[:, :inner]
        k_s[:half] = own[:, inner:2 * inner]
        k_s[half:] = rec[:, inner:2 * inner]
        row = lax.broadcasted_iota(jnp.int32, (128, 1), 0)
        for p in range(np_):
            cols = slice(2 * inner + p * 128, 2 * inner + (p + 1) * 128)
            vt = jnp.concatenate([own[:, cols], rec[:, cols]], axis=0).T
            for a in range(2):
                mine = (row < HD) if a == 0 else (row >= HD)
                vt_s[2 * p + a] = jnp.where(mine, vt, 1.0).astype(BF)
        peak = jnp.max(norm_peak(q_s[...], np_) * norm_peak(k_s[...], np_))
        fast[0] = (peak * (1.1 * SCALE * SCALE) < LIMIT * LIMIT).astype(jnp.int32)

    def store(o, rows, cols):
        oa, ob = o
        ra = 1.0 / oa[HD:]
        rb = 1.0 / ob[:HD]
        o_s[rows, cols] = jnp.concatenate([oa[:HD] * ra, ob[HD:] * rb], axis=0).T.astype(BF)
        r_s[rows, cols] = jnp.concatenate([ra, rb], axis=0).T

    def main(quick):
        p = t // nb
        b = t % nb
        rows = pl.ds(pl.multiple_of(b * BQ, BQ), BQ)
        cols = pl.ds(pl.multiple_of(p * 128, 128), 128)
        q = q_s[rows, cols]
        def weights(a):
            qa = jnp.where(pair_mask(a), q, 0.0).astype(BF)
            if quick:
                for j in range(full // TK):
                    tile = slice(j * TK, (j + 1) * TK)
                    s = nt(k_s[tile, cols], qa)
                    p_out[0, a, tile] = jnp.exp2(s * (LOG2E * SCALE)).astype(BF)
            else:
                s = nt(k_s[:, cols], qa)
                m = jnp.max(s, axis=0, keepdims=True)
                p_out[0, a] = jnp.exp2((s - m) * (LOG2E * SCALE)).astype(BF)
        weights(0)
        weights(1)
        oa = nn(vt_s[2 * p], p_out[0, 0])
        ob = nn(vt_s[2 * p + 1], p_out[0, 1])
        store((oa, ob), rows, cols)

    @pl.when((t < last) & (fast[0] == 1))
    def _():
        main(True)

    @pl.when((t < last) & (fast[0] == 0))
    def _():
        main(False)

    @pl.when(t == last)
    def _():
        if rem:
            lane = lax.broadcasted_iota(jnp.int32, (1, 256), 1)
            for u in range(np_ // 2):
                q = q_s[nb * BQ:, u * 256:(u + 1) * 256]
                qd = jnp.concatenate([jnp.where(lane // HD == h, q, 0.0).astype(BF) for h in range(4)], axis=0)
                s = nt(k_s[:, u * 256:(u + 1) * 256], qd)
                m = jnp.max(s, axis=0, keepdims=True)
                prem_out[u] = jnp.exp2((s - m) * (LOG2E * SCALE)).astype(BF)
                for v in range(2):
                    oa = nn(vt_s[4 * u + 2 * v], prem_out[u])
                    ob = nn(vt_s[4 * u + 2 * v + 1], prem_out[u])
                    ra = 1.0 / oa[HD:]
                    rb = 1.0 / ob[:HD]
                    x = jnp.concatenate([oa[:HD] * ra, ob[HD:] * rb], axis=0).T
                    r = jnp.concatenate([ra, rb], axis=0).T
                    ha, hb = 2 * v, 2 * v + 1
                    pick = lambda y: jnp.where(pair_mask(0), y[ha * rem:(ha + 1) * rem], y[hb * rem:(hb + 1) * rem])
                    cols = slice((2 * u + v) * 128, (2 * u + v + 1) * 128)
                    o_s[nb * BQ:, cols] = pick(x).astype(BF)
                    r_s[nb * BQ:, cols] = pick(r)
        oo[...] = o_s[:half]
        orr[...] = o_s[half:]
        ro[...] = r_s[:half]
        rr[...] = r_s[half:]

def attend(own, rec):
    half, w = own.shape
    inner = w // 3
    np_ = inner // 128
    full = 2 * half
    nb = full // BQ
    rem = full - nb * BQ
    last = np_ * nb
    whole = lambda shape: pl.BlockSpec(shape, lambda t: (0,) * len(shape))
    return pl.pallas_call(
        functools.partial(attend_kernel, nb=nb, np_=np_, rem=rem),
        grid=(last + 1,),
        in_specs=[whole((half, w))] * 2,
        out_specs=[whole((half, inner))] * 4 + [pl.BlockSpec((1, 2, full, BQ), lambda t: (jnp.minimum(t, last - 1), 0, 0, 0)), whole((np_ // 2, full, 4 * rem))],
        out_shape=[jax.ShapeDtypeStruct((half, inner), BF)] * 2 + [jax.ShapeDtypeStruct((half, inner), F32)] * 2
        + [jax.ShapeDtypeStruct((last, 2, full, BQ), BF), jax.ShapeDtypeStruct((np_ // 2, full, 4 * rem), BF)],
        scratch_shapes=[
            pltpu.VMEM((full, inner), BF), pltpu.VMEM((full, inner), BF), pltpu.VMEM((2 * np_, 128, full), BF),
            pltpu.VMEM((full, inner), BF), pltpu.VMEM((full, inner), F32), pltpu.SMEM((1,), jnp.int32)],
        cost_estimate=pl.CostEstimate(flops=0, bytes_accessed=0, transcendentals=0),
        compiler_params=pltpu.CompilerParams(vmem_limit_bytes=60 * 1024 * 1024),
    )(own, rec)


def attend_back_kernel(own, rec, do_o, do_r, o_o, o_r, r_o, r_r, e, erem, out_o, out_r,
               q_s, k_s, v_s, kt_s, do_s, pr_s, ds_s, dq_s, dk_s, dv_s, *, nb, np_, rem):
    half = own.shape[0]
    inner = own.shape[1] // 3
    full = 2 * half
    t = pl.program_id(0)
    last = np_ * nb

    @pl.when(t == 0)
    def _():
        for lo, src, d, o, r in ((0, own, do_o, o_o, r_o), (half, rec, do_r, o_r, r_r)):
            rows = slice(lo, lo + half)
            q_s[rows] = src[:, :inner]
            k_s[rows] = src[:, inner:2 * inner]
            v_s[rows] = src[:, 2 * inner:]
            dn = (d[...].astype(F32) * r[...]).astype(BF)
            do_s[rows] = dn
            pr_s[rows] = dn.astype(F32) * o[...].astype(F32)
        for p in range(np_):
            kt_s[p * 128:(p + 1) * 128] = k_s[:, p * 128:(p + 1) * 128].T
        dk_s[...] = jnp.zeros_like(dk_s)
        dv_s[...] = jnp.zeros_like(dv_s)

    @pl.when(t < last)
    def _():
        p = t // nb
        b = t % nb
        rows = pl.ds(pl.multiple_of(b * BQ, BQ), BQ)
        cols = pl.ds(pl.multiple_of(p * 128, 128), 128)
        q = q_s[rows, cols]
        dn = do_s[rows, cols]
        prod = pr_s[rows, cols].T
        qs, dns = [], []
        for a in range(2):
            qs.append(jnp.where(pair_mask(a), q, 0.0).astype(BF))
            dns.append(jnp.where(pair_mask(a), dn, 0.0).astype(BF))
        for a in range(2):
            delta = jnp.sum(prod[a * HD:(a + 1) * HD], axis=0, keepdims=True)
            for j in range(full // TK):
                tile = slice(j * TK, (j + 1) * TK)
                dp = nt(v_s[tile, cols], dns[a])
                ds_s[a, tile] = (e[0, a, tile].astype(F32) * (dp - delta)).astype(BF)
        for j in range(full // TK):
            tile = slice(j * TK, (j + 1) * TK)
            dv_s[tile, cols] += nn(e[0, 0, tile], dns[0]) + nn(e[0, 1, tile], dns[1])
        dqt = []
        for a in range(2):
            dqt.append(nn(kt_s[pl.ds(pl.multiple_of(p * 128, 128), 128)], ds_s[a])[a * HD:(a + 1) * HD])
        dq_s[rows, cols] = (jnp.concatenate(dqt, axis=0) * SCALE).T.astype(BF)
        for j in range(full // TK):
            tile = slice(j * TK, (j + 1) * TK)
            dk_s[tile, cols] += nn(ds_s[0, tile], qs[0]) + nn(ds_s[1, tile], qs[1])

    @pl.when(t == last)
    def _():
        if rem:
            lane = lax.broadcasted_iota(jnp.int32, (1, 256), 1)
            def spread(x):
                return jnp.concatenate([jnp.where(lane // HD == h, x, 0.0).astype(x.dtype) for h in range(4)], axis=0)
            for u in range(np_ // 2):
                cols = slice(u * 256, (u + 1) * 256)
                qd = spread(q_s[nb * BQ:, cols])
                dd = spread(do_s[nb * BQ:, cols])
                delta = jnp.sum(spread(pr_s[nb * BQ:, cols]).T, axis=0, keepdims=True)
                dp = nt(v_s[:, cols], dd)
                ds = (erem[u].astype(F32) * (dp - delta)).astype(BF)
                dv_s[:, cols] += nn(erem[u], dd)
                dk_s[:, cols] += nn(ds, qd)
                x = nn(kt_s[cols], ds).T * SCALE
                dq = x[:rem]
                for h in range(1, 4):
                    dq = jnp.where(lane // HD == h, x[h * rem:(h + 1) * rem], dq)
                dq_s[nb * BQ:, cols] = dq.astype(BF)
        for lo, dst in ((0, out_o), (half, out_r)):
            rows = slice(lo, lo + half)
            dst[:, :inner] = dq_s[rows]
            dst[:, inner:2 * inner] = (dk_s[rows] * SCALE).astype(BF)
            dst[:, 2 * inner:] = dv_s[rows].astype(BF)

def attend_back(slot, own, rec, do_o, do_r, o_o, o_r, r_o, r_r, e, erem):
    half, w = own.shape
    inner = w // 3
    np_ = inner // 128
    full = 2 * half
    nb = full // BQ
    rem = full - nb * BQ
    last = np_ * nb
    whole = lambda shape, **kw: pl.BlockSpec(shape, lambda t: (0,) * len(shape), **kw)
    one = dict(pipeline_mode=pl.Buffered(1))
    return pl.pallas_call(
        functools.partial(attend_back_kernel, nb=nb, np_=np_, rem=rem),
        grid=(last + 1,),
        in_specs=[whole((half, w), **one)] * 2
        + [whole((half, inner), **one), pl.BlockSpec((None, half, inner), lambda t: (slot, 0, 0), **one)]
        + [whole((half, inner), **one)] * 4
        + [pl.BlockSpec((1, 2, full, BQ), lambda t: (jnp.minimum(t, last - 1), 0, 0, 0)), whole(erem.shape, **one)],
        out_specs=[whole((half, w), **one)] * 2,
        out_shape=[jax.ShapeDtypeStruct((half, w), BF)] * 2,
        scratch_shapes=[
            pltpu.VMEM((full, inner), BF), pltpu.VMEM((full, inner), BF), pltpu.VMEM((full, inner), BF),
            pltpu.VMEM((inner, full), BF), pltpu.VMEM((full, inner), BF), pltpu.VMEM((full, inner), F32),
            pltpu.VMEM((2, full, BQ), BF), pltpu.VMEM((full, inner), BF),
            pltpu.VMEM((full, inner), F32), pltpu.VMEM((full, inner), F32)],
        cost_estimate=pl.CostEstimate(flops=COST, bytes_accessed=0, transcendentals=0),
        compiler_params=pltpu.CompilerParams(vmem_limit_bytes=62 * 1024 * 1024),
    )(own, rec, do_o, do_r, o_o, o_r, r_o, r_r, e, erem)


def matmul(left, right):
    return jnp.dot(left, right, preferred_element_type=jnp.float32)


def layer_norm(values, gain, shift):
    centred = values - jnp.mean(values, -1, keepdims=True)
    spread = jnp.mean(centred * centred, -1, keepdims=True)
    inverse = lax.rsqrt(spread + EPSILON)
    scaled = centred * inverse
    return (scaled, inverse, scaled * gain + shift)


def norm_back(scaled, inverse, gain, incoming):
    weighted = incoming * gain
    first = jnp.mean(weighted, -1, keepdims=True)
    second = jnp.mean(weighted * scaled, -1, keepdims=True)
    return inverse * (weighted - first - scaled * second)


def fetch_weights(shards):
    return (
        lax.all_gather(shards[0], "grp", axis=0, tiled=True),
        lax.all_gather(shards[1], "grp", axis=0, tiled=True),
        lax.all_gather(shards[2], "grp", axis=0, tiled=True),
        lax.all_gather(shards[3], "grp", axis=0, tiled=True),
        lax.all_gather(shards[4], "grp", axis=1, tiled=True),
        lax.all_gather(shards[5], "grp", axis=1, tiled=True),
        lax.all_gather(shards[6], "grp", axis=0, tiled=True),
    )


def shard_grads(weight_grads):
    return (
        lax.psum_scatter(weight_grads[0], "grp", scatter_dimension=1, tiled=True),
        lax.psum_scatter(weight_grads[1], "grp", scatter_dimension=1, tiled=True),
        lax.psum_scatter(weight_grads[2], "grp", scatter_dimension=0, tiled=True),
        lax.psum_scatter(weight_grads[3], "grp", scatter_dimension=0, tiled=True),
        lax.psum_scatter(weight_grads[4], "grp", scatter_dimension=0, tiled=True),
        lax.psum_scatter(weight_grads[5], "grp", scatter_dimension=0, tiled=True),
        lax.psum_scatter(weight_grads[6], "grp", scatter_dimension=0, tiled=True),
    )


def raw_scores(query, keys):
    rows = query.shape[0]
    length = keys.shape[0]
    return jnp.einsum(
        "qhd,khd->hqk",
        query.reshape(rows, H, HD),
        keys.reshape(length, H, HD),
        preferred_element_type=jnp.float32,
    ) * HD ** (-0.5)


def score_probs(query, keys):
    return jax.nn.softmax(raw_scores(query, keys), axis=-1)


def forward_pass(row_block, gathered):
    qkv_weight, out_weight, up_weight, down_weight, gains, biases, hidden_bias = gathered
    gain_f = gains.astype(jnp.float32)
    bias_f = biases.astype(jnp.float32)
    rows = row_block.shape[0]
    model_width = row_block.shape[1]
    inputs = row_block.astype(jnp.float32)
    scaled1, inverse1, normed = layer_norm(inputs, gain_f[0], bias_f[0])
    normed = normed.astype(jnp.bfloat16)
    shift = jnp.concatenate([bias_f[1], jnp.zeros_like(bias_f[1]), bias_f[2]])
    qkv = (matmul(normed, qkv_weight) + shift).astype(jnp.bfloat16)
    query = qkv[:, :model_width]
    key_part = qkv[:, model_width : 2 * model_width]
    value_part = qkv[:, 2 * model_width :]
    keys, values = (
        lax.all_gather(key_part, "grp", axis=0, tiled=True),
        lax.all_gather(value_part, "grp", axis=0, tiled=True),
    )
    length = keys.shape[0]
    probs = score_probs(query, keys)
    context = (
        jnp.einsum(
            "hqk,khd->qhd",
            probs.astype(jnp.bfloat16),
            values.reshape(length, H, HD),
            preferred_element_type=jnp.float32,
        )
        .reshape(rows, model_width)
        .astype(jnp.bfloat16)
    )
    hidden = inputs + matmul(context, out_weight) + bias_f[3]
    scaled2, inverse2, normed2 = layer_norm(hidden, gain_f[1], bias_f[4])
    normed2 = normed2.astype(jnp.bfloat16)
    pre = matmul(normed2, up_weight) + hidden_bias.astype(jnp.float32)
    active = jax.nn.gelu(pre, approximate=False).astype(jnp.bfloat16)
    result = hidden + matmul(active, down_weight) + bias_f[5]
    saved = (
        scaled1,
        inverse1,
        normed,
        query,
        keys,
        values,
        context,
        scaled2,
        inverse2,
        normed2,
        pre,
        active,
    )
    return (result, saved)


def backward_pass(incoming, weight, saved, gathered):
    qkv_weight, out_weight, up_weight, down_weight, gains, biases, hidden_bias = gathered
    gain_f = gains.astype(jnp.float32)
    (
        scaled1,
        inverse1,
        normed,
        query,
        keys,
        values,
        context,
        scaled2,
        inverse2,
        normed2,
        pre,
        active,
    ) = saved
    rows = query.shape[0]
    model_width = query.shape[1]
    length = keys.shape[0]
    d_out = incoming * weight.astype(jnp.bfloat16)
    d_out_f = d_out.astype(jnp.float32)
    grad_down = jnp.einsum("rf,rd->fd", active, d_out, preferred_element_type=jnp.float32)
    grad_b2 = jnp.sum(d_out_f, 0)
    d_act = jnp.einsum("rd,fd->rf", d_out, down_weight, preferred_element_type=jnp.float32)
    unused, gelu_pull = jax.vjp(lambda inputs: jax.nn.gelu(inputs, approximate=False), pre)
    d_pre = gelu_pull(d_act)[0].astype(jnp.bfloat16)
    grad_up = jnp.einsum("rd,rf->df", normed2, d_pre, preferred_element_type=jnp.float32)
    grad_hidden_bias = jnp.sum(d_pre.astype(jnp.float32), 0)
    d_norm2 = jnp.einsum("rf,df->rd", d_pre, up_weight, preferred_element_type=jnp.float32)
    d_hidden = d_out_f + norm_back(scaled2, inverse2, gain_f[1], d_norm2)
    grad_g2 = jnp.sum(d_norm2 * scaled2, 0)
    grad_beta2 = jnp.sum(d_norm2, 0)
    d_branch = d_hidden.astype(jnp.bfloat16)
    grad_out = jnp.einsum("rd,re->de", context, d_branch, preferred_element_type=jnp.float32)
    grad_bo = jnp.sum(d_branch.astype(jnp.float32), 0)
    d_context = jnp.einsum(
        "re,de->rd", d_branch, out_weight, preferred_element_type=jnp.float32
    ).astype(jnp.bfloat16)
    scores = raw_scores(query, keys)
    probs = jax.nn.softmax(scores, axis=-1)
    context_heads = d_context.reshape(rows, H, HD)
    d_probs = jnp.einsum(
        "qhd,khd->hqk",
        context_heads,
        values.reshape(length, H, HD),
        preferred_element_type=jnp.float32,
    )
    delta = jnp.sum(probs * d_probs, -1)
    d_scores = (probs * (d_probs - delta[..., None])).astype(jnp.bfloat16)
    d_query = (
        jnp.einsum(
            "hqk,khd->qhd",
            d_scores,
            keys.reshape(length, H, HD),
            preferred_element_type=jnp.float32,
        )
        * HD ** (-0.5)
    ).reshape(rows, model_width)
    d_value = jnp.einsum(
        "hqk,qhd->khd",
        probs.astype(jnp.bfloat16),
        context_heads,
        preferred_element_type=jnp.float32,
    ).reshape(length, model_width)
    d_key = (
        jnp.einsum(
            "hqk,qhd->khd", d_scores, query.reshape(rows, H, HD), preferred_element_type=jnp.float32
        )
        * HD ** (-0.5)
    ).reshape(length, model_width)
    d_key, d_value = (
        lax.psum_scatter(d_key, "grp", scatter_dimension=0, tiled=True),
        lax.psum_scatter(d_value, "grp", scatter_dimension=0, tiled=True),
    )
    d_qkv = jnp.concatenate(
        [d_query.astype(jnp.bfloat16), d_key.astype(jnp.bfloat16), d_value.astype(jnp.bfloat16)], 1
    )
    grad_qkv = jnp.einsum("rd,re->de", normed, d_qkv, preferred_element_type=jnp.float32)
    d_qkv_f = d_qkv.astype(jnp.float32)
    grad_bq = jnp.sum(d_qkv_f[:, :model_width], 0)
    grad_bv = jnp.sum(d_qkv_f[:, 2 * model_width :], 0)
    d_norm1 = jnp.einsum("re,de->rd", d_qkv, qkv_weight, preferred_element_type=jnp.float32)
    row_grad = d_hidden + norm_back(scaled1, inverse1, gain_f[0], d_norm1)
    grad_g1 = jnp.sum(d_norm1 * scaled1, 0)
    grad_beta1 = jnp.sum(d_norm1, 0)
    grad_gains = jnp.stack([grad_g1, grad_g2])
    grad_biases = jnp.stack([grad_beta1, grad_bq, grad_bv, grad_bo, grad_beta2, grad_b2])
    weight_grads = (
        grad_gains,
        grad_biases,
        grad_hidden_bias,
        grad_qkv,
        grad_out,
        grad_up,
        grad_down,
    )
    return (row_grad, weight_grads)


def plain_body(clips, clip_count, cotangent, norm_gain, bias_d, bias_ff, w_qkv, w_o, w_up, w_down):
    shards = (w_qkv, w_o, w_up, w_down, norm_gain, bias_d, bias_ff)
    number = clips.shape[0]
    outputs = []
    records = []
    actives = []
    for slot_index in range(number):
        gathered = fetch_weights(shards)
        active = (clip_count[0] > slot_index).astype(jnp.float32)
        result, saved = forward_pass(clips[slot_index], gathered)
        outputs.append((result * active).astype(jnp.bfloat16))
        records.append(saved)
        actives.append(active)
    row_grads = [None] * number
    totals = None
    for slot_index in reversed(range(number)):
        gathered = fetch_weights(shards)
        row_grad, weight_grads = backward_pass(
            cotangent[slot_index], actives[slot_index], records[slot_index], gathered
        )
        row_grads[slot_index] = row_grad
        totals = (
            weight_grads
            if totals is None
            else jax.tree.map(lambda left, right: left + right, totals, weight_grads)
        )
    totals = shard_grads(totals)
    small_sums = lax.psum((totals[0], totals[1], totals[2]), "rep")
    matrix_sums = (
        lax.psum_scatter(totals[3], "rep", scatter_dimension=1, tiled=True),
        lax.psum_scatter(totals[4], "rep", scatter_dimension=1, tiled=True),
        lax.psum_scatter(totals[5], "rep", scatter_dimension=1, tiled=True),
        lax.psum_scatter(totals[6], "rep", scatter_dimension=1, tiled=True),
    )
    return (jnp.stack(outputs), jnp.stack(row_grads)) + tuple(small_sums) + tuple(matrix_sums)


def row_stats(values):
    centred = values - jnp.mean(values, -1, keepdims=True)
    inverse = lax.rsqrt(jnp.mean(centred * centred, -1, keepdims=True) + EPSILON)
    return centred * inverse, inverse


def whole(shape, **kw):
    return pl.BlockSpec(shape, lambda *_: (0,) * len(shape), **kw)


def call(kernel, ids, grid, in_specs, out_specs, out_shape, args, scratch=(), flops=0, limit=60, aliases=()):
    return pl.pallas_call(
        kernel,
        grid_spec=pltpu.PrefetchScalarGridSpec(
            num_scalar_prefetch=1, grid=grid, in_specs=in_specs, out_specs=out_specs, scratch_shapes=list(scratch)
        ),
        out_shape=out_shape,
        cost_estimate=pl.CostEstimate(flops=int(flops), bytes_accessed=0, transcendentals=0),
        input_output_aliases=dict(aliases),
        compiler_params=pltpu.CompilerParams(vmem_limit_bytes=limit * 1024 * 1024),
    )(ids, *args)


def slot_of(shape, s):
    return pl.BlockSpec((None,) + shape, lambda *_: (s,) + (0,) * len(shape))


def piece_places(ids):
    y, core = ids[4], ids[0]
    return (2 * y + core, 2 * (1 - y) + core, 2 * y + 1 - core, 2 * (1 - y) + 1 - core)


def lay_pieces(ids, target, pieces):
    size = target.shape[0] // len(pieces)
    for piece, place in zip(pieces, piece_places(ids)):
        target[pl.ds(pl.multiple_of(place * size, size), size)] = piece[...]


def by_rows(ids, x, near, far):
    size = near.shape[0]
    own = pl.ds(pl.multiple_of(ids[3] * size, size), size)
    across = pl.ds(pl.multiple_of((1 - ids[3]) * size, size), size)
    return nn(x[:, own], near[...]) + nn(x[:, across], far[...])


def project_other_kernel(ids, mine, got, gain, shift, near, p0, p1, p2, p3, bias, block, normed, out, far_s):
    @pl.when(pl.program_id(0) == 0)
    def _():
        x = jnp.where(ids[1] == 1, got[...], mine[...])
        block[...] = x
        hat, unused = row_stats(x.astype(F32))
        normed[...] = (hat * gain[...] + shift[...]).astype(BF)

    lay_pieces(ids, far_s, (p0, p1, p2, p3))
    out[...] = (by_rows(ids, normed, near, far_s) + bias[...]).astype(BF)


def project_other(ids, mine, mine_slot, got, got_slot, gain, shift, near, far, bias):
    rows, width = mine.shape[1:]
    inner = width // 2
    columns = lambda i, ids: (0, 2 * i + 1 - ids[0])
    return call(
        project_other_kernel,
        ids,
        (3,),
        [
            slot_of((rows, width), mine_slot),
            slot_of((rows, width), got_slot),
            whole((1, width)),
            whole((1, width)),
            pl.BlockSpec((inner, inner), columns),
        ]
        + [pl.BlockSpec((inner // 4, inner), columns)] * 4
        + [pl.BlockSpec((1, inner), columns)],
        [whole((rows, width)), whole((rows, width)), pl.BlockSpec((rows, inner), lambda i, ids: (0, i))],
        [
            jax.ShapeDtypeStruct((rows, width), BF),
            jax.ShapeDtypeStruct((rows, width), BF),
            jax.ShapeDtypeStruct((rows, 3 * inner), BF),
        ],
        (mine, got, gain, shift, near, *far, bias),
        scratch=[pltpu.VMEM((inner, inner), BF)],
    )


def project_mine_kernel(ids, normed, near, p0, p1, p2, p3, bias, out, far_s):
    lay_pieces(ids, far_s, (p0, p1, p2, p3))
    out[...] = (by_rows(ids, normed, near, far_s) + bias[...]).astype(BF)


def project_mine(ids, normed, near, far, bias):
    rows, width = normed.shape
    inner = width // 2
    columns = lambda i, ids: (0, 2 * i + ids[0])
    return call(
        project_mine_kernel,
        ids,
        (3,),
        [whole((rows, width)), pl.BlockSpec((inner, inner), columns)]
        + [pl.BlockSpec((inner // 4, inner), columns)] * 4
        + [pl.BlockSpec((1, inner), columns)],
        pl.BlockSpec((rows, inner), lambda i, ids: (0, i)),
        jax.ShapeDtypeStruct((rows, 3 * inner), BF),
        (normed, near, *far, bias),
        scratch=[pltpu.VMEM((inner, inner), BF)],
    )


def feed_kernel(
    ids, block, ctx_mine, ctx_other, cot_mine, cot_got, out_near, o0, o1, o2, o3, up_near, u0, u1, u2, u3,
    down_near, d0, d1, d2, d3, gain, biases, bias_hidden, *rest,
):
    (
        active, d_pre, normed2, d_out, result, d_branch, d_ctx_mine, d_ctx_other, sums, sum_hidden,
        hidden_s, total_s, d_norm_s, up_far, w_down,
    ) = rest[-15:]
    j = pl.program_id(0)
    half = pl.num_programs(0) // 2
    inner = ctx_mine.shape[1]
    live = ids[2].astype(F32)
    own = pl.ds(pl.multiple_of(ids[3] * inner, inner), inner)
    across = pl.ds(pl.multiple_of((1 - ids[3]) * inner, inner), inner)
    lay_pieces(ids, up_far, (u0, u1, u2, u3))

    out_far = w_down.at[:inner]

    straight = ids[0] == ids[3]

    @pl.when(j == 0)
    def _():
        lay_pieces(ids, out_far, (o0, o1, o2, o3))
        w_mine = jnp.where(straight, out_near[...], out_far[...])
        w_other = jnp.where(straight, out_far[...], out_near[...])
        hidden = block[...].astype(F32) + (nn(ctx_mine[...], w_mine) + nn(ctx_other[...], w_other))
        hidden = hidden + biases[3:4]
        hidden_s[...] = hidden
        hat, unused = row_stats(hidden)
        normed2[...] = (hat * gain[1:2] + biases[4:5]).astype(BF)
        d = (jnp.where(ids[1] == 1, cot_got[...], cot_mine[...]).astype(F32) * live).astype(BF)
        d_out[...] = d

    @pl.when(j < half)
    def _():
        w_down[...] = down_near[...]

    @pl.when(j >= half)
    def _():
        here = ids[4] == j - half
        size = d0.shape[0]
        w_down[pl.ds(pl.multiple_of(ids[0] * size, size), size)] = jnp.where(here, d0[...], d1[...])
        w_down[pl.ds(pl.multiple_of((1 - ids[0]) * size, size), size)] = jnp.where(here, d2[...], d3[...])

    rows = block.shape[0]
    parts = (slice(0, rows // 32 * 16), slice(rows // 32 * 16, rows))

    def begin(part):
        pre = nn(normed2[part, own], up_near[...]) + nn(normed2[part, across], up_far[...])
        return pre, nt(d_out[part], w_down[...])

    def middle(part, pre, d_act):
        pre = pre + bias_hidden[...]
        phi = 0.5 + 0.5 * lax.erf(pre * 0.7071067811865476)
        act = (pre * phi).astype(BF)
        active[part] = act
        slope = phi + pre * (jnp.exp2(pre * pre * (-0.5 * LOG2E)) * 0.3989422804014327)
        dp = d_act * slope
        total = jnp.sum(dp, 0, keepdims=True)
        dp = dp.astype(BF)
        d_pre[part] = dp
        return act, dp, total

    def end(part, act, dp):
        total_s[part] += nn(act, w_down[...])
        d_norm_s[part, own] += nt(dp, up_near[...])
        d_norm_s[part, across] += nt(dp, up_far[...])

    @pl.when(j == 0)
    def _():
        total_s[...] = jnp.zeros_like(total_s)
        d_norm_s[...] = jnp.zeros_like(d_norm_s)

    first, second = parts
    begun = begin(first)
    begun_second = begin(second)
    act, dp, total = middle(first, *begun)
    end(first, act, dp)
    act, dp, total_second = middle(second, *begun_second)
    end(second, act, dp)
    sum_hidden[...] = jnp.broadcast_to(total + total_second, sum_hidden.shape)

    @pl.when(j == pl.num_programs(0) - 1)
    def _():
        hidden = hidden_s[...]
        result[...] = ((hidden + total_s[...] + biases[5:6]) * live).astype(BF)
        hat, inverse = row_stats(hidden)
        d_norm = d_norm_s[...]
        weighted = d_norm * gain[1:2]
        first = jnp.mean(weighted, -1, keepdims=True)
        second = jnp.mean(weighted * hat, -1, keepdims=True)
        d = d_out[...].astype(F32)
        branch = (d + inverse * (weighted - first - hat * second)).astype(BF)
        d_branch[...] = branch
        sums[...] = jnp.concatenate(
            [
                jnp.sum(d_norm * hat, 0, keepdims=True),
                jnp.sum(d_norm, 0, keepdims=True),
                jnp.sum(branch.astype(F32), 0, keepdims=True),
                jnp.sum(d, 0, keepdims=True),
                jnp.zeros((4, d.shape[1]), F32),
            ],
            0,
        )
        lay_pieces(ids, out_far, (o0, o1, o2, o3))
        w_mine = jnp.where(straight, out_near[...], out_far[...])
        w_other = jnp.where(straight, out_far[...], out_near[...])
        d_ctx_mine[...] = nt(branch, w_mine).astype(BF)
        d_ctx_other[...] = nt(branch, w_other).astype(BF)


def feed(ids, slot, slots, block, ctx_mine, ctx_other, cot_mine, cot_got, got_slot, w_out, w_up, w_down, far, far_down, gain, biases, bias_hidden, before):
    rows, width = block.shape
    inner = width // 2
    ff = w_up.shape[1]
    chunk = width
    steps = ff // chunk
    one = dict(pipeline_mode=pl.Buffered(1))
    full = whole((rows, width), **one)
    part = whole((rows, inner), **one)
    place = lambda j, ids: (0, (ids[3] * (steps // 2) + j) % steps)
    columns = pl.BlockSpec((rows, chunk), place)
    one_slot = lambda shape, at=slot: pl.BlockSpec((None,) + shape, lambda *_: (at, 0, 0), **one)
    wide = jax.ShapeDtypeStruct((rows, width), BF)
    args = (
        block, ctx_mine, ctx_other, cot_mine, cot_got, w_out, *far, w_up, *far, w_down, *far_down, gain, biases, bias_hidden,
    )
    return call(
        feed_kernel,
        ids,
        (steps,),
        [full, part, part, one_slot((rows, width)), one_slot((rows, width), got_slot), whole((inner, width), **one)]
        + [pl.BlockSpec((inner // 4, width), lambda j, ids: (steps, 0), **one)] * 4
        + [pl.BlockSpec((inner, chunk), place)]
        + [pl.BlockSpec((inner // 4, chunk), lambda j, ids: (place(j, ids)[1], 0))] * 4
        + [pl.BlockSpec((chunk, width), lambda j, ids: (jnp.minimum(j, steps // 2 - 1), 0), **one)]
        + [whole((ff // 8, width), **one)] * 4
        + [whole(gain.shape), whole(biases.shape), pl.BlockSpec((1, chunk), place)]
        + [pl.BlockSpec(memory_space=pl.ANY)] * len(before),
        [
            columns, columns, full, full, full, full, part, one_slot((rows, inner)),
            whole((8, width)),
            pl.BlockSpec((8, chunk), place),
        ],
        [
            jax.ShapeDtypeStruct((rows, ff), BF), jax.ShapeDtypeStruct((rows, ff), BF),
            wide, wide, wide, wide,
            jax.ShapeDtypeStruct((rows, inner), BF), jax.ShapeDtypeStruct((slots, rows, inner), BF),
            jax.ShapeDtypeStruct((8, width), F32), jax.ShapeDtypeStruct((8, ff), F32),
        ],
        args + tuple(before),
        scratch=[pltpu.VMEM((rows, width), F32)] * 3
        + [pltpu.VMEM((inner, chunk), BF), pltpu.VMEM((chunk, width), BF)],
        limit=62,
        aliases=[(1 + len(args), 7)] if before else (),
    )


def outer_sum(left, right):
    return tn(jnp.concatenate(left), jnp.concatenate(right))


def put_block(ids, outs, rec, piece, x, y, z, rows):
    place = 2 * (x != ids[3]).astype(jnp.int32) + (y != ids[4]).astype(jnp.int32)
    if rec is None:
        outs[0][place, z, rows] = piece.astype(BF)
        return
    for i, out in enumerate(outs):

        @pl.when(place == i)
        def _(i=i, out=out):
            out[z, rows] = (piece + rec[i, z, rows].astype(F32)).astype(BF)


def split_refs(refs, counts):
    parts, at = [], 0
    for count in counts:
        parts.append(refs[at : at + count])
        at += count
    rest = refs[at:]
    return parts + ([None, rest] if len(rest) == 1 else [rest[0], rest[-4:]])


def grad_down_kernel(ids, *refs, slots):
    left, right, rec, outs = split_refs(refs, (slots, slots))
    step = pl.program_id(0)
    x = jnp.where(step == 0, 1 - ids[3], ids[3])
    total = outer_sum([a[...] for a in left], [b[...] for b in right])
    chips, rows, cols = outs[0].shape[-3:]
    parts = total.shape[1] // cols
    rows = rows // parts
    for z in range(chips):
        for y in range(2):
            at = (2 * z + y) * rows
            for part in range(parts):
                piece = total[at : at + rows, part * cols : (part + 1) * cols]
                put_block(ids, outs, rec, piece, x, jnp.int32(y), z, slice(part * rows, (part + 1) * rows))


def grad_up_kernel(ids, *refs, slots):
    left, first, last, rec, outs = split_refs(refs, (slots, slots, slots))
    z = pl.program_id(0)
    right = [jnp.concatenate([a[...], b[...]], 1) for a, b in zip(first, last)]
    total = outer_sum([a[...] for a in left], right)
    rows, cols = outs[0].shape[-2:]
    for x in range(2):
        for y in range(2):
            piece = total[y * rows : (y + 1) * rows, x * cols : (x + 1) * cols]
            put_block(ids, outs, rec, piece, jnp.int32(x), jnp.int32(y), z, slice(0, rows))


def grad_out_kernel(ids, *refs, slots):
    left, mine, other, rec, outs = split_refs(refs, (slots, slots, slots))
    right = [jnp.concatenate([a[...], b[...]], 1) for a, b in zip(mine, other)]
    total = outer_sum([a[...] for a in left], right)
    chips, rows, cols = outs[0].shape[-3:]
    for near in range(2):
        x = ids[0] if near == 0 else 1 - ids[0]
        for z in range(chips):
            for y in range(2):
                at = (2 * z + y) * rows
                piece = total[at : at + rows, near * cols : (near + 1) * cols]
                put_block(ids, outs, rec, piece, x, jnp.int32(y), z, slice(0, rows))


def grad_qkv_kernel(ids, *refs, slots, steps):
    mine, other, first, last, rec, outs = split_refs(refs, (slots, slots, slots, slots))
    right = [jnp.concatenate([a[...], b[...]], 1) for a, b in zip(first, last)]
    near = outer_sum([a[...] for a in mine], right)
    far = outer_sum([a[...] for a in other], right)
    total = jnp.concatenate([jnp.where(ids[0] == 0, near, far), jnp.where(ids[0] == 0, far, near)])
    chips, rows, cols = outs[0].shape[-3:]
    span = total.shape[0]
    for step in range(steps):

        @pl.when(pl.program_id(0) == step)
        def _(step=step):
            for block in range(2 * chips):
                begin = max(block * rows, step * span)
                end = min((block + 1) * rows, (step + 1) * span)
                if begin >= end:
                    continue
                for x in range(2):
                    piece = total[begin - step * span : end - step * span, x * cols : (x + 1) * cols]
                    put_block(
                        ids, outs, rec, piece, jnp.int32(x), jnp.int32(block % 2), block // 2,
                        slice(begin - block * rows, end - block * rows),
                    )


def grad_call(kernel, ids, grid, groups, shape, rec, flops, joint=None, **kw):
    specs, args = [], []
    for arrays, block, index in groups:
        specs += [pl.BlockSpec(block, index)] * len(arrays)
        args += arrays
    if rec is None:
        out_specs, out_shapes, aliases = whole(shape, pipeline_mode=pl.Buffered(1)), jax.ShapeDtypeStruct(shape, BF), ()
    else:
        specs.append(whole(shape, pipeline_mode=pl.Buffered(1)))
        args.append(rec)
        all_rows, at, arrays = joint
        out_specs = [pl.BlockSpec(shape[1:], lambda *_: (0, at, 0), pipeline_mode=pl.Buffered(1))] * 4
        out_shapes = [jax.ShapeDtypeStruct((shape[1], all_rows, shape[3]), BF)] * 4
        aliases = [(1 + len(args) + i, i) for i in range(len(arrays))]
        specs += [pl.BlockSpec(memory_space=pl.ANY)] * len(arrays)
        args += arrays
    return call(
        functools.partial(kernel, slots=len(groups[0][0]), **kw),
        ids, grid, specs, out_specs, out_shapes, tuple(args), flops=flops, aliases=aliases,
    )


def column_half(ids, rec):
    return 1 - ids[0] if rec is None else ids[0]


def grad_down_part(ids, chips, d_out, active, rec, joint=None):
    rows, width = d_out[0].shape
    ff = active[0].shape[1]
    cols = ff // 4
    parts = 4 * cols // width
    block = lambda i, ids: (0, 2 * jnp.where(i == 0, 1 - ids[3], ids[3]) + column_half(ids, rec))
    groups = [(d_out, (rows, width), lambda i, ids: (0, 0)), (active, (rows, cols), block)]
    shape = (4, chips, parts * width // (2 * chips), cols // parts)
    return grad_call(grad_down_kernel, ids, (2,), groups, shape, rec, 0, joint)


def grad_up_part(ids, chips, d_pre, normed, rec, joint=None):
    rows, width = normed[0].shape
    ff = d_pre[0].shape[1]
    cols = width // 4
    groups = [
        (d_pre, (rows, ff // chips), lambda i, ids: (0, i)),
        (normed, (rows, cols), lambda i, ids: (0, column_half(ids, rec))),
        (normed, (rows, cols), lambda i, ids: (0, 2 + column_half(ids, rec))),
    ]
    return grad_call(grad_up_kernel, ids, (chips,), groups, (4, chips, ff // (2 * chips), cols), rec, 0, joint)


def grad_out_part(ids, chips, d_branch, mine, other, rec, joint=None):
    rows, width = d_branch[0].shape
    cols = width // 4
    half = lambda i, ids: (0, column_half(ids, rec))
    groups = [(d_branch, (rows, width), lambda i, ids: (0, 0)), (mine, (rows, cols), half), (other, (rows, cols), half)]
    return grad_call(grad_out_kernel, ids, (1,), groups, (4, chips, width // (2 * chips), cols), rec, 0, joint)


def grad_qkv_part(ids, chips, mine, other, normed, rec, joint=None):
    rows, width = normed[0].shape
    cols = width // 4
    columns = lambda i, ids: (0, i)
    groups = [
        (mine, (rows, width // 2), columns),
        (other, (rows, width // 2), columns),
        (normed, (rows, cols), lambda i, ids: (0, column_half(ids, rec))),
        (normed, (rows, cols), lambda i, ids: (0, 2 + column_half(ids, rec))),
    ]
    flops = COST // 2
    return grad_call(
        grad_qkv_kernel, ids, (3,), groups, (4, chips, 3 * width // (2 * chips), cols), rec, flops, joint, steps=3
    )


def add_kernel(ids, *refs):
    refs[-1][...] = sum(term[...].astype(F32) for term in refs[:-1]).astype(BF)


def add_chips(ids, terms, chips, rows):
    cols = terms[0].shape[1]
    return call(
        add_kernel,
        ids,
        (chips,),
        [pl.BlockSpec((rows, cols), lambda i, ids: (ids[5] ^ i, 0))] * len(terms),
        pl.BlockSpec((None, rows, cols), lambda i, ids: (i, 0, 0)),
        jax.ShapeDtypeStruct((chips, rows, cols), BF),
        tuple(terms),
    )


def finish_kernel(
    ids, d_mine, d_other, mine_near, m0, m1, m2, m3, other_near, o0, o1, o2, o3, block, d_hidden, gain,
    row_grad, sums, sum_mine, sum_other, total_s, mine_far, other_far,
):
    i = pl.program_id(0)
    size = mine_near.shape[0]
    lay_pieces(ids, mine_far, (m0, m1, m2, m3))
    lay_pieces(ids, other_far, (o0, o1, o2, o3))
    own = pl.ds(pl.multiple_of(ids[3] * size, size), size)
    across = pl.ds(pl.multiple_of((1 - ids[3]) * size, size), size)
    term = nt(d_mine[...], mine_near[...]) + nt(d_other[...], other_near[...])
    term_far = nt(d_mine[...], mine_far[...]) + nt(d_other[...], other_far[...])
    sum_mine[...] = jnp.broadcast_to(jnp.sum(d_mine[...].astype(F32), 0, keepdims=True), sum_mine.shape)
    sum_other[...] = jnp.broadcast_to(jnp.sum(d_other[...].astype(F32), 0, keepdims=True), sum_other.shape)

    @pl.when(i == 0)
    def _():
        total_s[:, own] = term
        total_s[:, across] = term_far

    @pl.when(i > 0)
    def _():
        total_s[:, own] += term
        total_s[:, across] += term_far

    @pl.when(i == pl.num_programs(0) - 1)
    def _():
        hat, inverse = row_stats(block[...].astype(F32))
        d_norm = total_s[...]
        weighted = d_norm * gain[0:1]
        first = jnp.mean(weighted, -1, keepdims=True)
        second = jnp.mean(weighted * hat, -1, keepdims=True)
        row_grad[...] = (d_hidden[...].astype(F32) + inverse * (weighted - first - hat * second)).astype(BF)
        sums[...] = jnp.concatenate(
            [jnp.sum(d_norm * hat, 0, keepdims=True), jnp.sum(d_norm, 0, keepdims=True), jnp.zeros((6, d_norm.shape[1]), F32)], 0
        )


def finish(ids, d_mine, d_other, near, far, block, d_hidden, gain):
    rows, width = block.shape
    inner = width // 2
    full = whole((rows, width))
    part = pl.BlockSpec((rows, inner), lambda i, ids: (0, i))
    row = pl.BlockSpec((8, inner), lambda i, ids: (0, i))
    mine = lambda i, ids: (0, 2 * i + ids[0])
    other = lambda i, ids: (0, 2 * i + 1 - ids[0])
    return call(
        finish_kernel,
        ids,
        (3,),
        [
            part, part,
            pl.BlockSpec((inner, inner), mine), *[pl.BlockSpec((inner // 4, inner), mine)] * 4,
            pl.BlockSpec((inner, inner), other), *[pl.BlockSpec((inner // 4, inner), other)] * 4,
            full, full, whole(gain.shape),
        ],
        [full, whole((8, width)), row, row],
        [
            jax.ShapeDtypeStruct((rows, width), BF), jax.ShapeDtypeStruct((8, width), F32),
            jax.ShapeDtypeStruct((8, 3 * inner), F32), jax.ShapeDtypeStruct((8, 3 * inner), F32),
        ],
        (d_mine, d_other, near, *far, near, *far, block, d_hidden, gain),
        scratch=[pltpu.VMEM((rows, width), F32)] + [pltpu.VMEM((inner, inner), BF)] * 2,
        flops=COST,
    )


def swap_axis(x, axis, step=1):
    size = lax.axis_size(axis)
    return lax.ppermute(x, axis, [(i, i ^ step) for i in range(size)])


def swap_across(x):
    return lax.ppermute(x, ("mid", "grp"), [(0, 3), (1, 2), (2, 1), (3, 0)])


def swap_owner(x, chips):
    pairs = []
    for k in range(2 * chips):
        pairs += [(4 * k + 1, 4 * k + 2), (4 * k + 2, 4 * k + 1)]
    return lax.ppermute(x, AXES, pairs)


def after(values, first):
    return lax.optimization_barrier((values, first))[0]


def in_order(index, mine, other, axis=0):
    return jnp.concatenate([jnp.where(index == 0, mine, other), jnp.where(index == 0, other, mine)], axis)


def own_half(x, index, axis=0):
    size = x.shape[axis] // 2
    return lax.dynamic_slice_in_dim(x, index * size, size, axis)


def send_piece(piece):
    return swap_axis(piece, "grp")


def own_piece(shard):
    place = 2 * lax.axis_index("mid") + lax.axis_index("core")
    part = shard.shape[0] // 4
    return lax.dynamic_slice_in_dim(shard, place * part, part, 0)


def as_lines(x, cols):
    parts = []
    for _ in range(3):
        part = lax.reduce_precision(x, 8, 7)
        parts.append(part.astype(BF))
        x = x - part
    return jnp.concatenate(parts).reshape(-1, cols)


def from_lines(lines, shape):
    return lines.astype(F32).reshape((3,) + shape).sum(0)


def send_sums(part):
    return [part[0], swap_axis(part[1], "mid"), swap_axis(part[2], "grp"), swap_across(part[3])]


def send_chips(part):
    return [part[0]] + [swap_axis(part[i], "z", i) for i in range(1, lax.axis_size("z"))]


def settle(total, parts, core):
    mine = jnp.concatenate([lax.dynamic_index_in_dim(part, core, 0, False) for part in parts])
    other = jnp.concatenate([lax.dynamic_index_in_dim(part, 1 - core, 0, False) for part in parts])
    return mine, swap_axis(other, "core")


def body(chips, clips, clip_count, cotangent, norm_gain, bias_d, bias_ff, w_qkv, w_o, w_up, w_down):
    core, x, y, z = (lax.axis_index(axis) for axis in ("core", "grp", "mid", "z"))
    slots, half, width = clips.shape
    inner = width // 2
    ff = w_up.shape[1]
    swap = (core != x).astype(jnp.int32)

    qkv_piece = own_piece(w_qkv)
    small = jnp.concatenate([norm_gain.reshape(-1), bias_d.reshape(-1), bias_ff]).reshape(-1, 128)
    qkv_0 = send_piece(qkv_piece)
    got_small = swap_axis(after(small, qkv_piece), "grp")
    got_first = swap_owner(after(clips[:1], qkv_piece), chips)
    other_count = swap_axis(clip_count, "core")
    qkv_1 = swap_axis(qkv_0, "mid")
    qkv_2 = swap_axis(qkv_0, "core")
    rest = after(clips[1:], qkv_0)
    got_rest = swap_owner(rest, chips)
    piece = own_piece(w_up).reshape(-1, ff // width, width).transpose(1, 0, 2).reshape(-1, width)
    piece = jnp.concatenate([piece, own_piece(w_o)])
    down_piece = own_piece(w_down)
    qkv_3 = swap_axis(qkv_1, "core")
    qkv_far = (qkv_0, qkv_1, qkv_2, qkv_3)
    piece, down_piece = after((piece, down_piece), qkv_1)
    far_0 = send_piece(piece)
    down_0 = send_piece(down_piece)

    pair = in_order(x, small[None], got_small[None]).reshape(2, -1).astype(F32)
    gains = pair[:, : 2 * inner].reshape(2, 2, inner).transpose(1, 0, 2).reshape(2, width)
    biases = pair[:, 2 * inner : 8 * inner].reshape(2, 6, inner).transpose(1, 0, 2).reshape(6, width)
    bias_hidden = pair[:, 8 * inner :].reshape(1, -1)
    count = jnp.where(swap == 1, other_count, clip_count)[0]
    qkv_bias = jnp.concatenate([biases[1], jnp.zeros_like(biases[1]), biases[2]])[None]
    ids = [jnp.stack([core, swap, (count > s).astype(jnp.int32), x, y, z]).astype(jnp.int32) for s in range(slots)]

    got_first = after(got_first, (rest, piece, down_piece))
    blocks, normed, saved, ctx_mine, ctx_other = [], [], [], [], []
    for s in range(slots):
        got, slot = (got_first, 0) if s == 0 else (got_rest, s - 1)
        block, norm, other = project_other(ids[s], clips, s, got, slot, gains[0:1], biases[0:1], w_qkv, qkv_far, qkv_bias)
        received = swap_axis(other, "core")
        mine = project_mine(ids[s], norm, w_qkv, qkv_far, qkv_bias)
        here, there, r_here, r_there, weights, weights_rem = attend(mine, received)
        saved.append((mine, received, here, there, r_here, r_there, weights, weights_rem))
        ctx_mine.append(here)
        ctx_other.append(swap_axis(there, "core"))
        blocks.append(block)
        normed.append(norm)
        if s == 0:
            down_0 = after(down_0, here)
            down_1 = swap_axis(down_0, "mid")
            down_2 = swap_axis(down_0, "core")
            got_rest = after(got_rest, (here, down_0))
        elif s == 1:
            down_1, far_0 = after((down_1, far_0), here)
            down_3 = swap_axis(down_1, "core")
            far_1 = swap_axis(far_0, "mid")
            far_2 = swap_axis(far_0, "core")
            got_rest = after(got_rest, (here, down_1, far_0))
        elif s == 2:
            far_1 = after(far_1, here)
            far_3 = swap_axis(far_1, "core")
    far = (far_0, far_1, far_2, far_3)
    far_down = (down_0, down_1, down_2, down_3)

    first, others = swap_owner(cotangent[:1], chips), swap_owner(cotangent[1:], chips)
    got_cot = [(first, 0)] + [(others, s - 1) for s in range(1, slots)]
    fed, got_result = [], []
    before = ()
    for s in range(slots):
        if s == 2:
            got_cot[s] = (after(others, got_result[0]), s - 1)
        fed.append(
            feed(
                ids[s], s, slots, blocks[s], ctx_mine[s], ctx_other[s], cotangent, *got_cot[s], w_o, w_up, w_down, far, far_down,
                gains, biases, bias_hidden, before,
            )
        )
        before = (fed[-1][7],)
        got_result.append(swap_owner(fed[-1][4], chips))
    active, d_pre, normed2, d_out, result, d_branch, d_ctx_mine, d_ctx_other, sums2, sums_hidden = map(list, zip(*fed))
    d_ctx_got = swap_axis(d_ctx_other[-1], "core")

    sent_down = grad_down_part(ids[0], chips, after(d_out, got_result[1]), active, None)
    sent_up = grad_up_part(ids[0], chips, d_pre, normed2, None)
    sent_out = grad_out_part(ids[0], chips, d_branch, ctx_mine, ctx_other, None)
    rows_down, rows_up, rows_out = (part.shape[2] for part in (sent_down, sent_up, sent_out))
    rows = rows_down + rows_up + rows_out
    joint = grad_down_part(ids[0], chips, d_out, active, swap_axis(sent_down, "core"), (rows, 0, []))
    joint = grad_up_part(
        ids[0], chips, d_pre, normed2, after(swap_axis(sent_up, "core"), got_result[2]),
        (rows, rows_down // rows_up, joint),
    )
    joint = grad_out_part(
        ids[0], chips, d_branch, ctx_mine, ctx_other, swap_axis(sent_out, "core"),
        (rows, (rows_down + rows_up) // rows_out, joint),
    )
    cols = joint[0].shape[-1]
    sums = send_sums([part.reshape(-1, cols) for part in joint])
    early = jnp.concatenate([sum(sums2)[:4], sum(sums_hidden)[0].reshape(-1, width)])

    got_rows = []
    d_mine, d_other, row_grads, sums1, sums_mine, sums_other = [], [], [], [], [], []

    def complete(s, first):
        row_grad, sum1, sum_mine, sum_other = finish(
            ids[s], d_mine[s], after(d_other[s], first), w_qkv, qkv_far, blocks[s], d_branch[s], gains
        )
        row_grads.append(row_grad)
        got_rows.append(swap_owner(row_grad, chips))
        sums1.append(sum1)
        sums_mine.append(sum_mine[0])
        sums_other.append(sum_other[0])
        return row_grad

    gate = joint
    for s in range(slots):
        mine, received, here, there, r_here, r_there, weights, weights_rem = saved[s]
        d_here, d_there = attend_back(
            s, mine, received, after(d_ctx_mine[s], gate), d_ctx_got, here, there, r_here, r_there, weights, weights_rem
        )
        d_mine.append(d_here)
        d_other.append(swap_axis(d_there, "core"))
        gate = (d_here,)
        if s == 0:
            sums[3] = after(sums[3], d_here)
            gate = (d_here, sums[3])
        elif s == 1:
            sums = add_chips(ids[0], after(sums, d_here), chips, rows)
            gate = sums
            terms = send_chips(sums)
            gate = (gate, [sums[i] for i in range(chips)])
        if s == 2:
            gate = complete(0, (d_here, terms))
            gate = complete(1, gate)
    sent_qkv = grad_qkv_part(ids[0], chips, d_mine, after(d_other, gate), normed, None)
    row_grad = complete(slots - 1, sent_qkv)
    part_qkv = grad_qkv_part(
        ids[0], chips, d_mine, d_other, normed, after(swap_axis(sent_qkv, "core"), (row_grad, got_rows[0])),
        (sent_qkv.shape[2], 0, []),
    )
    total1 = sum(sums1)
    total_mine, total_other = sum(sums_mine), sum(sums_other)
    grad_bq = in_order(core, total_mine[:inner], total_other[:inner])
    grad_bv = in_order(core, total_mine[2 * inner :], total_other[2 * inner :])
    lines = jnp.concatenate(
        [jnp.stack([total1[0], early[0], total1[1], grad_bq, grad_bv, early[2], early[1], early[3]]), early[4:]]
    )
    lines = lines + swap_axis(lines, "core")
    shape = lines.shape
    under = as_lines(lines, cols)
    qkv_rows = part_qkv[0].shape[1]
    qkv_terms = send_sums([jnp.concatenate([part.reshape(-1, cols), under]) for part in part_qkv])

    sums = add_chips(ids[0], qkv_terms, chips, qkv_rows)
    lines = sum(from_lines(term[chips * qkv_rows :], shape) for term in qkv_terms)
    under = as_lines(lines, cols)
    sends = [jnp.concatenate([sums[i], under]) for i in range(chips)]
    qkv_terms = send_chips(sends)
    total = sum(term.astype(F32) for term in after(terms, sends))
    chunks = rows_down // rows_out
    down = total[:rows_down].reshape(chunks, 2, -1, cols).transpose(1, 0, 2, 3).reshape(2, -1, cols)
    up = total[rows_down : rows_down + rows_up].reshape(2, -1, cols)
    out = total[rows_down + rows_up :].reshape(2, -1, cols)
    mine, other = settle(total, (down, up, out), core)
    whole_rows = in_order(core, mine, other, 1)
    n_down, n_up = rows_down // 2, rows_up // 2
    own_down = in_order(core, mine[:n_down].reshape(chunks, -1, cols), other[:n_down].reshape(chunks, -1, cols))
    grad_down = own_down.transpose(0, 2, 1).reshape(2 * chunks * cols, -1)
    grad_up = whole_rows[n_down : n_down + n_up].T
    grad_out = whole_rows[n_down + n_up :].T

    outs = jnp.stack([jnp.where(swap == 1, after(got_result[s], sends), result[s]) for s in range(slots)])
    input_grad = jnp.stack([jnp.where(swap == 1, after(got_rows[s], sends), row_grads[s]) for s in range(slots)]).astype(F32)
    lines = sum(from_lines(term[qkv_rows:], shape) for term in qkv_terms)
    columns = own_half(lines[:8], x, 1)
    hidden_part = own_half(lines[8:], x).reshape(-1)
    total = sum(term[:qkv_rows].astype(F32) for term in qkv_terms)
    mine, other = settle(total, (total.reshape(2, -1, cols),), core)
    grad_qkv = in_order(core, mine, other, 1).T
    return (outs, input_grad, columns[:2], columns[2:], hidden_part, grad_qkv, grad_out, grad_up, grad_down)


def solution(mesh):
    in_specs = (
        P("rep", "grp", None),
        P("rep"),
        P("rep", "grp", None),
        P(None, "grp"),
        P(None, "grp"),
        P("grp"),
        P("grp", None),
        P("grp", None),
        P("grp", None),
        P("grp", None),
    )
    out_specs = (
        P("rep", "grp", None),
        P("rep", "grp", None),
        P(None, "grp"),
        P(None, "grp"),
        P("grp"),
        P("grp", "rep"),
        P("grp", "rep"),
        P("grp", "rep"),
        P("grp", "rep"),
    )
    if mesh.shape["grp"] != 2 or mesh.shape["rep"] != 16:
        return jax.shard_map(plain_body, mesh=mesh, in_specs=in_specs, out_specs=out_specs, check_vma=False)
    chips = mesh.shape["rep"] // 4
    split = Mesh(mesh.devices.reshape(chips, 2, 2, 2), AXES)
    rep = lambda spec: P(*[AXES[:3] if axis == "rep" else axis for axis in spec])
    return jax.shard_map(
        functools.partial(body, chips),
        mesh=split,
        in_specs=tuple(rep(spec) for spec in in_specs),
        out_specs=tuple(rep(spec) for spec in out_specs),
        check_vma=False,
    )
```

```python
import functools

import jax
import jax.numpy as jnp
from jax import lax
from jax.experimental import pallas as pl
from jax.experimental.pallas import tpu as pltpu
from jax.sharding import Mesh
from jax.sharding import PartitionSpec as P

H = 16
HD = 64
EPSILON = 1e-06

F32 = jnp.float32
BF = jnp.bfloat16
LOG2E = 1.4426950408889634
SCALE = HD ** -0.5
AXES = ("z", "mid", "core", "grp")
BQ = 512
TK = 224
COST = 5 * 10**10
LIMIT = 70.0


def dot(a, b, dims):
    return lax.dot_general(a, b, (dims, ((), ())), preferred_element_type=F32)


def nt(a, b):
    return dot(a, b, ((1,), (1,)))


def nn(a, b):
    return dot(a, b, ((1,), (0,)))


def tn(a, b):
    return dot(a, b, ((0,), (0,)))


def pair_mask(a):
    lane = lax.broadcasted_iota(jnp.int32, (1, 128), 1)
    return (lane < HD) if a == 0 else (lane >= HD)

def norm_peak(x, np_):
    inner = x.shape[1]
    r = lax.broadcasted_iota(jnp.int32, (inner, 128), 0)
    c = lax.broadcasted_iota(jnp.int32, (inner, 128), 1)
    ones = jnp.where(r // HD == c, 1.0, 0.0).astype(BF)
    xf = x.astype(F32)
    return jnp.max(nn((xf * xf).astype(BF), ones), axis=0, keepdims=True)

def attend_kernel(own, rec, oo, orr, ro, rr, p_out, prem_out, q_s, k_s, vt_s, o_s, r_s, fast, *, nb, np_, rem):
    half = own.shape[0]
    inner = own.shape[1] // 3
    full = 2 * half
    t = pl.program_id(0)
    last = np_ * nb

    @pl.when(t == 0)
    def _():
        q_s[:half] = own[:, :inner]
        q_s[half:] = rec[:, :inner]
        k_s[:half] = own[:, inner:2 * inner]
        k_s[half:] = rec[:, inner:2 * inner]
        row = lax.broadcasted_iota(jnp.int32, (128, 1), 0)
        for p in range(np_):
            cols = slice(2 * inner + p * 128, 2 * inner + (p + 1) * 128)
            vt = jnp.concatenate([own[:, cols], rec[:, cols]], axis=0).T
            for a in range(2):
                mine = (row < HD) if a == 0 else (row >= HD)
                vt_s[2 * p + a] = jnp.where(mine, vt, 1.0).astype(BF)
        peak = jnp.max(norm_peak(q_s[...], np_) * norm_peak(k_s[...], np_))
        fast[0] = (peak * (1.1 * SCALE * SCALE) < LIMIT * LIMIT).astype(jnp.int32)

    def store(o, rows, cols):
        oa, ob = o
        ra = 1.0 / oa[HD:]
        rb = 1.0 / ob[:HD]
        o_s[rows, cols] = jnp.concatenate([oa[:HD] * ra, ob[HD:] * rb], axis=0).T.astype(BF)
        r_s[rows, cols] = jnp.concatenate([ra, rb], axis=0).T

    def main(quick):
        p = t // nb
        b = t % nb
        rows = pl.ds(pl.multiple_of(b * BQ, BQ), BQ)
        cols = pl.ds(pl.multiple_of(p * 128, 128), 128)
        q = q_s[rows, cols]
        def weights(a):
            qa = jnp.where(pair_mask(a), q, 0.0).astype(BF)
            if quick:
                for j in range(full // TK):
                    tile = slice(j * TK, (j + 1) * TK)
                    s = nt(k_s[tile, cols], qa)
                    p_out[0, a, tile] = jnp.exp2(s * (LOG2E * SCALE)).astype(BF)
            else:
                s = nt(k_s[:, cols], qa)
                m = jnp.max(s, axis=0, keepdims=True)
                p_out[0, a] = jnp.exp2((s - m) * (LOG2E * SCALE)).astype(BF)
        weights(0)
        weights(1)
        oa = nn(vt_s[2 * p], p_out[0, 0])
        ob = nn(vt_s[2 * p + 1], p_out[0, 1])
        store((oa, ob), rows, cols)

    @pl.when((t < last) & (fast[0] == 1))
    def _():
        main(True)

    @pl.when((t < last) & (fast[0] == 0))
    def _():
        main(False)

    @pl.when(t == last)
    def _():
        if rem:
            lane = lax.broadcasted_iota(jnp.int32, (1, 256), 1)
            for u in range(np_ // 2):
                q = q_s[nb * BQ:, u * 256:(u + 1) * 256]
                qd = jnp.concatenate([jnp.where(lane // HD == h, q, 0.0).astype(BF) for h in range(4)], axis=0)
                s = nt(k_s[:, u * 256:(u + 1) * 256], qd)
                m = jnp.max(s, axis=0, keepdims=True)
                prem_out[u] = jnp.exp2((s - m) * (LOG2E * SCALE)).astype(BF)
                for v in range(2):
                    oa = nn(vt_s[4 * u + 2 * v], prem_out[u])
                    ob = nn(vt_s[4 * u + 2 * v + 1], prem_out[u])
                    ra = 1.0 / oa[HD:]
                    rb = 1.0 / ob[:HD]
                    x = jnp.concatenate([oa[:HD] * ra, ob[HD:] * rb], axis=0).T
                    r = jnp.concatenate([ra, rb], axis=0).T
                    ha, hb = 2 * v, 2 * v + 1
                    pick = lambda y: jnp.where(pair_mask(0), y[ha * rem:(ha + 1) * rem], y[hb * rem:(hb + 1) * rem])
                    cols = slice((2 * u + v) * 128, (2 * u + v + 1) * 128)
                    o_s[nb * BQ:, cols] = pick(x).astype(BF)
                    r_s[nb * BQ:, cols] = pick(r)
        oo[...] = o_s[:half]
        orr[...] = o_s[half:]
        ro[...] = r_s[:half]
        rr[...] = r_s[half:]

def attend(own, rec):
    half, w = own.shape
    inner = w // 3
    np_ = inner // 128
    full = 2 * half
    nb = full // BQ
    rem = full - nb * BQ
    last = np_ * nb
    whole = lambda shape: pl.BlockSpec(shape, lambda t: (0,) * len(shape))
    return pl.pallas_call(
        functools.partial(attend_kernel, nb=nb, np_=np_, rem=rem),
        grid=(last + 1,),
        in_specs=[whole((half, w))] * 2,
        out_specs=[whole((half, inner))] * 4 + [pl.BlockSpec((1, 2, full, BQ), lambda t: (jnp.minimum(t, last - 1), 0, 0, 0)), whole((np_ // 2, full, 4 * rem))],
        out_shape=[jax.ShapeDtypeStruct((half, inner), BF)] * 2 + [jax.ShapeDtypeStruct((half, inner), F32)] * 2
        + [jax.ShapeDtypeStruct((last, 2, full, BQ), BF), jax.ShapeDtypeStruct((np_ // 2, full, 4 * rem), BF)],
        scratch_shapes=[
            pltpu.VMEM((full, inner), BF), pltpu.VMEM((full, inner), BF), pltpu.VMEM((2 * np_, 128, full), BF),
            pltpu.VMEM((full, inner), BF), pltpu.VMEM((full, inner), F32), pltpu.SMEM((1,), jnp.int32)],
        cost_estimate=pl.CostEstimate(flops=0, bytes_accessed=0, transcendentals=0),
        compiler_params=pltpu.CompilerParams(vmem_limit_bytes=60 * 1024 * 1024),
    )(own, rec)


def attend_back_kernel(own, rec, do_o, do_r, o_o, o_r, r_o, r_r, e, erem, out_o, out_r,
               q_s, k_s, v_s, kt_s, do_s, pr_s, ds_s, dq_s, dk_s, dv_s, *, nb, np_, rem):
    half = own.shape[0]
    inner = own.shape[1] // 3
    full = 2 * half
    t = pl.program_id(0)
    last = np_ * nb

    @pl.when(t == 0)
    def _():
        for lo, src, d, o, r in ((0, own, do_o, o_o, r_o), (half, rec, do_r, o_r, r_r)):
            rows = slice(lo, lo + half)
            q_s[rows] = src[:, :inner]
            k_s[rows] = src[:, inner:2 * inner]
            v_s[rows] = src[:, 2 * inner:]
            dn = (d[...].astype(F32) * r[...]).astype(BF)
            do_s[rows] = dn
            pr_s[rows] = dn.astype(F32) * o[...].astype(F32)
        for p in range(np_):
            kt_s[p * 128:(p + 1) * 128] = k_s[:, p * 128:(p + 1) * 128].T
        dk_s[...] = jnp.zeros_like(dk_s)
        dv_s[...] = jnp.zeros_like(dv_s)

    @pl.when(t < last)
    def _():
        p = t // nb
        b = t % nb
        rows = pl.ds(pl.multiple_of(b * BQ, BQ), BQ)
        cols = pl.ds(pl.multiple_of(p * 128, 128), 128)
        q = q_s[rows, cols]
        dn = do_s[rows, cols]
        prod = pr_s[rows, cols].T
        qs, dns = [], []
        for a in range(2):
            qs.append(jnp.where(pair_mask(a), q, 0.0).astype(BF))
            dns.append(jnp.where(pair_mask(a), dn, 0.0).astype(BF))
        for a in range(2):
            delta = jnp.sum(prod[a * HD:(a + 1) * HD], axis=0, keepdims=True)
            for j in range(full // TK):
                tile = slice(j * TK, (j + 1) * TK)
                dp = nt(v_s[tile, cols], dns[a])
                ds_s[a, tile] = (e[0, a, tile].astype(F32) * (dp - delta)).astype(BF)
        for j in range(full // TK):
            tile = slice(j * TK, (j + 1) * TK)
            dv_s[tile, cols] += nn(e[0, 0, tile], dns[0]) + nn(e[0, 1, tile], dns[1])
        dqt = []
        for a in range(2):
            dqt.append(nn(kt_s[pl.ds(pl.multiple_of(p * 128, 128), 128)], ds_s[a])[a * HD:(a + 1) * HD])
        dq_s[rows, cols] = (jnp.concatenate(dqt, axis=0) * SCALE).T.astype(BF)
        for j in range(full // TK):
            tile = slice(j * TK, (j + 1) * TK)
            dk_s[tile, cols] += nn(ds_s[0, tile], qs[0]) + nn(ds_s[1, tile], qs[1])

    @pl.when(t == last)
    def _():
        if rem:
            lane = lax.broadcasted_iota(jnp.int32, (1, 256), 1)
            def spread(x):
                return jnp.concatenate([jnp.where(lane // HD == h, x, 0.0).astype(x.dtype) for h in range(4)], axis=0)
            for u in range(np_ // 2):
                cols = slice(u * 256, (u + 1) * 256)
                qd = spread(q_s[nb * BQ:, cols])
                dd = spread(do_s[nb * BQ:, cols])
                delta = jnp.sum(spread(pr_s[nb * BQ:, cols]).T, axis=0, keepdims=True)
                dp = nt(v_s[:, cols], dd)
                ds = (erem[u].astype(F32) * (dp - delta)).astype(BF)
                dv_s[:, cols] += nn(erem[u], dd)
                dk_s[:, cols] += nn(ds, qd)
                x = nn(kt_s[cols], ds).T * SCALE
                dq = x[:rem]
                for h in range(1, 4):
                    dq = jnp.where(lane // HD == h, x[h * rem:(h + 1) * rem], dq)
                dq_s[nb * BQ:, cols] = dq.astype(BF)
        for lo, dst in ((0, out_o), (half, out_r)):
            rows = slice(lo, lo + half)
            dst[:, :inner] = dq_s[rows]
            dst[:, inner:2 * inner] = (dk_s[rows] * SCALE).astype(BF)
            dst[:, 2 * inner:] = dv_s[rows].astype(BF)

def attend_back(slot, own, rec, do_o, do_r, o_o, o_r, r_o, r_r, e, erem):
    half, w = own.shape
    inner = w // 3
    np_ = inner // 128
    full = 2 * half
    nb = full // BQ
    rem = full - nb * BQ
    last = np_ * nb
    whole = lambda shape, **kw: pl.BlockSpec(shape, lambda t: (0,) * len(shape), **kw)
    one = dict(pipeline_mode=pl.Buffered(1))
    return pl.pallas_call(
        functools.partial(attend_back_kernel, nb=nb, np_=np_, rem=rem),
        grid=(last + 1,),
        in_specs=[whole((half, w), **one)] * 2
        + [whole((half, inner), **one), pl.BlockSpec((None, half, inner), lambda t: (slot, 0, 0), **one)]
        + [whole((half, inner), **one)] * 4
        + [pl.BlockSpec((1, 2, full, BQ), lambda t: (jnp.minimum(t, last - 1), 0, 0, 0)), whole(erem.shape, **one)],
        out_specs=[whole((half, w), **one)] * 2,
        out_shape=[jax.ShapeDtypeStruct((half, w), BF)] * 2,
        scratch_shapes=[
            pltpu.VMEM((full, inner), BF), pltpu.VMEM((full, inner), BF), pltpu.VMEM((full, inner), BF),
            pltpu.VMEM((inner, full), BF), pltpu.VMEM((full, inner), BF), pltpu.VMEM((full, inner), F32),
            pltpu.VMEM((2, full, BQ), BF), pltpu.VMEM((full, inner), BF),
            pltpu.VMEM((full, inner), F32), pltpu.VMEM((full, inner), F32)],
        cost_estimate=pl.CostEstimate(flops=COST, bytes_accessed=0, transcendentals=0),
        compiler_params=pltpu.CompilerParams(vmem_limit_bytes=62 * 1024 * 1024),
    )(own, rec, do_o, do_r, o_o, o_r, r_o, r_r, e, erem)


def matmul(left, right):
    return jnp.dot(left, right, preferred_element_type=jnp.float32)


def layer_norm(values, gain, shift):
    centred = values - jnp.mean(values, -1, keepdims=True)
    spread = jnp.mean(centred * centred, -1, keepdims=True)
    inverse = lax.rsqrt(spread + EPSILON)
    scaled = centred * inverse
    return (scaled, inverse, scaled * gain + shift)


def norm_back(scaled, inverse, gain, incoming):
    weighted = incoming * gain
    first = jnp.mean(weighted, -1, keepdims=True)
    second = jnp.mean(weighted * scaled, -1, keepdims=True)
    return inverse * (weighted - first - scaled * second)


def fetch_weights(shards):
    return (
        lax.all_gather(shards[0], "grp", axis=0, tiled=True),
        lax.all_gather(shards[1], "grp", axis=0, tiled=True),
        lax.all_gather(shards[2], "grp", axis=0, tiled=True),
        lax.all_gather(shards[3], "grp", axis=0, tiled=True),
        lax.all_gather(shards[4], "grp", axis=1, tiled=True),
        lax.all_gather(shards[5], "grp", axis=1, tiled=True),
        lax.all_gather(shards[6], "grp", axis=0, tiled=True),
    )


def shard_grads(weight_grads):
    return (
        lax.psum_scatter(weight_grads[0], "grp", scatter_dimension=1, tiled=True),
        lax.psum_scatter(weight_grads[1], "grp", scatter_dimension=1, tiled=True),
        lax.psum_scatter(weight_grads[2], "grp", scatter_dimension=0, tiled=True),
        lax.psum_scatter(weight_grads[3], "grp", scatter_dimension=0, tiled=True),
        lax.psum_scatter(weight_grads[4], "grp", scatter_dimension=0, tiled=True),
        lax.psum_scatter(weight_grads[5], "grp", scatter_dimension=0, tiled=True),
        lax.psum_scatter(weight_grads[6], "grp", scatter_dimension=0, tiled=True),
    )


def raw_scores(query, keys):
    rows = query.shape[0]
    length = keys.shape[0]
    return jnp.einsum(
        "qhd,khd->hqk",
        query.reshape(rows, H, HD),
        keys.reshape(length, H, HD),
        preferred_element_type=jnp.float32,
    ) * HD ** (-0.5)


def score_probs(query, keys):
    return jax.nn.softmax(raw_scores(query, keys), axis=-1)


def forward_pass(row_block, gathered):
    qkv_weight, out_weight, up_weight, down_weight, gains, biases, hidden_bias = gathered
    gain_f = gains.astype(jnp.float32)
    bias_f = biases.astype(jnp.float32)
    rows = row_block.shape[0]
    model_width = row_block.shape[1]
    inputs = row_block.astype(jnp.float32)
    scaled1, inverse1, normed = layer_norm(inputs, gain_f[0], bias_f[0])
    normed = normed.astype(jnp.bfloat16)
    shift = jnp.concatenate([bias_f[1], jnp.zeros_like(bias_f[1]), bias_f[2]])
    qkv = (matmul(normed, qkv_weight) + shift).astype(jnp.bfloat16)
    query = qkv[:, :model_width]
    key_part = qkv[:, model_width : 2 * model_width]
    value_part = qkv[:, 2 * model_width :]
    keys, values = (
        lax.all_gather(key_part, "grp", axis=0, tiled=True),
        lax.all_gather(value_part, "grp", axis=0, tiled=True),
    )
    length = keys.shape[0]
    probs = score_probs(query, keys)
    context = (
        jnp.einsum(
            "hqk,khd->qhd",
            probs.astype(jnp.bfloat16),
            values.reshape(length, H, HD),
            preferred_element_type=jnp.float32,
        )
        .reshape(rows, model_width)
        .astype(jnp.bfloat16)
    )
    hidden = inputs + matmul(context, out_weight) + bias_f[3]
    scaled2, inverse2, normed2 = layer_norm(hidden, gain_f[1], bias_f[4])
    normed2 = normed2.astype(jnp.bfloat16)
    pre = matmul(normed2, up_weight) + hidden_bias.astype(jnp.float32)
    active = jax.nn.gelu(pre, approximate=False).astype(jnp.bfloat16)
    result = hidden + matmul(active, down_weight) + bias_f[5]
    saved = (
        scaled1,
        inverse1,
        normed,
        query,
        keys,
        values,
        context,
        scaled2,
        inverse2,
        normed2,
        pre,
        active,
    )
    return (result, saved)


def backward_pass(incoming, weight, saved, gathered):
    qkv_weight, out_weight, up_weight, down_weight, gains, biases, hidden_bias = gathered
    gain_f = gains.astype(jnp.float32)
    (
        scaled1,
        inverse1,
        normed,
        query,
        keys,
        values,
        context,
        scaled2,
        inverse2,
        normed2,
        pre,
        active,
    ) = saved
    rows = query.shape[0]
    model_width = query.shape[1]
    length = keys.shape[0]
    d_out = incoming * weight.astype(jnp.bfloat16)
    d_out_f = d_out.astype(jnp.float32)
    grad_down = jnp.einsum("rf,rd->fd", active, d_out, preferred_element_type=jnp.float32)
    grad_b2 = jnp.sum(d_out_f, 0)
    d_act = jnp.einsum("rd,fd->rf", d_out, down_weight, preferred_element_type=jnp.float32)
    unused, gelu_pull = jax.vjp(lambda inputs: jax.nn.gelu(inputs, approximate=False), pre)
    d_pre = gelu_pull(d_act)[0].astype(jnp.bfloat16)
    grad_up = jnp.einsum("rd,rf->df", normed2, d_pre, preferred_element_type=jnp.float32)
    grad_hidden_bias = jnp.sum(d_pre.astype(jnp.float32), 0)
    d_norm2 = jnp.einsum("rf,df->rd", d_pre, up_weight, preferred_element_type=jnp.float32)
    d_hidden = d_out_f + norm_back(scaled2, inverse2, gain_f[1], d_norm2)
    grad_g2 = jnp.sum(d_norm2 * scaled2, 0)
    grad_beta2 = jnp.sum(d_norm2, 0)
    d_branch = d_hidden.astype(jnp.bfloat16)
    grad_out = jnp.einsum("rd,re->de", context, d_branch, preferred_element_type=jnp.float32)
    grad_bo = jnp.sum(d_branch.astype(jnp.float32), 0)
    d_context = jnp.einsum(
        "re,de->rd", d_branch, out_weight, preferred_element_type=jnp.float32
    ).astype(jnp.bfloat16)
    scores = raw_scores(query, keys)
    probs = jax.nn.softmax(scores, axis=-1)
    context_heads = d_context.reshape(rows, H, HD)
    d_probs = jnp.einsum(
        "qhd,khd->hqk",
        context_heads,
        values.reshape(length, H, HD),
        preferred_element_type=jnp.float32,
    )
    delta = jnp.sum(probs * d_probs, -1)
    d_scores = (probs * (d_probs - delta[..., None])).astype(jnp.bfloat16)
    d_query = (
        jnp.einsum(
            "hqk,khd->qhd",
            d_scores,
            keys.reshape(length, H, HD),
            preferred_element_type=jnp.float32,
        )
        * HD ** (-0.5)
    ).reshape(rows, model_width)
    d_value = jnp.einsum(
        "hqk,qhd->khd",
        probs.astype(jnp.bfloat16),
        context_heads,
        preferred_element_type=jnp.float32,
    ).reshape(length, model_width)
    d_key = (
        jnp.einsum(
            "hqk,qhd->khd", d_scores, query.reshape(rows, H, HD), preferred_element_type=jnp.float32
        )
        * HD ** (-0.5)
    ).reshape(length, model_width)
    d_key, d_value = (
        lax.psum_scatter(d_key, "grp", scatter_dimension=0, tiled=True),
        lax.psum_scatter(d_value, "grp", scatter_dimension=0, tiled=True),
    )
    d_qkv = jnp.concatenate(
        [d_query.astype(jnp.bfloat16), d_key.astype(jnp.bfloat16), d_value.astype(jnp.bfloat16)], 1
    )
    grad_qkv = jnp.einsum("rd,re->de", normed, d_qkv, preferred_element_type=jnp.float32)
    d_qkv_f = d_qkv.astype(jnp.float32)
    grad_bq = jnp.sum(d_qkv_f[:, :model_width], 0)
    grad_bv = jnp.sum(d_qkv_f[:, 2 * model_width :], 0)
    d_norm1 = jnp.einsum("re,de->rd", d_qkv, qkv_weight, preferred_element_type=jnp.float32)
    row_grad = d_hidden + norm_back(scaled1, inverse1, gain_f[0], d_norm1)
    grad_g1 = jnp.sum(d_norm1 * scaled1, 0)
    grad_beta1 = jnp.sum(d_norm1, 0)
    grad_gains = jnp.stack([grad_g1, grad_g2])
    grad_biases = jnp.stack([grad_beta1, grad_bq, grad_bv, grad_bo, grad_beta2, grad_b2])
    weight_grads = (
        grad_gains,
        grad_biases,
        grad_hidden_bias,
        grad_qkv,
        grad_out,
        grad_up,
        grad_down,
    )
    return (row_grad, weight_grads)


def plain_body(clips, clip_count, cotangent, norm_gain, bias_d, bias_ff, w_qkv, w_o, w_up, w_down):
    shards = (w_qkv, w_o, w_up, w_down, norm_gain, bias_d, bias_ff)
    number = clips.shape[0]
    outputs = []
    records = []
    actives = []
    for slot_index in range(number):
        gathered = fetch_weights(shards)
        active = (clip_count[0] > slot_index).astype(jnp.float32)
        result, saved = forward_pass(clips[slot_index], gathered)
        outputs.append((result * active).astype(jnp.bfloat16))
        records.append(saved)
        actives.append(active)
    row_grads = [None] * number
    totals = None
    for slot_index in reversed(range(number)):
        gathered = fetch_weights(shards)
        row_grad, weight_grads = backward_pass(
            cotangent[slot_index], actives[slot_index], records[slot_index], gathered
        )
        row_grads[slot_index] = row_grad
        totals = (
            weight_grads
            if totals is None
            else jax.tree.map(lambda left, right: left + right, totals, weight_grads)
        )
    totals = shard_grads(totals)
    small_sums = lax.psum((totals[0], totals[1], totals[2]), "rep")
    matrix_sums = (
        lax.psum_scatter(totals[3], "rep", scatter_dimension=1, tiled=True),
        lax.psum_scatter(totals[4], "rep", scatter_dimension=1, tiled=True),
        lax.psum_scatter(totals[5], "rep", scatter_dimension=1, tiled=True),
        lax.psum_scatter(totals[6], "rep", scatter_dimension=1, tiled=True),
    )
    return (jnp.stack(outputs), jnp.stack(row_grads)) + tuple(small_sums) + tuple(matrix_sums)


def row_stats(values):
    centred = values - jnp.mean(values, -1, keepdims=True)
    inverse = lax.rsqrt(jnp.mean(centred * centred, -1, keepdims=True) + EPSILON)
    return centred * inverse, inverse


def whole(shape, **kw):
    return pl.BlockSpec(shape, lambda *_: (0,) * len(shape), **kw)


def call(kernel, ids, grid, in_specs, out_specs, out_shape, args, scratch=(), flops=0, limit=60, aliases=()):
    return pl.pallas_call(
        kernel,
        grid_spec=pltpu.PrefetchScalarGridSpec(
            num_scalar_prefetch=1, grid=grid, in_specs=in_specs, out_specs=out_specs, scratch_shapes=list(scratch)
        ),
        out_shape=out_shape,
        cost_estimate=pl.CostEstimate(flops=int(flops), bytes_accessed=0, transcendentals=0),
        input_output_aliases=dict(aliases),
        compiler_params=pltpu.CompilerParams(vmem_limit_bytes=limit * 1024 * 1024),
    )(ids, *args)


def slot_of(shape, s):
    return pl.BlockSpec((None,) + shape, lambda *_: (s,) + (0,) * len(shape))


def piece_places(ids):
    y, core = ids[4], ids[0]
    return (2 * y + core, 2 * (1 - y) + core, 2 * y + 1 - core, 2 * (1 - y) + 1 - core)


def lay_pieces(ids, target, pieces):
    size = target.shape[0] // len(pieces)
    for piece, place in zip(pieces, piece_places(ids)):
        target[pl.ds(pl.multiple_of(place * size, size), size)] = piece[...]


def by_rows(ids, x, near, far):
    size = near.shape[0]
    own = pl.ds(pl.multiple_of(ids[3] * size, size), size)
    across = pl.ds(pl.multiple_of((1 - ids[3]) * size, size), size)
    return nn(x[:, own], near[...]) + nn(x[:, across], far[...])


def project_other_kernel(ids, mine, got, gain, shift, near, p0, p1, p2, p3, bias, block, normed, out, far_s):
    @pl.when(pl.program_id(0) == 0)
    def _():
        x = jnp.where(ids[1] == 1, got[...], mine[...])
        block[...] = x
        hat, unused = row_stats(x.astype(F32))
        normed[...] = (hat * gain[...] + shift[...]).astype(BF)

    lay_pieces(ids, far_s, (p0, p1, p2, p3))
    out[...] = (by_rows(ids, normed, near, far_s) + bias[...]).astype(BF)


def project_other(ids, mine, mine_slot, got, got_slot, gain, shift, near, far, bias):
    rows, width = mine.shape[1:]
    inner = width // 2
    columns = lambda i, ids: (0, 2 * i + 1 - ids[0])
    return call(
        project_other_kernel,
        ids,
        (3,),
        [
            slot_of((rows, width), mine_slot),
            slot_of((rows, width), got_slot),
            whole((1, width)),
            whole((1, width)),
            pl.BlockSpec((inner, inner), columns),
        ]
        + [pl.BlockSpec((inner // 4, inner), columns)] * 4
        + [pl.BlockSpec((1, inner), columns)],
        [whole((rows, width)), whole((rows, width)), pl.BlockSpec((rows, inner), lambda i, ids: (0, i))],
        [
            jax.ShapeDtypeStruct((rows, width), BF),
            jax.ShapeDtypeStruct((rows, width), BF),
            jax.ShapeDtypeStruct((rows, 3 * inner), BF),
        ],
        (mine, got, gain, shift, near, *far, bias),
        scratch=[pltpu.VMEM((inner, inner), BF)],
    )


def project_mine_kernel(ids, normed, near, p0, p1, p2, p3, bias, out, far_s):
    lay_pieces(ids, far_s, (p0, p1, p2, p3))
    out[...] = (by_rows(ids, normed, near, far_s) + bias[...]).astype(BF)


def project_mine(ids, normed, near, far, bias):
    rows, width = normed.shape
    inner = width // 2
    columns = lambda i, ids: (0, 2 * i + ids[0])
    return call(
        project_mine_kernel,
        ids,
        (3,),
        [whole((rows, width)), pl.BlockSpec((inner, inner), columns)]
        + [pl.BlockSpec((inner // 4, inner), columns)] * 4
        + [pl.BlockSpec((1, inner), columns)],
        pl.BlockSpec((rows, inner), lambda i, ids: (0, i)),
        jax.ShapeDtypeStruct((rows, 3 * inner), BF),
        (normed, near, *far, bias),
        scratch=[pltpu.VMEM((inner, inner), BF)],
    )


def feed_kernel(
    ids, block, ctx_mine, ctx_other, cot_mine, cot_got, out_near, o0, o1, o2, o3, up_near, u0, u1, u2, u3,
    down_near, d0, d1, d2, d3, gain, biases, bias_hidden, *rest,
):
    (
        active, d_pre, normed2, d_out, result, d_branch, d_ctx_mine, d_ctx_other, sums, sum_hidden,
        hidden_s, total_s, d_norm_s, up_far, w_down,
    ) = rest[-15:]
    j = pl.program_id(0)
    half = pl.num_programs(0) // 2
    inner = ctx_mine.shape[1]
    live = ids[2].astype(F32)
    own = pl.ds(pl.multiple_of(ids[3] * inner, inner), inner)
    across = pl.ds(pl.multiple_of((1 - ids[3]) * inner, inner), inner)
    lay_pieces(ids, up_far, (u0, u1, u2, u3))

    out_far = w_down.at[:inner]

    straight = ids[0] == ids[3]

    @pl.when(j == 0)
    def _():
        lay_pieces(ids, out_far, (o0, o1, o2, o3))
        w_mine = jnp.where(straight, out_near[...], out_far[...])
        w_other = jnp.where(straight, out_far[...], out_near[...])
        hidden = block[...].astype(F32) + (nn(ctx_mine[...], w_mine) + nn(ctx_other[...], w_other))
        hidden = hidden + biases[3:4]
        hidden_s[...] = hidden
        hat, unused = row_stats(hidden)
        normed2[...] = (hat * gain[1:2] + biases[4:5]).astype(BF)
        d = (jnp.where(ids[1] == 1, cot_got[...], cot_mine[...]).astype(F32) * live).astype(BF)
        d_out[...] = d

    @pl.when(j < half)
    def _():
        w_down[...] = down_near[...]

    @pl.when(j >= half)
    def _():
        here = ids[4] == j - half
        size = d0.shape[0]
        w_down[pl.ds(pl.multiple_of(ids[0] * size, size), size)] = jnp.where(here, d0[...], d1[...])
        w_down[pl.ds(pl.multiple_of((1 - ids[0]) * size, size), size)] = jnp.where(here, d2[...], d3[...])

    rows = block.shape[0]
    parts = (slice(0, rows // 32 * 16), slice(rows // 32 * 16, rows))

    def begin(part):
        pre = nn(normed2[part, own], up_near[...]) + nn(normed2[part, across], up_far[...])
        return pre, nt(d_out[part], w_down[...])

    def middle(part, pre, d_act):
        pre = pre + bias_hidden[...]
        phi = 0.5 + 0.5 * lax.erf(pre * 0.7071067811865476)
        act = (pre * phi).astype(BF)
        active[part] = act
        slope = phi + pre * (jnp.exp2(pre * pre * (-0.5 * LOG2E)) * 0.3989422804014327)
        dp = d_act * slope
        total = jnp.sum(dp, 0, keepdims=True)
        dp = dp.astype(BF)
        d_pre[part] = dp
        return act, dp, total

    def end(part, act, dp):
        total_s[part] += nn(act, w_down[...])
        d_norm_s[part, own] += nt(dp, up_near[...])
        d_norm_s[part, across] += nt(dp, up_far[...])

    @pl.when(j == 0)
    def _():
        total_s[...] = jnp.zeros_like(total_s)
        d_norm_s[...] = jnp.zeros_like(d_norm_s)

    first, second = parts
    begun = begin(first)
    begun_second = begin(second)
    act, dp, total = middle(first, *begun)
    end(first, act, dp)
    act, dp, total_second = middle(second, *begun_second)
    end(second, act, dp)
    sum_hidden[...] = jnp.broadcast_to(total + total_second, sum_hidden.shape)

    @pl.when(j == pl.num_programs(0) - 1)
    def _():
        hidden = hidden_s[...]
        result[...] = ((hidden + total_s[...] + biases[5:6]) * live).astype(BF)
        hat, inverse = row_stats(hidden)
        d_norm = d_norm_s[...]
        weighted = d_norm * gain[1:2]
        first = jnp.mean(weighted, -1, keepdims=True)
        second = jnp.mean(weighted * hat, -1, keepdims=True)
        d = d_out[...].astype(F32)
        branch = (d + inverse * (weighted - first - hat * second)).astype(BF)
        d_branch[...] = branch
        sums[...] = jnp.concatenate(
            [
                jnp.sum(d_norm * hat, 0, keepdims=True),
                jnp.sum(d_norm, 0, keepdims=True),
                jnp.sum(branch.astype(F32), 0, keepdims=True),
                jnp.sum(d, 0, keepdims=True),
                jnp.zeros((4, d.shape[1]), F32),
            ],
            0,
        )
        lay_pieces(ids, out_far, (o0, o1, o2, o3))
        w_mine = jnp.where(straight, out_near[...], out_far[...])
        w_other = jnp.where(straight, out_far[...], out_near[...])
        d_ctx_mine[...] = nt(branch, w_mine).astype(BF)
        d_ctx_other[...] = nt(branch, w_other).astype(BF)


def feed(ids, slot, slots, block, ctx_mine, ctx_other, cot_mine, cot_got, got_slot, w_out, w_up, w_down, far, far_down, gain, biases, bias_hidden, before):
    rows, width = block.shape
    inner = width // 2
    ff = w_up.shape[1]
    chunk = width
    steps = ff // chunk
    one = dict(pipeline_mode=pl.Buffered(1))
    full = whole((rows, width), **one)
    part = whole((rows, inner), **one)
    place = lambda j, ids: (0, (ids[3] * (steps // 2) + j) % steps)
    columns = pl.BlockSpec((rows, chunk), place)
    one_slot = lambda shape, at=slot: pl.BlockSpec((None,) + shape, lambda *_: (at, 0, 0), **one)
    wide = jax.ShapeDtypeStruct((rows, width), BF)
    args = (
        block, ctx_mine, ctx_other, cot_mine, cot_got, w_out, *far, w_up, *far, w_down, *far_down, gain, biases, bias_hidden,
    )
    return call(
        feed_kernel,
        ids,
        (steps,),
        [full, part, part, one_slot((rows, width)), one_slot((rows, width), got_slot), whole((inner, width), **one)]
        + [pl.BlockSpec((inner // 4, width), lambda j, ids: (steps, 0), **one)] * 4
        + [pl.BlockSpec((inner, chunk), place)]
        + [pl.BlockSpec((inner // 4, chunk), lambda j, ids: (place(j, ids)[1], 0))] * 4
        + [pl.BlockSpec((chunk, width), lambda j, ids: (jnp.minimum(j, steps // 2 - 1), 0), **one)]
        + [whole((ff // 8, width), **one)] * 4
        + [whole(gain.shape), whole(biases.shape), pl.BlockSpec((1, chunk), place)]
        + [pl.BlockSpec(memory_space=pl.ANY)] * len(before),
        [
            columns, columns, full, full, full, full, part, one_slot((rows, inner)),
            whole((8, width)),
            pl.BlockSpec((8, chunk), place),
        ],
        [
            jax.ShapeDtypeStruct((rows, ff), BF), jax.ShapeDtypeStruct((rows, ff), BF),
            wide, wide, wide, wide,
            jax.ShapeDtypeStruct((rows, inner), BF), jax.ShapeDtypeStruct((slots, rows, inner), BF),
            jax.ShapeDtypeStruct((8, width), F32), jax.ShapeDtypeStruct((8, ff), F32),
        ],
        args + tuple(before),
        scratch=[pltpu.VMEM((rows, width), F32)] * 3
        + [pltpu.VMEM((inner, chunk), BF), pltpu.VMEM((chunk, width), BF)],
        flops=COST,
        limit=62,
        aliases=[(1 + len(args), 7)] if before else (),
    )


def outer_sum(left, right):
    return tn(jnp.concatenate(left), jnp.concatenate(right))


def put_block(ids, outs, rec, piece, x, y, z, rows):
    place = 2 * (x != ids[3]).astype(jnp.int32) + (y != ids[4]).astype(jnp.int32)
    if rec is None:
        outs[0][place, z, rows] = piece.astype(BF)
        return
    for i, out in enumerate(outs):

        @pl.when(place == i)
        def _(i=i, out=out):
            out[z, rows] = (piece + rec[i, z, rows].astype(F32)).astype(BF)


def split_refs(refs, counts):
    parts, at = [], 0
    for count in counts:
        parts.append(refs[at : at + count])
        at += count
    rest = refs[at:]
    return parts + ([None, rest] if len(rest) == 1 else [rest[0], rest[-4:]])


def grad_down_kernel(ids, *refs, slots):
    left, right, rec, outs = split_refs(refs, (slots, slots))
    step = pl.program_id(0)
    x = jnp.where(step == 0, 1 - ids[3], ids[3])
    total = outer_sum([a[...] for a in left], [b[...] for b in right])
    chips, rows, cols = outs[0].shape[-3:]
    parts = total.shape[1] // cols
    rows = rows // parts
    for z in range(chips):
        for y in range(2):
            at = (2 * z + y) * rows
            for part in range(parts):
                piece = total[at : at + rows, part * cols : (part + 1) * cols]
                put_block(ids, outs, rec, piece, x, jnp.int32(y), z, slice(part * rows, (part + 1) * rows))


def grad_up_kernel(ids, *refs, slots):
    left, first, last, rec, outs = split_refs(refs, (slots, slots, slots))
    z = pl.program_id(0)
    right = [jnp.concatenate([a[...], b[...]], 1) for a, b in zip(first, last)]
    total = outer_sum([a[...] for a in left], right)
    rows, cols = outs[0].shape[-2:]
    for x in range(2):
        for y in range(2):
            piece = total[y * rows : (y + 1) * rows, x * cols : (x + 1) * cols]
            put_block(ids, outs, rec, piece, jnp.int32(x), jnp.int32(y), z, slice(0, rows))


def grad_out_kernel(ids, *refs, slots):
    left, mine, other, rec, outs = split_refs(refs, (slots, slots, slots))
    right = [jnp.concatenate([a[...], b[...]], 1) for a, b in zip(mine, other)]
    total = outer_sum([a[...] for a in left], right)
    chips, rows, cols = outs[0].shape[-3:]
    for near in range(2):
        x = ids[0] if near == 0 else 1 - ids[0]
        for z in range(chips):
            for y in range(2):
                at = (2 * z + y) * rows
                piece = total[at : at + rows, near * cols : (near + 1) * cols]
                put_block(ids, outs, rec, piece, x, jnp.int32(y), z, slice(0, rows))


def grad_qkv_kernel(ids, *refs, slots, steps):
    mine, other, first, last, rec, outs = split_refs(refs, (slots, slots, slots, slots))
    right = [jnp.concatenate([a[...], b[...]], 1) for a, b in zip(first, last)]
    near = outer_sum([a[...] for a in mine], right)
    far = outer_sum([a[...] for a in other], right)
    total = jnp.concatenate([jnp.where(ids[0] == 0, near, far), jnp.where(ids[0] == 0, far, near)])
    chips, rows, cols = outs[0].shape[-3:]
    span = total.shape[0]
    for step in range(steps):

        @pl.when(pl.program_id(0) == step)
        def _(step=step):
            for block in range(2 * chips):
                begin = max(block * rows, step * span)
                end = min((block + 1) * rows, (step + 1) * span)
                if begin >= end:
                    continue
                for x in range(2):
                    piece = total[begin - step * span : end - step * span, x * cols : (x + 1) * cols]
                    put_block(
                        ids, outs, rec, piece, jnp.int32(x), jnp.int32(block % 2), block // 2,
                        slice(begin - block * rows, end - block * rows),
                    )


def grad_call(kernel, ids, grid, groups, shape, rec, flops, joint=None, **kw):
    specs, args = [], []
    for arrays, block, index in groups:
        specs += [pl.BlockSpec(block, index)] * len(arrays)
        args += arrays
    if rec is None:
        out_specs, out_shapes, aliases = whole(shape, pipeline_mode=pl.Buffered(1)), jax.ShapeDtypeStruct(shape, BF), ()
    else:
        specs.append(whole(shape, pipeline_mode=pl.Buffered(1)))
        args.append(rec)
        all_rows, at, arrays = joint
        out_specs = [pl.BlockSpec(shape[1:], lambda *_: (0, at, 0), pipeline_mode=pl.Buffered(1))] * 4
        out_shapes = [jax.ShapeDtypeStruct((shape[1], all_rows, shape[3]), BF)] * 4
        aliases = [(1 + len(args) + i, i) for i in range(len(arrays))]
        specs += [pl.BlockSpec(memory_space=pl.ANY)] * len(arrays)
        args += arrays
    return call(
        functools.partial(kernel, slots=len(groups[0][0]), **kw),
        ids, grid, specs, out_specs, out_shapes, tuple(args), flops=flops, aliases=aliases,
    )


def column_half(ids, rec):
    return 1 - ids[0] if rec is None else ids[0]


def grad_down_part(ids, chips, d_out, active, rec, joint=None):
    rows, width = d_out[0].shape
    ff = active[0].shape[1]
    cols = ff // 4
    parts = 4 * cols // width
    block = lambda i, ids: (0, 2 * jnp.where(i == 0, 1 - ids[3], ids[3]) + column_half(ids, rec))
    groups = [(d_out, (rows, width), lambda i, ids: (0, 0)), (active, (rows, cols), block)]
    shape = (4, chips, parts * width // (2 * chips), cols // parts)
    return grad_call(grad_down_kernel, ids, (2,), groups, shape, rec, COST // 2, joint)


def grad_up_part(ids, chips, d_pre, normed, rec, joint=None):
    rows, width = normed[0].shape
    ff = d_pre[0].shape[1]
    cols = width // 4
    groups = [
        (d_pre, (rows, ff // chips), lambda i, ids: (0, i)),
        (normed, (rows, cols), lambda i, ids: (0, column_half(ids, rec))),
        (normed, (rows, cols), lambda i, ids: (0, 2 + column_half(ids, rec))),
    ]
    return grad_call(grad_up_kernel, ids, (chips,), groups, (4, chips, ff // (2 * chips), cols), rec, COST // 2, joint)


def grad_out_part(ids, chips, d_branch, mine, other, rec, joint=None):
    rows, width = d_branch[0].shape
    cols = width // 4
    half = lambda i, ids: (0, column_half(ids, rec))
    groups = [(d_branch, (rows, width), lambda i, ids: (0, 0)), (mine, (rows, cols), half), (other, (rows, cols), half)]
    return grad_call(grad_out_kernel, ids, (1,), groups, (4, chips, width // (2 * chips), cols), rec, COST // 2, joint)


def grad_qkv_part(ids, chips, mine, other, normed, rec, joint=None):
    rows, width = normed[0].shape
    cols = width // 4
    columns = lambda i, ids: (0, i)
    groups = [
        (mine, (rows, width // 2), columns),
        (other, (rows, width // 2), columns),
        (normed, (rows, cols), lambda i, ids: (0, column_half(ids, rec))),
        (normed, (rows, cols), lambda i, ids: (0, 2 + column_half(ids, rec))),
    ]
    return grad_call(
        grad_qkv_kernel, ids, (3,), groups, (4, chips, 3 * width // (2 * chips), cols), rec, COST // 2, joint, steps=3
    )


def add_kernel(ids, *refs):
    refs[-1][...] = sum(term[...].astype(F32) for term in refs[:-1]).astype(BF)


def add_chips(ids, terms, chips, rows):
    cols = terms[0].shape[1]
    return call(
        add_kernel,
        ids,
        (chips,),
        [pl.BlockSpec((rows, cols), lambda i, ids: (ids[5] ^ i, 0))] * len(terms),
        pl.BlockSpec((None, rows, cols), lambda i, ids: (i, 0, 0)),
        jax.ShapeDtypeStruct((chips, rows, cols), BF),
        tuple(terms),
    )


def finish_kernel(
    ids, d_mine, d_other, mine_near, m0, m1, m2, m3, other_near, o0, o1, o2, o3, block, d_hidden, gain,
    row_grad, sums, sum_mine, sum_other, total_s, mine_far, other_far,
):
    i = pl.program_id(0)
    size = mine_near.shape[0]
    lay_pieces(ids, mine_far, (m0, m1, m2, m3))
    lay_pieces(ids, other_far, (o0, o1, o2, o3))
    own = pl.ds(pl.multiple_of(ids[3] * size, size), size)
    across = pl.ds(pl.multiple_of((1 - ids[3]) * size, size), size)
    term = nt(d_mine[...], mine_near[...]) + nt(d_other[...], other_near[...])
    term_far = nt(d_mine[...], mine_far[...]) + nt(d_other[...], other_far[...])
    sum_mine[...] = jnp.broadcast_to(jnp.sum(d_mine[...].astype(F32), 0, keepdims=True), sum_mine.shape)
    sum_other[...] = jnp.broadcast_to(jnp.sum(d_other[...].astype(F32), 0, keepdims=True), sum_other.shape)

    @pl.when(i == 0)
    def _():
        total_s[:, own] = term
        total_s[:, across] = term_far

    @pl.when(i > 0)
    def _():
        total_s[:, own] += term
        total_s[:, across] += term_far

    @pl.when(i == pl.num_programs(0) - 1)
    def _():
        hat, inverse = row_stats(block[...].astype(F32))
        d_norm = total_s[...]
        weighted = d_norm * gain[0:1]
        first = jnp.mean(weighted, -1, keepdims=True)
        second = jnp.mean(weighted * hat, -1, keepdims=True)
        row_grad[...] = (d_hidden[...].astype(F32) + inverse * (weighted - first - hat * second)).astype(BF)
        sums[...] = jnp.concatenate(
            [jnp.sum(d_norm * hat, 0, keepdims=True), jnp.sum(d_norm, 0, keepdims=True), jnp.zeros((6, d_norm.shape[1]), F32)], 0
        )


def finish(ids, d_mine, d_other, near, far, block, d_hidden, gain):
    rows, width = block.shape
    inner = width // 2
    full = whole((rows, width))
    part = pl.BlockSpec((rows, inner), lambda i, ids: (0, i))
    row = pl.BlockSpec((8, inner), lambda i, ids: (0, i))
    mine = lambda i, ids: (0, 2 * i + ids[0])
    other = lambda i, ids: (0, 2 * i + 1 - ids[0])
    return call(
        finish_kernel,
        ids,
        (3,),
        [
            part, part,
            pl.BlockSpec((inner, inner), mine), *[pl.BlockSpec((inner // 4, inner), mine)] * 4,
            pl.BlockSpec((inner, inner), other), *[pl.BlockSpec((inner // 4, inner), other)] * 4,
            full, full, whole(gain.shape),
        ],
        [full, whole((8, width)), row, row],
        [
            jax.ShapeDtypeStruct((rows, width), BF), jax.ShapeDtypeStruct((8, width), F32),
            jax.ShapeDtypeStruct((8, 3 * inner), F32), jax.ShapeDtypeStruct((8, 3 * inner), F32),
        ],
        (d_mine, d_other, near, *far, near, *far, block, d_hidden, gain),
        scratch=[pltpu.VMEM((rows, width), F32)] + [pltpu.VMEM((inner, inner), BF)] * 2,
        flops=COST,
    )


def swap_axis(x, axis, step=1):
    size = lax.axis_size(axis)
    return lax.ppermute(x, axis, [(i, i ^ step) for i in range(size)])


def swap_across(x):
    return lax.ppermute(x, ("mid", "grp"), [(0, 3), (1, 2), (2, 1), (3, 0)])


def swap_owner(x, chips):
    pairs = []
    for k in range(2 * chips):
        pairs += [(4 * k + 1, 4 * k + 2), (4 * k + 2, 4 * k + 1)]
    return lax.ppermute(x, AXES, pairs)


def after(values, first):
    return lax.optimization_barrier((values, first))[0]


def in_order(index, mine, other, axis=0):
    return jnp.concatenate([jnp.where(index == 0, mine, other), jnp.where(index == 0, other, mine)], axis)


def own_half(x, index, axis=0):
    size = x.shape[axis] // 2
    return lax.dynamic_slice_in_dim(x, index * size, size, axis)


def send_piece(piece):
    return swap_axis(piece, "grp")


def own_piece(shard):
    place = 2 * lax.axis_index("mid") + lax.axis_index("core")
    part = shard.shape[0] // 4
    return lax.dynamic_slice_in_dim(shard, place * part, part, 0)


def as_lines(x, cols):
    parts = []
    for _ in range(2):
        part = lax.reduce_precision(x, 8, 7)
        parts.append(part.astype(BF))
        x = x - part
    return jnp.concatenate(parts).reshape(-1, cols)


def from_lines(lines, shape):
    return lines.astype(F32).reshape((2,) + shape).sum(0)


def send_sums(part):
    return [part[0], swap_axis(part[1], "mid"), swap_axis(part[2], "grp"), swap_across(part[3])]


def send_chips(part):
    return [part[0]] + [swap_axis(part[i], "z", i) for i in range(1, lax.axis_size("z"))]


def settle(total, parts, core):
    mine = jnp.concatenate([lax.dynamic_index_in_dim(part, core, 0, False) for part in parts])
    other = jnp.concatenate([lax.dynamic_index_in_dim(part, 1 - core, 0, False) for part in parts])
    return mine, swap_axis(other, "core")


def body(chips, clips, clip_count, cotangent, norm_gain, bias_d, bias_ff, w_qkv, w_o, w_up, w_down):
    core, x, y, z = (lax.axis_index(axis) for axis in ("core", "grp", "mid", "z"))
    slots, half, width = clips.shape
    inner = width // 2
    ff = w_up.shape[1]
    swap = (core != x).astype(jnp.int32)

    qkv_piece = own_piece(w_qkv)
    small = jnp.concatenate([norm_gain.reshape(-1), bias_d.reshape(-1), bias_ff]).reshape(-1, 128)
    qkv_0 = send_piece(qkv_piece)
    got_small = swap_axis(after(small, qkv_piece), "grp")
    got_first = swap_owner(after(clips[:1], qkv_piece), chips)
    other_count = swap_axis(clip_count, "core")
    qkv_1 = swap_axis(qkv_0, "mid")
    qkv_2 = swap_axis(qkv_0, "core")
    rest = after(clips[1:], qkv_0)
    got_rest = swap_owner(rest, chips)
    piece = own_piece(w_up).reshape(-1, ff // width, width).transpose(1, 0, 2).reshape(-1, width)
    piece = jnp.concatenate([piece, own_piece(w_o)])
    down_piece = own_piece(w_down)
    qkv_3 = swap_axis(qkv_1, "core")
    qkv_far = (qkv_0, qkv_1, qkv_2, qkv_3)
    piece, down_piece = after((piece, down_piece), qkv_1)
    far_0 = send_piece(piece)
    down_0 = send_piece(down_piece)

    pair = in_order(x, small[None], got_small[None]).reshape(2, -1).astype(F32)
    gains = pair[:, : 2 * inner].reshape(2, 2, inner).transpose(1, 0, 2).reshape(2, width)
    biases = pair[:, 2 * inner : 8 * inner].reshape(2, 6, inner).transpose(1, 0, 2).reshape(6, width)
    bias_hidden = pair[:, 8 * inner :].reshape(1, -1)
    count = jnp.where(swap == 1, other_count, clip_count)[0]
    qkv_bias = jnp.concatenate([biases[1], jnp.zeros_like(biases[1]), biases[2]])[None]
    ids = [jnp.stack([core, swap, (count > s).astype(jnp.int32), x, y, z]).astype(jnp.int32) for s in range(slots)]

    cot_first, cot_others = after((cotangent[:1], cotangent[1:]), qkv_0)
    got_first = after(got_first, (rest, piece, down_piece, cot_first, cot_others))
    blocks, normed, saved, ctx_mine, ctx_other = [], [], [], [], []
    for s in range(slots):
        got, slot = (got_first, 0) if s == 0 else (got_rest, s - 1)
        block, norm, other = project_other(ids[s], clips, s, got, slot, gains[0:1], biases[0:1], w_qkv, qkv_far, qkv_bias)
        received = swap_axis(other, "core")
        mine = project_mine(ids[s], norm, w_qkv, qkv_far, qkv_bias)
        here, there, r_here, r_there, weights, weights_rem = attend(mine, received)
        saved.append((mine, received, here, there, r_here, r_there, weights, weights_rem))
        ctx_mine.append(here)
        ctx_other.append(swap_axis(there, "core"))
        blocks.append(block)
        normed.append(norm)
        if s == 0:
            down_0 = after(down_0, here)
            down_1 = swap_axis(down_0, "mid")
            down_2 = swap_axis(down_0, "core")
            got_rest = after(got_rest, (here, down_0))
        elif s == 1:
            down_1, far_0 = after((down_1, far_0), here)
            down_3 = swap_axis(down_1, "core")
            far_1 = swap_axis(far_0, "mid")
            far_2 = swap_axis(far_0, "core")
            got_rest = after(got_rest, (here, down_1, far_0))
        elif s == 2:
            far_1 = after(far_1, here)
            far_3 = swap_axis(far_1, "core")
    far = (far_0, far_1, far_2, far_3)
    far_down = (down_0, down_1, down_2, down_3)

    others = swap_owner(after(cot_others, here), chips)
    got_cot = [(swap_owner(cot_first, chips), 0)] + [(others, s - 1) for s in range(1, slots)]
    fed, got_result = [], []
    before = ()
    for s in range(slots):
        if s == 2:
            got_cot[s] = (after(others, got_result[0]), s - 1)
        fed.append(
            feed(
                ids[s], s, slots, blocks[s], ctx_mine[s], ctx_other[s], cotangent, *got_cot[s], w_o, w_up, w_down, far, far_down,
                gains, biases, bias_hidden, before,
            )
        )
        before = (fed[-1][7],)
        got_result.append(swap_owner(fed[-1][4], chips))
    active, d_pre, normed2, d_out, result, d_branch, d_ctx_mine, d_ctx_other, sums2, sums_hidden = map(list, zip(*fed))
    d_ctx_got = swap_axis(d_ctx_other[-1], "core")

    sent_down = grad_down_part(ids[0], chips, after(d_out, got_result[1]), active, None)
    sent_up = grad_up_part(ids[0], chips, d_pre, normed2, None)
    sent_out = grad_out_part(ids[0], chips, d_branch, ctx_mine, ctx_other, None)
    rows_down, rows_up, rows_out = (part.shape[2] for part in (sent_down, sent_up, sent_out))
    rows = rows_down + rows_up + rows_out
    joint = grad_down_part(ids[0], chips, d_out, active, swap_axis(sent_down, "core"), (rows, 0, []))
    joint = grad_up_part(
        ids[0], chips, d_pre, normed2, swap_axis(sent_up, "core"),
        (rows, rows_down // rows_up, joint),
    )
    joint = grad_out_part(
        ids[0], chips, d_branch, ctx_mine, ctx_other, swap_axis(sent_out, "core"),
        (rows, (rows_down + rows_up) // rows_out, joint),
    )
    cols = joint[0].shape[-1]
    sums = send_sums([part.reshape(-1, cols) for part in joint])
    early = jnp.concatenate([sum(sums2)[:4], sum(sums_hidden)[0].reshape(-1, width)])

    got_rows = []
    d_mine, d_other, row_grads, sums1, sums_mine, sums_other = [], [], [], [], [], []

    def complete(s, first):
        row_grad, sum1, sum_mine, sum_other = finish(
            ids[s], d_mine[s], after(d_other[s], first), w_qkv, qkv_far, blocks[s], d_branch[s], gains
        )
        row_grads.append(row_grad)
        sums1.append(sum1)
        sums_mine.append(sum_mine[0])
        sums_other.append(sum_other[0])
        return row_grad

    gate = joint
    for s in range(slots):
        mine, received, here, there, r_here, r_there, weights, weights_rem = saved[s]
        d_here, d_there = attend_back(
            s, mine, received, after(d_ctx_mine[s], gate), d_ctx_got, here, there, r_here, r_there, weights, weights_rem
        )
        d_mine.append(d_here)
        d_other.append(swap_axis(d_there, "core"))
        gate = (d_here,)
        if s == 0:
            sums[3] = after(sums[3], d_here)
            gate = (d_here, sums[3])
        elif s == 1:
            sums = add_chips(ids[0], after(sums, d_here), chips, rows)
            gate = sums
            terms = send_chips(sums)
            gate = (gate, [sums[i] for i in range(chips)])
        if s == 2:
            gate = complete(0, (d_here, terms, got_result[2]))
    got_rows.append(swap_owner(row_grads[0], chips))
    sent_qkv = grad_qkv_part(ids[0], chips, d_mine, after(d_other, gate), normed, None)
    gate = complete(1, sent_qkv)
    got_rows.append(swap_owner(row_grads[1], chips))
    part_qkv = grad_qkv_part(
        ids[0], chips, d_mine, d_other, normed, after(swap_axis(sent_qkv, "core"), (gate, got_rows[0])),
        (sent_qkv.shape[2], 0, []),
    )
    qkv_rows = part_qkv[0].shape[1]
    qkv_terms = send_sums([part.reshape(-1, cols) for part in part_qkv])
    complete(2, (part_qkv, got_rows[1]))
    total1 = sum(sums1)
    total_mine, total_other = sum(sums_mine), sum(sums_other)
    grad_bq = in_order(core, total_mine[:inner], total_other[:inner])
    grad_bv = in_order(core, total_mine[2 * inner :], total_other[2 * inner :])
    lines = jnp.concatenate(
        [jnp.stack([total1[0], early[0], total1[1], grad_bq, grad_bv, early[2], early[1], early[3]]), early[4:]]
    )
    lines = lines + swap_axis(lines, "core")
    shape = lines.shape
    lines = sum(send_sums([lines] * 4))
    got_rows.append(swap_owner(after(row_grads[2], lines), chips))
    sums = add_chips(ids[0], qkv_terms, chips, qkv_rows)
    under = as_lines(lines, cols)
    sends = [jnp.concatenate([sums[i], under]) for i in range(chips)]
    qkv_terms = send_chips(sends)
    total = sum(term.astype(F32) for term in after(terms, sends))
    chunks = rows_down // rows_out
    down = total[:rows_down].reshape(chunks, 2, -1, cols).transpose(1, 0, 2, 3).reshape(2, -1, cols)
    up = total[rows_down : rows_down + rows_up].reshape(2, -1, cols)
    out = total[rows_down + rows_up :].reshape(2, -1, cols)
    mine, other = settle(total, (down, up, out), core)
    whole_rows = in_order(core, mine, other, 1)
    n_down, n_up = rows_down // 2, rows_up // 2
    own_down = in_order(core, mine[:n_down].reshape(chunks, -1, cols), other[:n_down].reshape(chunks, -1, cols))
    grad_down = own_down.transpose(0, 2, 1).reshape(2 * chunks * cols, -1)
    grad_up = whole_rows[n_down : n_down + n_up].T
    grad_out = whole_rows[n_down + n_up :].T

    outs = jnp.stack([jnp.where(swap == 1, after(got_result[s], sends), result[s]) for s in range(slots)])
    input_grad = jnp.stack([jnp.where(swap == 1, after(got_rows[s], sends), row_grads[s]) for s in range(slots)]).astype(F32)
    lines = sum(from_lines(term[qkv_rows:], shape) for term in qkv_terms)
    columns = own_half(lines[:8], x, 1)
    hidden_part = own_half(lines[8:], x).reshape(-1)
    total = sum(term[:qkv_rows].astype(F32) for term in qkv_terms)
    mine, other = settle(total, (total.reshape(2, -1, cols),), core)
    grad_qkv = in_order(core, mine, other, 1).T
    return (outs, input_grad, columns[:2], columns[2:], hidden_part, grad_qkv, grad_out, grad_up, grad_down)


def solution(mesh):
    in_specs = (
        P("rep", "grp", None),
        P("rep"),
        P("rep", "grp", None),
        P(None, "grp"),
        P(None, "grp"),
        P("grp"),
        P("grp", None),
        P("grp", None),
        P("grp", None),
        P("grp", None),
    )
    out_specs = (
        P("rep", "grp", None),
        P("rep", "grp", None),
        P(None, "grp"),
        P(None, "grp"),
        P("grp"),
        P("grp", "rep"),
        P("grp", "rep"),
        P("grp", "rep"),
        P("grp", "rep"),
    )
    if mesh.shape["grp"] != 2 or mesh.shape["rep"] != 16:
        return jax.shard_map(plain_body, mesh=mesh, in_specs=in_specs, out_specs=out_specs, check_vma=False)
    chips = mesh.shape["rep"] // 4
    split = Mesh(mesh.devices.reshape(chips, 2, 2, 2), AXES)
    rep = lambda spec: P(*[AXES[:3] if axis == "rep" else axis for axis in spec])
    return jax.shard_map(
        functools.partial(body, chips),
        mesh=split,
        in_specs=tuple(rep(spec) for spec in in_specs),
        out_specs=tuple(rep(spec) for spec in out_specs),
        check_vma=False,
    )
```

```python
import functools

import jax
import jax.numpy as jnp
from jax import lax
from jax.experimental import pallas as pl
from jax.experimental.pallas import tpu as pltpu
from jax.sharding import Mesh
from jax.sharding import PartitionSpec as P

H = 16
HD = 64
EPSILON = 1e-06

F32 = jnp.float32
BF = jnp.bfloat16
LOG2E = 1.4426950408889634
SCALE = HD ** -0.5
AXES = ("z", "mid", "core", "grp")
BQ = 512
TK = 224
COST = 5 * 10**10
LIMIT = 70.0


def dot(a, b, dims):
    return lax.dot_general(a, b, (dims, ((), ())), preferred_element_type=F32)


def nt(a, b):
    return dot(a, b, ((1,), (1,)))


def nn(a, b):
    return dot(a, b, ((1,), (0,)))


def tn(a, b):
    return dot(a, b, ((0,), (0,)))


def pair_mask(a):
    lane = lax.broadcasted_iota(jnp.int32, (1, 128), 1)
    return (lane < HD) if a == 0 else (lane >= HD)

def norm_peak(x, np_):
    inner = x.shape[1]
    r = lax.broadcasted_iota(jnp.int32, (inner, 128), 0)
    c = lax.broadcasted_iota(jnp.int32, (inner, 128), 1)
    ones = jnp.where(r // HD == c, 1.0, 0.0).astype(BF)
    xf = x.astype(F32)
    return jnp.max(nn((xf * xf).astype(BF), ones), axis=0, keepdims=True)

def attend_kernel(own, rec, oo, orr, ro, rr, p_out, prem_out, q_s, k_s, vt_s, o_s, r_s, fast, *, nb, np_, rem):
    half = own.shape[0]
    inner = own.shape[1] // 3
    full = 2 * half
    t = pl.program_id(0)
    last = np_ * nb

    @pl.when(t == 0)
    def _():
        q_s[:half] = own[:, :inner]
        q_s[half:] = rec[:, :inner]
        k_s[:half] = own[:, inner:2 * inner]
        k_s[half:] = rec[:, inner:2 * inner]
        row = lax.broadcasted_iota(jnp.int32, (128, 1), 0)
        for p in range(np_):
            cols = slice(2 * inner + p * 128, 2 * inner + (p + 1) * 128)
            vt = jnp.concatenate([own[:, cols], rec[:, cols]], axis=0).T
            for a in range(2):
                mine = (row < HD) if a == 0 else (row >= HD)
                vt_s[2 * p + a] = jnp.where(mine, vt, 1.0).astype(BF)
        peak = jnp.max(norm_peak(q_s[...], np_) * norm_peak(k_s[...], np_))
        fast[0] = (peak * (1.1 * SCALE * SCALE) < LIMIT * LIMIT).astype(jnp.int32)

    def store(o, rows, cols):
        oa, ob = o
        ra = 1.0 / oa[HD:]
        rb = 1.0 / ob[:HD]
        o_s[rows, cols] = jnp.concatenate([oa[:HD] * ra, ob[HD:] * rb], axis=0).T.astype(BF)
        r_s[rows, cols] = jnp.concatenate([ra, rb], axis=0).T

    def main(quick):
        p = t // nb
        b = t % nb
        rows = pl.ds(pl.multiple_of(b * BQ, BQ), BQ)
        cols = pl.ds(pl.multiple_of(p * 128, 128), 128)
        q = q_s[rows, cols]
        def weights(a):
            qa = jnp.where(pair_mask(a), q, 0.0).astype(BF)
            if quick:
                for j in range(full // TK):
                    tile = slice(j * TK, (j + 1) * TK)
                    s = nt(k_s[tile, cols], qa)
                    p_out[0, a, tile] = jnp.exp2(s * (LOG2E * SCALE)).astype(BF)
            else:
                s = nt(k_s[:, cols], qa)
                m = jnp.max(s, axis=0, keepdims=True)
                p_out[0, a] = jnp.exp2((s - m) * (LOG2E * SCALE)).astype(BF)
        weights(0)
        weights(1)
        oa = nn(vt_s[2 * p], p_out[0, 0])
        ob = nn(vt_s[2 * p + 1], p_out[0, 1])
        store((oa, ob), rows, cols)

    @pl.when((t < last) & (fast[0] == 1))
    def _():
        main(True)

    @pl.when((t < last) & (fast[0] == 0))
    def _():
        main(False)

    @pl.when(t == last)
    def _():
        if rem:
            lane = lax.broadcasted_iota(jnp.int32, (1, 256), 1)
            for u in range(np_ // 2):
                q = q_s[nb * BQ:, u * 256:(u + 1) * 256]
                qd = jnp.concatenate([jnp.where(lane // HD == h, q, 0.0).astype(BF) for h in range(4)], axis=0)
                s = nt(k_s[:, u * 256:(u + 1) * 256], qd)
                m = jnp.max(s, axis=0, keepdims=True)
                prem_out[u] = jnp.exp2((s - m) * (LOG2E * SCALE)).astype(BF)
                for v in range(2):
                    oa = nn(vt_s[4 * u + 2 * v], prem_out[u])
                    ob = nn(vt_s[4 * u + 2 * v + 1], prem_out[u])
                    ra = 1.0 / oa[HD:]
                    rb = 1.0 / ob[:HD]
                    x = jnp.concatenate([oa[:HD] * ra, ob[HD:] * rb], axis=0).T
                    r = jnp.concatenate([ra, rb], axis=0).T
                    ha, hb = 2 * v, 2 * v + 1
                    pick = lambda y: jnp.where(pair_mask(0), y[ha * rem:(ha + 1) * rem], y[hb * rem:(hb + 1) * rem])
                    cols = slice((2 * u + v) * 128, (2 * u + v + 1) * 128)
                    o_s[nb * BQ:, cols] = pick(x).astype(BF)
                    r_s[nb * BQ:, cols] = pick(r)
        oo[...] = o_s[:half]
        orr[...] = o_s[half:]
        ro[...] = r_s[:half]
        rr[...] = r_s[half:]

def attend(own, rec):
    half, w = own.shape
    inner = w // 3
    np_ = inner // 128
    full = 2 * half
    nb = full // BQ
    rem = full - nb * BQ
    last = np_ * nb
    whole = lambda shape: pl.BlockSpec(shape, lambda t: (0,) * len(shape))
    return pl.pallas_call(
        functools.partial(attend_kernel, nb=nb, np_=np_, rem=rem),
        grid=(last + 1,),
        in_specs=[whole((half, w))] * 2,
        out_specs=[whole((half, inner))] * 4 + [pl.BlockSpec((1, 2, full, BQ), lambda t: (jnp.minimum(t, last - 1), 0, 0, 0)), whole((np_ // 2, full, 4 * rem))],
        out_shape=[jax.ShapeDtypeStruct((half, inner), BF)] * 2 + [jax.ShapeDtypeStruct((half, inner), F32)] * 2
        + [jax.ShapeDtypeStruct((last, 2, full, BQ), BF), jax.ShapeDtypeStruct((np_ // 2, full, 4 * rem), BF)],
        scratch_shapes=[
            pltpu.VMEM((full, inner), BF), pltpu.VMEM((full, inner), BF), pltpu.VMEM((2 * np_, 128, full), BF),
            pltpu.VMEM((full, inner), BF), pltpu.VMEM((full, inner), F32), pltpu.SMEM((1,), jnp.int32)],
        cost_estimate=pl.CostEstimate(flops=0, bytes_accessed=0, transcendentals=0),
        compiler_params=pltpu.CompilerParams(vmem_limit_bytes=60 * 1024 * 1024),
    )(own, rec)


def attend_back_kernel(own, rec, do_o, do_r, o_o, o_r, r_o, r_r, e, erem, out_o, out_r,
               q_s, k_s, v_s, kt_s, do_s, pr_s, ds_s, dq_s, dk_s, dv_s, *, nb, np_, rem):
    half = own.shape[0]
    inner = own.shape[1] // 3
    full = 2 * half
    t = pl.program_id(0)
    last = np_ * nb

    @pl.when(t == 0)
    def _():
        for lo, src, d, o, r in ((0, own, do_o, o_o, r_o), (half, rec, do_r, o_r, r_r)):
            rows = slice(lo, lo + half)
            q_s[rows] = src[:, :inner]
            k_s[rows] = src[:, inner:2 * inner]
            v_s[rows] = src[:, 2 * inner:]
            dn = (d[...].astype(F32) * r[...]).astype(BF)
            do_s[rows] = dn
            pr_s[rows] = dn.astype(F32) * o[...].astype(F32)
        for p in range(np_):
            kt_s[p * 128:(p + 1) * 128] = k_s[:, p * 128:(p + 1) * 128].T
        dk_s[...] = jnp.zeros_like(dk_s)
        dv_s[...] = jnp.zeros_like(dv_s)

    @pl.when(t < last)
    def _():
        p = t // nb
        b = t % nb
        rows = pl.ds(pl.multiple_of(b * BQ, BQ), BQ)
        cols = pl.ds(pl.multiple_of(p * 128, 128), 128)
        q = q_s[rows, cols]
        dn = do_s[rows, cols]
        prod = pr_s[rows, cols].T
        qs, dns = [], []
        for a in range(2):
            qs.append(jnp.where(pair_mask(a), q, 0.0).astype(BF))
            dns.append(jnp.where(pair_mask(a), dn, 0.0).astype(BF))
        for a in range(2):
            delta = jnp.sum(prod[a * HD:(a + 1) * HD], axis=0, keepdims=True)
            for j in range(full // TK):
                tile = slice(j * TK, (j + 1) * TK)
                dp = nt(v_s[tile, cols], dns[a])
                ds_s[a, tile] = (e[0, a, tile].astype(F32) * (dp - delta)).astype(BF)
        for j in range(full // TK):
            tile = slice(j * TK, (j + 1) * TK)
            dv_s[tile, cols] += nn(e[0, 0, tile], dns[0]) + nn(e[0, 1, tile], dns[1])
        dqt = []
        for a in range(2):
            dqt.append(nn(kt_s[pl.ds(pl.multiple_of(p * 128, 128), 128)], ds_s[a])[a * HD:(a + 1) * HD])
        dq_s[rows, cols] = (jnp.concatenate(dqt, axis=0) * SCALE).T.astype(BF)
        for j in range(full // TK):
            tile = slice(j * TK, (j + 1) * TK)
            dk_s[tile, cols] += nn(ds_s[0, tile], qs[0]) + nn(ds_s[1, tile], qs[1])

    @pl.when(t == last)
    def _():
        if rem:
            lane = lax.broadcasted_iota(jnp.int32, (1, 256), 1)
            def spread(x):
                return jnp.concatenate([jnp.where(lane // HD == h, x, 0.0).astype(x.dtype) for h in range(4)], axis=0)
            for u in range(np_ // 2):
                cols = slice(u * 256, (u + 1) * 256)
                qd = spread(q_s[nb * BQ:, cols])
                dd = spread(do_s[nb * BQ:, cols])
                delta = jnp.sum(spread(pr_s[nb * BQ:, cols]).T, axis=0, keepdims=True)
                dp = nt(v_s[:, cols], dd)
                ds = (erem[u].astype(F32) * (dp - delta)).astype(BF)
                dv_s[:, cols] += nn(erem[u], dd)
                dk_s[:, cols] += nn(ds, qd)
                x = nn(kt_s[cols], ds).T * SCALE
                dq = x[:rem]
                for h in range(1, 4):
                    dq = jnp.where(lane // HD == h, x[h * rem:(h + 1) * rem], dq)
                dq_s[nb * BQ:, cols] = dq.astype(BF)
        for lo, dst in ((0, out_o), (half, out_r)):
            rows = slice(lo, lo + half)
            dst[:, :inner] = dq_s[rows]
            dst[:, inner:2 * inner] = (dk_s[rows] * SCALE).astype(BF)
            dst[:, 2 * inner:] = dv_s[rows].astype(BF)

def attend_back(slot, own, rec, do_o, do_r, o_o, o_r, r_o, r_r, e, erem):
    half, w = own.shape
    inner = w // 3
    np_ = inner // 128
    full = 2 * half
    nb = full // BQ
    rem = full - nb * BQ
    last = np_ * nb
    whole = lambda shape, **kw: pl.BlockSpec(shape, lambda t: (0,) * len(shape), **kw)
    one = dict(pipeline_mode=pl.Buffered(1))
    return pl.pallas_call(
        functools.partial(attend_back_kernel, nb=nb, np_=np_, rem=rem),
        grid=(last + 1,),
        in_specs=[whole((half, w), **one)] * 2
        + [whole((half, inner), **one), pl.BlockSpec((None, half, inner), lambda t: (slot, 0, 0), **one)]
        + [whole((half, inner), **one)] * 4
        + [pl.BlockSpec((1, 2, full, BQ), lambda t: (jnp.minimum(t, last - 1), 0, 0, 0)), whole(erem.shape, **one)],
        out_specs=[whole((half, w), **one)] * 2,
        out_shape=[jax.ShapeDtypeStruct((half, w), BF)] * 2,
        scratch_shapes=[
            pltpu.VMEM((full, inner), BF), pltpu.VMEM((full, inner), BF), pltpu.VMEM((full, inner), BF),
            pltpu.VMEM((inner, full), BF), pltpu.VMEM((full, inner), BF), pltpu.VMEM((full, inner), F32),
            pltpu.VMEM((2, full, BQ), BF), pltpu.VMEM((full, inner), BF),
            pltpu.VMEM((full, inner), F32), pltpu.VMEM((full, inner), F32)],
        cost_estimate=pl.CostEstimate(flops=COST, bytes_accessed=0, transcendentals=0),
        compiler_params=pltpu.CompilerParams(vmem_limit_bytes=62 * 1024 * 1024),
    )(own, rec, do_o, do_r, o_o, o_r, r_o, r_r, e, erem)


def matmul(left, right):
    return jnp.dot(left, right, preferred_element_type=jnp.float32)


def layer_norm(values, gain, shift):
    centred = values - jnp.mean(values, -1, keepdims=True)
    spread = jnp.mean(centred * centred, -1, keepdims=True)
    inverse = lax.rsqrt(spread + EPSILON)
    scaled = centred * inverse
    return (scaled, inverse, scaled * gain + shift)


def norm_back(scaled, inverse, gain, incoming):
    weighted = incoming * gain
    first = jnp.mean(weighted, -1, keepdims=True)
    second = jnp.mean(weighted * scaled, -1, keepdims=True)
    return inverse * (weighted - first - scaled * second)


def fetch_weights(shards):
    return (
        lax.all_gather(shards[0], "grp", axis=0, tiled=True),
        lax.all_gather(shards[1], "grp", axis=0, tiled=True),
        lax.all_gather(shards[2], "grp", axis=0, tiled=True),
        lax.all_gather(shards[3], "grp", axis=0, tiled=True),
        lax.all_gather(shards[4], "grp", axis=1, tiled=True),
        lax.all_gather(shards[5], "grp", axis=1, tiled=True),
        lax.all_gather(shards[6], "grp", axis=0, tiled=True),
    )


def shard_grads(weight_grads):
    return (
        lax.psum_scatter(weight_grads[0], "grp", scatter_dimension=1, tiled=True),
        lax.psum_scatter(weight_grads[1], "grp", scatter_dimension=1, tiled=True),
        lax.psum_scatter(weight_grads[2], "grp", scatter_dimension=0, tiled=True),
        lax.psum_scatter(weight_grads[3], "grp", scatter_dimension=0, tiled=True),
        lax.psum_scatter(weight_grads[4], "grp", scatter_dimension=0, tiled=True),
        lax.psum_scatter(weight_grads[5], "grp", scatter_dimension=0, tiled=True),
        lax.psum_scatter(weight_grads[6], "grp", scatter_dimension=0, tiled=True),
    )


def raw_scores(query, keys):
    rows = query.shape[0]
    length = keys.shape[0]
    return jnp.einsum(
        "qhd,khd->hqk",
        query.reshape(rows, H, HD),
        keys.reshape(length, H, HD),
        preferred_element_type=jnp.float32,
    ) * HD ** (-0.5)


def score_probs(query, keys):
    return jax.nn.softmax(raw_scores(query, keys), axis=-1)


def forward_pass(row_block, gathered):
    qkv_weight, out_weight, up_weight, down_weight, gains, biases, hidden_bias = gathered
    gain_f = gains.astype(jnp.float32)
    bias_f = biases.astype(jnp.float32)
    rows = row_block.shape[0]
    model_width = row_block.shape[1]
    inputs = row_block.astype(jnp.float32)
    scaled1, inverse1, normed = layer_norm(inputs, gain_f[0], bias_f[0])
    normed = normed.astype(jnp.bfloat16)
    shift = jnp.concatenate([bias_f[1], jnp.zeros_like(bias_f[1]), bias_f[2]])
    qkv = (matmul(normed, qkv_weight) + shift).astype(jnp.bfloat16)
    query = qkv[:, :model_width]
    key_part = qkv[:, model_width : 2 * model_width]
    value_part = qkv[:, 2 * model_width :]
    keys, values = (
        lax.all_gather(key_part, "grp", axis=0, tiled=True),
        lax.all_gather(value_part, "grp", axis=0, tiled=True),
    )
    length = keys.shape[0]
    probs = score_probs(query, keys)
    context = (
        jnp.einsum(
            "hqk,khd->qhd",
            probs.astype(jnp.bfloat16),
            values.reshape(length, H, HD),
            preferred_element_type=jnp.float32,
        )
        .reshape(rows, model_width)
        .astype(jnp.bfloat16)
    )
    hidden = inputs + matmul(context, out_weight) + bias_f[3]
    scaled2, inverse2, normed2 = layer_norm(hidden, gain_f[1], bias_f[4])
    normed2 = normed2.astype(jnp.bfloat16)
    pre = matmul(normed2, up_weight) + hidden_bias.astype(jnp.float32)
    active = jax.nn.gelu(pre, approximate=False).astype(jnp.bfloat16)
    result = hidden + matmul(active, down_weight) + bias_f[5]
    saved = (
        scaled1,
        inverse1,
        normed,
        query,
        keys,
        values,
        context,
        scaled2,
        inverse2,
        normed2,
        pre,
        active,
    )
    return (result, saved)


def backward_pass(incoming, weight, saved, gathered):
    qkv_weight, out_weight, up_weight, down_weight, gains, biases, hidden_bias = gathered
    gain_f = gains.astype(jnp.float32)
    (
        scaled1,
        inverse1,
        normed,
        query,
        keys,
        values,
        context,
        scaled2,
        inverse2,
        normed2,
        pre,
        active,
    ) = saved
    rows = query.shape[0]
    model_width = query.shape[1]
    length = keys.shape[0]
    d_out = incoming * weight.astype(jnp.bfloat16)
    d_out_f = d_out.astype(jnp.float32)
    grad_down = jnp.einsum("rf,rd->fd", active, d_out, preferred_element_type=jnp.float32)
    grad_b2 = jnp.sum(d_out_f, 0)
    d_act = jnp.einsum("rd,fd->rf", d_out, down_weight, preferred_element_type=jnp.float32)
    unused, gelu_pull = jax.vjp(lambda inputs: jax.nn.gelu(inputs, approximate=False), pre)
    d_pre = gelu_pull(d_act)[0].astype(jnp.bfloat16)
    grad_up = jnp.einsum("rd,rf->df", normed2, d_pre, preferred_element_type=jnp.float32)
    grad_hidden_bias = jnp.sum(d_pre.astype(jnp.float32), 0)
    d_norm2 = jnp.einsum("rf,df->rd", d_pre, up_weight, preferred_element_type=jnp.float32)
    d_hidden = d_out_f + norm_back(scaled2, inverse2, gain_f[1], d_norm2)
    grad_g2 = jnp.sum(d_norm2 * scaled2, 0)
    grad_beta2 = jnp.sum(d_norm2, 0)
    d_branch = d_hidden.astype(jnp.bfloat16)
    grad_out = jnp.einsum("rd,re->de", context, d_branch, preferred_element_type=jnp.float32)
    grad_bo = jnp.sum(d_branch.astype(jnp.float32), 0)
    d_context = jnp.einsum(
        "re,de->rd", d_branch, out_weight, preferred_element_type=jnp.float32
    ).astype(jnp.bfloat16)
    scores = raw_scores(query, keys)
    probs = jax.nn.softmax(scores, axis=-1)
    context_heads = d_context.reshape(rows, H, HD)
    d_probs = jnp.einsum(
        "qhd,khd->hqk",
        context_heads,
        values.reshape(length, H, HD),
        preferred_element_type=jnp.float32,
    )
    delta = jnp.sum(probs * d_probs, -1)
    d_scores = (probs * (d_probs - delta[..., None])).astype(jnp.bfloat16)
    d_query = (
        jnp.einsum(
            "hqk,khd->qhd",
            d_scores,
            keys.reshape(length, H, HD),
            preferred_element_type=jnp.float32,
        )
        * HD ** (-0.5)
    ).reshape(rows, model_width)
    d_value = jnp.einsum(
        "hqk,qhd->khd",
        probs.astype(jnp.bfloat16),
        context_heads,
        preferred_element_type=jnp.float32,
    ).reshape(length, model_width)
    d_key = (
        jnp.einsum(
            "hqk,qhd->khd", d_scores, query.reshape(rows, H, HD), preferred_element_type=jnp.float32
        )
        * HD ** (-0.5)
    ).reshape(length, model_width)
    d_key, d_value = (
        lax.psum_scatter(d_key, "grp", scatter_dimension=0, tiled=True),
        lax.psum_scatter(d_value, "grp", scatter_dimension=0, tiled=True),
    )
    d_qkv = jnp.concatenate(
        [d_query.astype(jnp.bfloat16), d_key.astype(jnp.bfloat16), d_value.astype(jnp.bfloat16)], 1
    )
    grad_qkv = jnp.einsum("rd,re->de", normed, d_qkv, preferred_element_type=jnp.float32)
    d_qkv_f = d_qkv.astype(jnp.float32)
    grad_bq = jnp.sum(d_qkv_f[:, :model_width], 0)
    grad_bv = jnp.sum(d_qkv_f[:, 2 * model_width :], 0)
    d_norm1 = jnp.einsum("re,de->rd", d_qkv, qkv_weight, preferred_element_type=jnp.float32)
    row_grad = d_hidden + norm_back(scaled1, inverse1, gain_f[0], d_norm1)
    grad_g1 = jnp.sum(d_norm1 * scaled1, 0)
    grad_beta1 = jnp.sum(d_norm1, 0)
    grad_gains = jnp.stack([grad_g1, grad_g2])
    grad_biases = jnp.stack([grad_beta1, grad_bq, grad_bv, grad_bo, grad_beta2, grad_b2])
    weight_grads = (
        grad_gains,
        grad_biases,
        grad_hidden_bias,
        grad_qkv,
        grad_out,
        grad_up,
        grad_down,
    )
    return (row_grad, weight_grads)


def plain_body(clips, clip_count, cotangent, norm_gain, bias_d, bias_ff, w_qkv, w_o, w_up, w_down):
    shards = (w_qkv, w_o, w_up, w_down, norm_gain, bias_d, bias_ff)
    number = clips.shape[0]
    outputs = []
    records = []
    actives = []
    for slot_index in range(number):
        gathered = fetch_weights(shards)
        active = (clip_count[0] > slot_index).astype(jnp.float32)
        result, saved = forward_pass(clips[slot_index], gathered)
        outputs.append((result * active).astype(jnp.bfloat16))
        records.append(saved)
        actives.append(active)
    row_grads = [None] * number
    totals = None
    for slot_index in reversed(range(number)):
        gathered = fetch_weights(shards)
        row_grad, weight_grads = backward_pass(
            cotangent[slot_index], actives[slot_index], records[slot_index], gathered
        )
        row_grads[slot_index] = row_grad
        totals = (
            weight_grads
            if totals is None
            else jax.tree.map(lambda left, right: left + right, totals, weight_grads)
        )
    totals = shard_grads(totals)
    small_sums = lax.psum((totals[0], totals[1], totals[2]), "rep")
    matrix_sums = (
        lax.psum_scatter(totals[3], "rep", scatter_dimension=1, tiled=True),
        lax.psum_scatter(totals[4], "rep", scatter_dimension=1, tiled=True),
        lax.psum_scatter(totals[5], "rep", scatter_dimension=1, tiled=True),
        lax.psum_scatter(totals[6], "rep", scatter_dimension=1, tiled=True),
    )
    return (jnp.stack(outputs), jnp.stack(row_grads)) + tuple(small_sums) + tuple(matrix_sums)


def row_stats(values):
    centred = values - jnp.mean(values, -1, keepdims=True)
    inverse = lax.rsqrt(jnp.mean(centred * centred, -1, keepdims=True) + EPSILON)
    return centred * inverse, inverse


def whole(shape, **kw):
    return pl.BlockSpec(shape, lambda *_: (0,) * len(shape), **kw)


def call(kernel, ids, grid, in_specs, out_specs, out_shape, args, scratch=(), flops=0, limit=60, aliases=()):
    return pl.pallas_call(
        kernel,
        grid_spec=pltpu.PrefetchScalarGridSpec(
            num_scalar_prefetch=1, grid=grid, in_specs=in_specs, out_specs=out_specs, scratch_shapes=list(scratch)
        ),
        out_shape=out_shape,
        cost_estimate=pl.CostEstimate(flops=int(flops), bytes_accessed=0, transcendentals=0),
        input_output_aliases=dict(aliases),
        compiler_params=pltpu.CompilerParams(vmem_limit_bytes=limit * 1024 * 1024),
    )(ids, *args)


def slot_of(shape, s):
    return pl.BlockSpec((None,) + shape, lambda *_: (s,) + (0,) * len(shape))


def piece_places(ids):
    y, core = ids[4], ids[0]
    return (2 * y + core, 2 * (1 - y) + core, 2 * y + 1 - core, 2 * (1 - y) + 1 - core)


def lay_pieces(ids, target, pieces):
    size = target.shape[0] // len(pieces)
    for piece, place in zip(pieces, piece_places(ids)):
        target[pl.ds(pl.multiple_of(place * size, size), size)] = piece[...]


def by_rows(ids, x, near, far):
    size = near.shape[0]
    own = pl.ds(pl.multiple_of(ids[3] * size, size), size)
    across = pl.ds(pl.multiple_of((1 - ids[3]) * size, size), size)
    return nn(x[:, own], near[...]) + nn(x[:, across], far[...])


def project_other_kernel(ids, mine, got, gain, shift, near, p0, p1, p2, p3, bias, block, normed, out, far_s):
    @pl.when(pl.program_id(0) == 0)
    def _():
        x = jnp.where(ids[1] == 1, got[...], mine[...])
        block[...] = x
        hat, unused = row_stats(x.astype(F32))
        normed[...] = (hat * gain[...] + shift[...]).astype(BF)

    lay_pieces(ids, far_s, (p0, p1, p2, p3))
    out[...] = (by_rows(ids, normed, near, far_s) + bias[...]).astype(BF)


def project_other(ids, mine, mine_slot, got, got_slot, gain, shift, near, far, bias):
    rows, width = mine.shape[1:]
    inner = width // 2
    columns = lambda i, ids: (0, 2 * i + 1 - ids[0])
    return call(
        project_other_kernel,
        ids,
        (3,),
        [
            slot_of((rows, width), mine_slot),
            slot_of((rows, width), got_slot),
            whole((1, width)),
            whole((1, width)),
            pl.BlockSpec((inner, inner), columns),
        ]
        + [pl.BlockSpec((inner // 4, inner), columns)] * 4
        + [pl.BlockSpec((1, inner), columns)],
        [whole((rows, width)), whole((rows, width)), pl.BlockSpec((rows, inner), lambda i, ids: (0, i))],
        [
            jax.ShapeDtypeStruct((rows, width), BF),
            jax.ShapeDtypeStruct((rows, width), BF),
            jax.ShapeDtypeStruct((rows, 3 * inner), BF),
        ],
        (mine, got, gain, shift, near, *far, bias),
        scratch=[pltpu.VMEM((inner, inner), BF)],
    )


def project_mine_kernel(ids, normed, near, p0, p1, p2, p3, bias, out, far_s):
    lay_pieces(ids, far_s, (p0, p1, p2, p3))
    out[...] = (by_rows(ids, normed, near, far_s) + bias[...]).astype(BF)


def project_mine(ids, normed, near, far, bias):
    rows, width = normed.shape
    inner = width // 2
    columns = lambda i, ids: (0, 2 * i + ids[0])
    return call(
        project_mine_kernel,
        ids,
        (3,),
        [whole((rows, width)), pl.BlockSpec((inner, inner), columns)]
        + [pl.BlockSpec((inner // 4, inner), columns)] * 4
        + [pl.BlockSpec((1, inner), columns)],
        pl.BlockSpec((rows, inner), lambda i, ids: (0, i)),
        jax.ShapeDtypeStruct((rows, 3 * inner), BF),
        (normed, near, *far, bias),
        scratch=[pltpu.VMEM((inner, inner), BF)],
    )


def feed_kernel(
    ids, block, ctx_mine, ctx_other, cot_mine, cot_got, out_near, o0, o1, o2, o3, up_near, u0, u1, u2, u3,
    down_near, d0, d1, d2, d3, gain, biases, bias_hidden, *rest,
):
    (
        active, d_pre, normed2, d_out, result, d_branch, d_ctx_mine, d_ctx_other, sums, sum_hidden,
        hidden_s, total_s, d_norm_s, up_far, w_down,
    ) = rest[-15:]
    j = pl.program_id(0)
    half = pl.num_programs(0) // 2
    inner = ctx_mine.shape[1]
    live = ids[2].astype(F32)
    own = pl.ds(pl.multiple_of(ids[3] * inner, inner), inner)
    across = pl.ds(pl.multiple_of((1 - ids[3]) * inner, inner), inner)
    lay_pieces(ids, up_far, (u0, u1, u2, u3))

    out_far = w_down.at[:inner]

    straight = ids[0] == ids[3]

    @pl.when(j == 0)
    def _():
        lay_pieces(ids, out_far, (o0, o1, o2, o3))
        w_mine = jnp.where(straight, out_near[...], out_far[...])
        w_other = jnp.where(straight, out_far[...], out_near[...])
        hidden = block[...].astype(F32) + (nn(ctx_mine[...], w_mine) + nn(ctx_other[...], w_other))
        hidden = hidden + biases[3:4]
        hidden_s[...] = hidden
        hat, unused = row_stats(hidden)
        normed2[...] = (hat * gain[1:2] + biases[4:5]).astype(BF)
        d = (jnp.where(ids[1] == 1, cot_got[...], cot_mine[...]).astype(F32) * live).astype(BF)
        d_out[...] = d

    @pl.when(j < half)
    def _():
        w_down[...] = down_near[...]

    @pl.when(j >= half)
    def _():
        here = ids[4] == j - half
        size = d0.shape[0]
        w_down[pl.ds(pl.multiple_of(ids[0] * size, size), size)] = jnp.where(here, d0[...], d1[...])
        w_down[pl.ds(pl.multiple_of((1 - ids[0]) * size, size), size)] = jnp.where(here, d2[...], d3[...])

    rows = block.shape[0]
    parts = (slice(0, rows // 32 * 16), slice(rows // 32 * 16, rows))

    def begin(part):
        pre = nn(normed2[part, own], up_near[...]) + nn(normed2[part, across], up_far[...])
        return pre, nt(d_out[part], w_down[...])

    def middle(part, pre, d_act):
        pre = pre + bias_hidden[...]
        phi = 0.5 + 0.5 * lax.erf(pre * 0.7071067811865476)
        act = (pre * phi).astype(BF)
        active[part] = act
        slope = phi + pre * (jnp.exp2(pre * pre * (-0.5 * LOG2E)) * 0.3989422804014327)
        dp = d_act * slope
        total = jnp.sum(dp, 0, keepdims=True)
        dp = dp.astype(BF)
        d_pre[part] = dp
        return act, dp, total

    def end(part, act, dp):
        total_s[part] += nn(act, w_down[...])
        d_norm_s[part, own] += nt(dp, up_near[...])
        d_norm_s[part, across] += nt(dp, up_far[...])

    @pl.when(j == 0)
    def _():
        total_s[...] = jnp.zeros_like(total_s)
        d_norm_s[...] = jnp.zeros_like(d_norm_s)

    first, second = parts
    begun = begin(first)
    begun_second = begin(second)
    act, dp, total = middle(first, *begun)
    end(first, act, dp)
    act, dp, total_second = middle(second, *begun_second)
    end(second, act, dp)
    sum_hidden[...] = jnp.broadcast_to(total + total_second, sum_hidden.shape)

    @pl.when(j == pl.num_programs(0) - 1)
    def _():
        hidden = hidden_s[...]
        result[...] = ((hidden + total_s[...] + biases[5:6]) * live).astype(BF)
        hat, inverse = row_stats(hidden)
        d_norm = d_norm_s[...]
        weighted = d_norm * gain[1:2]
        first = jnp.mean(weighted, -1, keepdims=True)
        second = jnp.mean(weighted * hat, -1, keepdims=True)
        d = d_out[...].astype(F32)
        branch = (d + inverse * (weighted - first - hat * second)).astype(BF)
        d_branch[...] = branch
        sums[...] = jnp.concatenate(
            [
                jnp.sum(d_norm * hat, 0, keepdims=True),
                jnp.sum(d_norm, 0, keepdims=True),
                jnp.sum(branch.astype(F32), 0, keepdims=True),
                jnp.sum(d, 0, keepdims=True),
                jnp.zeros((4, d.shape[1]), F32),
            ],
            0,
        )
        lay_pieces(ids, out_far, (o0, o1, o2, o3))
        w_mine = jnp.where(straight, out_near[...], out_far[...])
        w_other = jnp.where(straight, out_far[...], out_near[...])
        d_ctx_mine[...] = nt(branch, w_mine).astype(BF)
        d_ctx_other[...] = nt(branch, w_other).astype(BF)


def feed(ids, slot, slots, block, ctx_mine, ctx_other, cot_mine, cot_got, got_slot, w_out, w_up, w_down, far, far_down, gain, biases, bias_hidden, before):
    rows, width = block.shape
    inner = width // 2
    ff = w_up.shape[1]
    chunk = width
    steps = ff // chunk
    one = dict(pipeline_mode=pl.Buffered(1))
    full = whole((rows, width), **one)
    part = whole((rows, inner), **one)
    place = lambda j, ids: (0, (ids[3] * (steps // 2) + j) % steps)
    columns = pl.BlockSpec((rows, chunk), place)
    one_slot = lambda shape, at=slot: pl.BlockSpec((None,) + shape, lambda *_: (at, 0, 0), **one)
    wide = jax.ShapeDtypeStruct((rows, width), BF)
    args = (
        block, ctx_mine, ctx_other, cot_mine, cot_got, w_out, *far, w_up, *far, w_down, *far_down, gain, biases, bias_hidden,
    )
    return call(
        feed_kernel,
        ids,
        (steps,),
        [full, part, part, one_slot((rows, width)), one_slot((rows, width), got_slot), whole((inner, width), **one)]
        + [pl.BlockSpec((inner // 4, width), lambda j, ids: (steps, 0), **one)] * 4
        + [pl.BlockSpec((inner, chunk), place)]
        + [pl.BlockSpec((inner // 4, chunk), lambda j, ids: (place(j, ids)[1], 0))] * 4
        + [pl.BlockSpec((chunk, width), lambda j, ids: (jnp.minimum(j, steps // 2 - 1), 0), **one)]
        + [whole((ff // 8, width), **one)] * 4
        + [whole(gain.shape), whole(biases.shape), pl.BlockSpec((1, chunk), place)]
        + [pl.BlockSpec(memory_space=pl.ANY)] * len(before),
        [
            columns, columns, full, full, full, full, part, one_slot((rows, inner)),
            whole((8, width)),
            pl.BlockSpec((8, chunk), place),
        ],
        [
            jax.ShapeDtypeStruct((rows, ff), BF), jax.ShapeDtypeStruct((rows, ff), BF),
            wide, wide, wide, wide,
            jax.ShapeDtypeStruct((rows, inner), BF), jax.ShapeDtypeStruct((slots, rows, inner), BF),
            jax.ShapeDtypeStruct((8, width), F32), jax.ShapeDtypeStruct((8, ff), F32),
        ],
        args + tuple(before),
        scratch=[pltpu.VMEM((rows, width), F32)] * 3
        + [pltpu.VMEM((inner, chunk), BF), pltpu.VMEM((chunk, width), BF)],
        flops=COST,
        limit=62,
        aliases=[(1 + len(args), 7)] if before else (),
    )


def outer_sum(left, right):
    return tn(jnp.concatenate(left), jnp.concatenate(right))


def put_block(ids, outs, rec, piece, x, y, z, rows):
    place = 2 * (x != ids[3]).astype(jnp.int32) + (y != ids[4]).astype(jnp.int32)
    if rec is None:
        outs[0][place, z, rows] = piece.astype(BF)
        return
    for i, out in enumerate(outs):

        @pl.when(place == i)
        def _(i=i, out=out):
            out[z, rows] = (piece + rec[i, z, rows].astype(F32)).astype(BF)


def split_refs(refs, counts):
    parts, at = [], 0
    for count in counts:
        parts.append(refs[at : at + count])
        at += count
    rest = refs[at:]
    return parts + ([None, rest] if len(rest) == 1 else [rest[0], rest[-4:]])


def grad_down_kernel(ids, *refs, slots):
    left, right, rec, outs = split_refs(refs, (slots, slots))
    step = pl.program_id(0)
    x = jnp.where(step == 0, 1 - ids[3], ids[3])
    total = outer_sum([a[...] for a in left], [b[...] for b in right])
    chips, rows, cols = outs[0].shape[-3:]
    parts = total.shape[1] // cols
    rows = rows // parts
    for z in range(chips):
        for y in range(2):
            at = (2 * z + y) * rows
            for part in range(parts):
                piece = total[at : at + rows, part * cols : (part + 1) * cols]
                put_block(ids, outs, rec, piece, x, jnp.int32(y), z, slice(part * rows, (part + 1) * rows))


def grad_up_kernel(ids, *refs, slots):
    left, first, last, rec, outs = split_refs(refs, (slots, slots, slots))
    z = pl.program_id(0)
    right = [jnp.concatenate([a[...], b[...]], 1) for a, b in zip(first, last)]
    total = outer_sum([a[...] for a in left], right)
    rows, cols = outs[0].shape[-2:]
    for x in range(2):
        for y in range(2):
            piece = total[y * rows : (y + 1) * rows, x * cols : (x + 1) * cols]
            put_block(ids, outs, rec, piece, jnp.int32(x), jnp.int32(y), z, slice(0, rows))


def grad_out_kernel(ids, *refs, slots):
    left, mine, other, rec, outs = split_refs(refs, (slots, slots, slots))
    right = [jnp.concatenate([a[...], b[...]], 1) for a, b in zip(mine, other)]
    total = outer_sum([a[...] for a in left], right)
    chips, rows, cols = outs[0].shape[-3:]
    for near in range(2):
        x = ids[0] if near == 0 else 1 - ids[0]
        for z in range(chips):
            for y in range(2):
                at = (2 * z + y) * rows
                piece = total[at : at + rows, near * cols : (near + 1) * cols]
                put_block(ids, outs, rec, piece, x, jnp.int32(y), z, slice(0, rows))


def grad_qkv_kernel(ids, *refs, slots, steps):
    mine, other, first, last, rec, outs = split_refs(refs, (slots, slots, slots, slots))
    right = [jnp.concatenate([a[...], b[...]], 1) for a, b in zip(first, last)]
    near = outer_sum([a[...] for a in mine], right)
    far = outer_sum([a[...] for a in other], right)
    total = jnp.concatenate([jnp.where(ids[0] == 0, near, far), jnp.where(ids[0] == 0, far, near)])
    chips, rows, cols = outs[0].shape[-3:]
    span = total.shape[0]
    for step in range(steps):

        @pl.when(pl.program_id(0) == step)
        def _(step=step):
            for block in range(2 * chips):
                begin = max(block * rows, step * span)
                end = min((block + 1) * rows, (step + 1) * span)
                if begin >= end:
                    continue
                for x in range(2):
                    piece = total[begin - step * span : end - step * span, x * cols : (x + 1) * cols]
                    put_block(
                        ids, outs, rec, piece, jnp.int32(x), jnp.int32(block % 2), block // 2,
                        slice(begin - block * rows, end - block * rows),
                    )


def grad_call(kernel, ids, grid, groups, shape, rec, flops, joint=None, **kw):
    specs, args = [], []
    for arrays, block, index in groups:
        specs += [pl.BlockSpec(block, index)] * len(arrays)
        args += arrays
    if rec is None:
        out_specs, out_shapes, aliases = whole(shape, pipeline_mode=pl.Buffered(1)), jax.ShapeDtypeStruct(shape, BF), ()
    else:
        specs.append(whole(shape, pipeline_mode=pl.Buffered(1)))
        args.append(rec)
        all_rows, at, arrays = joint
        out_specs = [pl.BlockSpec(shape[1:], lambda *_: (0, at, 0), pipeline_mode=pl.Buffered(1))] * 4
        out_shapes = [jax.ShapeDtypeStruct((shape[1], all_rows, shape[3]), BF)] * 4
        aliases = [(1 + len(args) + i, i) for i in range(len(arrays))]
        specs += [pl.BlockSpec(memory_space=pl.ANY)] * len(arrays)
        args += arrays
    return call(
        functools.partial(kernel, slots=len(groups[0][0]), **kw),
        ids, grid, specs, out_specs, out_shapes, tuple(args), flops=flops, aliases=aliases,
    )


def column_half(ids, rec):
    return 1 - ids[0] if rec is None else ids[0]


def grad_down_part(ids, chips, d_out, active, rec, joint=None):
    rows, width = d_out[0].shape
    ff = active[0].shape[1]
    cols = ff // 4
    parts = 4 * cols // width
    block = lambda i, ids: (0, 2 * jnp.where(i == 0, 1 - ids[3], ids[3]) + column_half(ids, rec))
    groups = [(d_out, (rows, width), lambda i, ids: (0, 0)), (active, (rows, cols), block)]
    shape = (4, chips, parts * width // (2 * chips), cols // parts)
    return grad_call(grad_down_kernel, ids, (2,), groups, shape, rec, COST // 2, joint)


def grad_up_part(ids, chips, d_pre, normed, rec, joint=None):
    rows, width = normed[0].shape
    ff = d_pre[0].shape[1]
    cols = width // 4
    groups = [
        (d_pre, (rows, ff // chips), lambda i, ids: (0, i)),
        (normed, (rows, cols), lambda i, ids: (0, column_half(ids, rec))),
        (normed, (rows, cols), lambda i, ids: (0, 2 + column_half(ids, rec))),
    ]
    return grad_call(grad_up_kernel, ids, (chips,), groups, (4, chips, ff // (2 * chips), cols), rec, COST // 2, joint)


def grad_out_part(ids, chips, d_branch, mine, other, rec, joint=None):
    rows, width = d_branch[0].shape
    cols = width // 4
    half = lambda i, ids: (0, column_half(ids, rec))
    groups = [(d_branch, (rows, width), lambda i, ids: (0, 0)), (mine, (rows, cols), half), (other, (rows, cols), half)]
    return grad_call(grad_out_kernel, ids, (1,), groups, (4, chips, width // (2 * chips), cols), rec, COST // 2, joint)


def grad_qkv_part(ids, chips, mine, other, normed, rec, joint=None):
    rows, width = normed[0].shape
    cols = width // 4
    columns = lambda i, ids: (0, i)
    groups = [
        (mine, (rows, width // 2), columns),
        (other, (rows, width // 2), columns),
        (normed, (rows, cols), lambda i, ids: (0, column_half(ids, rec))),
        (normed, (rows, cols), lambda i, ids: (0, 2 + column_half(ids, rec))),
    ]
    return grad_call(
        grad_qkv_kernel, ids, (3,), groups, (4, chips, 3 * width // (2 * chips), cols), rec, COST // 2, joint, steps=3
    )


def add_kernel(ids, *refs):
    refs[-1][...] = sum(term[...].astype(F32) for term in refs[:-1]).astype(BF)


def add_chips(ids, terms, chips, rows):
    cols = terms[0].shape[1]
    return call(
        add_kernel,
        ids,
        (chips,),
        [pl.BlockSpec((rows, cols), lambda i, ids: (ids[5] ^ i, 0))] * len(terms),
        pl.BlockSpec((None, rows, cols), lambda i, ids: (i, 0, 0)),
        jax.ShapeDtypeStruct((chips, rows, cols), BF),
        tuple(terms),
    )


def finish_kernel(
    ids, d_mine, d_other, mine_near, m0, m1, m2, m3, other_near, o0, o1, o2, o3, block, d_hidden, gain,
    row_grad, sums, sum_mine, sum_other, total_s, mine_far, other_far,
):
    i = pl.program_id(0)
    size = mine_near.shape[0]
    lay_pieces(ids, mine_far, (m0, m1, m2, m3))
    lay_pieces(ids, other_far, (o0, o1, o2, o3))
    own = pl.ds(pl.multiple_of(ids[3] * size, size), size)
    across = pl.ds(pl.multiple_of((1 - ids[3]) * size, size), size)
    term = nt(d_mine[...], mine_near[...]) + nt(d_other[...], other_near[...])
    term_far = nt(d_mine[...], mine_far[...]) + nt(d_other[...], other_far[...])
    sum_mine[...] = jnp.broadcast_to(jnp.sum(d_mine[...].astype(F32), 0, keepdims=True), sum_mine.shape)
    sum_other[...] = jnp.broadcast_to(jnp.sum(d_other[...].astype(F32), 0, keepdims=True), sum_other.shape)

    @pl.when(i == 0)
    def _():
        total_s[:, own] = term
        total_s[:, across] = term_far

    @pl.when(i > 0)
    def _():
        total_s[:, own] += term
        total_s[:, across] += term_far

    @pl.when(i == pl.num_programs(0) - 1)
    def _():
        hat, inverse = row_stats(block[...].astype(F32))
        d_norm = total_s[...]
        weighted = d_norm * gain[0:1]
        first = jnp.mean(weighted, -1, keepdims=True)
        second = jnp.mean(weighted * hat, -1, keepdims=True)
        row_grad[...] = (d_hidden[...].astype(F32) + inverse * (weighted - first - hat * second)).astype(BF)
        sums[...] = jnp.concatenate(
            [jnp.sum(d_norm * hat, 0, keepdims=True), jnp.sum(d_norm, 0, keepdims=True), jnp.zeros((6, d_norm.shape[1]), F32)], 0
        )


def finish(ids, d_mine, d_other, near, far, block, d_hidden, gain):
    rows, width = block.shape
    inner = width // 2
    full = whole((rows, width))
    part = pl.BlockSpec((rows, inner), lambda i, ids: (0, i))
    row = pl.BlockSpec((8, inner), lambda i, ids: (0, i))
    mine = lambda i, ids: (0, 2 * i + ids[0])
    other = lambda i, ids: (0, 2 * i + 1 - ids[0])
    return call(
        finish_kernel,
        ids,
        (3,),
        [
            part, part,
            pl.BlockSpec((inner, inner), mine), *[pl.BlockSpec((inner // 4, inner), mine)] * 4,
            pl.BlockSpec((inner, inner), other), *[pl.BlockSpec((inner // 4, inner), other)] * 4,
            full, full, whole(gain.shape),
        ],
        [full, whole((8, width)), row, row],
        [
            jax.ShapeDtypeStruct((rows, width), BF), jax.ShapeDtypeStruct((8, width), F32),
            jax.ShapeDtypeStruct((8, 3 * inner), F32), jax.ShapeDtypeStruct((8, 3 * inner), F32),
        ],
        (d_mine, d_other, near, *far, near, *far, block, d_hidden, gain),
        scratch=[pltpu.VMEM((rows, width), F32)] + [pltpu.VMEM((inner, inner), BF)] * 2,
        flops=COST,
    )


def swap_axis(x, axis, step=1):
    size = lax.axis_size(axis)
    return lax.ppermute(x, axis, [(i, i ^ step) for i in range(size)])


def swap_across(x):
    return lax.ppermute(x, ("mid", "grp"), [(0, 3), (1, 2), (2, 1), (3, 0)])


def swap_owner(x, chips):
    pairs = []
    for k in range(2 * chips):
        pairs += [(4 * k + 1, 4 * k + 2), (4 * k + 2, 4 * k + 1)]
    return lax.ppermute(x, AXES, pairs)


def after(values, first):
    return lax.optimization_barrier((values, first))[0]


def in_order(index, mine, other, axis=0):
    return jnp.concatenate([jnp.where(index == 0, mine, other), jnp.where(index == 0, other, mine)], axis)


def own_half(x, index, axis=0):
    size = x.shape[axis] // 2
    return lax.dynamic_slice_in_dim(x, index * size, size, axis)


def send_piece(piece):
    return swap_axis(piece, "grp")


def own_piece(shard):
    place = 2 * lax.axis_index("mid") + lax.axis_index("core")
    part = shard.shape[0] // 4
    return lax.dynamic_slice_in_dim(shard, place * part, part, 0)


def as_lines(x, cols):
    parts = []
    for _ in range(2):
        part = lax.reduce_precision(x, 8, 7)
        parts.append(part.astype(BF))
        x = x - part
    return jnp.concatenate(parts).reshape(-1, cols)


def from_lines(lines, shape):
    return lines.astype(F32).reshape((2,) + shape).sum(0)


def send_sums(part):
    return [part[0], swap_axis(part[1], "mid"), swap_axis(part[2], "grp"), swap_across(part[3])]


def send_chips(part):
    return [part[0]] + [swap_axis(part[i], "z", i) for i in range(1, lax.axis_size("z"))]


def settle(total, parts, core):
    mine = jnp.concatenate([lax.dynamic_index_in_dim(part, core, 0, False) for part in parts])
    other = jnp.concatenate([lax.dynamic_index_in_dim(part, 1 - core, 0, False) for part in parts])
    return mine, swap_axis(other, "core")


def body(chips, clips, clip_count, cotangent, norm_gain, bias_d, bias_ff, w_qkv, w_o, w_up, w_down):
    core, x, y, z = (lax.axis_index(axis) for axis in ("core", "grp", "mid", "z"))
    slots, half, width = clips.shape
    inner = width // 2
    ff = w_up.shape[1]
    swap = (core != x).astype(jnp.int32)

    qkv_piece = own_piece(w_qkv)
    small = jnp.concatenate([norm_gain.reshape(-1), bias_d.reshape(-1), bias_ff]).reshape(-1, 128)
    qkv_0 = send_piece(qkv_piece)
    got_small = swap_axis(after(small, qkv_piece), "grp")
    got_first = swap_owner(after(clips[:1], qkv_piece), chips)
    other_count = swap_axis(clip_count, "core")
    qkv_1 = swap_axis(qkv_0, "mid")
    qkv_2 = swap_axis(qkv_0, "core")
    rest = after(clips[1:], qkv_0)
    got_rest = swap_owner(rest, chips)
    piece = own_piece(w_up).reshape(-1, ff // width, width).transpose(1, 0, 2).reshape(-1, width)
    piece = jnp.concatenate([piece, own_piece(w_o)])
    down_piece = own_piece(w_down)
    qkv_3 = swap_axis(qkv_1, "core")
    qkv_far = (qkv_0, qkv_1, qkv_2, qkv_3)
    piece, down_piece = after((piece, down_piece), qkv_1)
    far_0 = send_piece(piece)
    down_0 = send_piece(down_piece)

    pair = in_order(x, small[None], got_small[None]).reshape(2, -1).astype(F32)
    gains = pair[:, : 2 * inner].reshape(2, 2, inner).transpose(1, 0, 2).reshape(2, width)
    biases = pair[:, 2 * inner : 8 * inner].reshape(2, 6, inner).transpose(1, 0, 2).reshape(6, width)
    bias_hidden = pair[:, 8 * inner :].reshape(1, -1)
    count = jnp.where(swap == 1, other_count, clip_count)[0]
    qkv_bias = jnp.concatenate([biases[1], jnp.zeros_like(biases[1]), biases[2]])[None]
    ids = [jnp.stack([core, swap, (count > s).astype(jnp.int32), x, y, z]).astype(jnp.int32) for s in range(slots)]

    cot_first, cot_others = after((cotangent[:1], cotangent[1:]), qkv_0)
    got_first = after(got_first, (rest, piece, down_piece, cot_first, cot_others))
    blocks, normed, saved, ctx_mine, ctx_other = [], [], [], [], []
    for s in range(slots):
        got, slot = (got_first, 0) if s == 0 else (got_rest, s - 1)
        block, norm, other = project_other(ids[s], clips, s, got, slot, gains[0:1], biases[0:1], w_qkv, qkv_far, qkv_bias)
        received = swap_axis(other, "core")
        mine = project_mine(ids[s], norm, w_qkv, qkv_far, qkv_bias)
        here, there, r_here, r_there, weights, weights_rem = attend(mine, received)
        saved.append((mine, received, here, there, r_here, r_there, weights, weights_rem))
        ctx_mine.append(here)
        ctx_other.append(swap_axis(there, "core"))
        blocks.append(block)
        normed.append(norm)
        if s == 0:
            down_0 = after(down_0, here)
            down_1 = swap_axis(down_0, "mid")
            down_2 = swap_axis(down_0, "core")
            got_rest = after(got_rest, (here, down_0))
        elif s == 1:
            down_1, far_0 = after((down_1, far_0), here)
            down_3 = swap_axis(down_1, "core")
            far_1 = swap_axis(far_0, "mid")
            far_2 = swap_axis(far_0, "core")
            got_rest = after(got_rest, (here, down_1, far_0))
        elif s == 2:
            far_1 = after(far_1, here)
            far_3 = swap_axis(far_1, "core")
    far = (far_0, far_1, far_2, far_3)
    far_down = (down_0, down_1, down_2, down_3)

    others = swap_owner(after(cot_others, here), chips)
    got_cot = [(swap_owner(cot_first, chips), 0)] + [(others, s - 1) for s in range(1, slots)]
    fed, got_result = [], []
    before = ()
    for s in range(slots):
        if s == 2:
            got_cot[s] = (after(others, got_result[0]), s - 1)
        fed.append(
            feed(
                ids[s], s, slots, blocks[s], ctx_mine[s], ctx_other[s], cotangent, *got_cot[s], w_o, w_up, w_down, far, far_down,
                gains, biases, bias_hidden, before,
            )
        )
        before = (fed[-1][7],)
        got_result.append(swap_owner(fed[-1][4], chips))
    active, d_pre, normed2, d_out, result, d_branch, d_ctx_mine, d_ctx_other, sums2, sums_hidden = map(list, zip(*fed))
    d_ctx_got = swap_axis(d_ctx_other[-1], "core")

    sent_down = grad_down_part(ids[0], chips, after(d_out, got_result[1]), active, None)
    sent_up = grad_up_part(ids[0], chips, d_pre, normed2, None)
    sent_out = grad_out_part(ids[0], chips, d_branch, ctx_mine, ctx_other, None)
    rows_down, rows_up, rows_out = (part.shape[2] for part in (sent_down, sent_up, sent_out))
    rows = rows_down + rows_up + rows_out
    joint = grad_down_part(ids[0], chips, d_out, active, swap_axis(sent_down, "core"), (rows, 0, []))
    joint = grad_up_part(
        ids[0], chips, d_pre, normed2, swap_axis(sent_up, "core"),
        (rows, rows_down // rows_up, joint),
    )
    joint = grad_out_part(
        ids[0], chips, d_branch, ctx_mine, ctx_other, swap_axis(sent_out, "core"),
        (rows, (rows_down + rows_up) // rows_out, joint),
    )
    cols = joint[0].shape[-1]
    sums = send_sums([part.reshape(-1, cols) for part in joint])
    early = jnp.concatenate([sum(sums2)[:4], sum(sums_hidden)[0].reshape(-1, width)])

    got_rows = []
    d_mine, d_other, row_grads, sums1, sums_mine, sums_other = [], [], [], [], [], []

    def complete(s, first):
        row_grad, sum1, sum_mine, sum_other = finish(
            ids[s], d_mine[s], after(d_other[s], first), w_qkv, qkv_far, blocks[s], d_branch[s], gains
        )
        row_grads.append(row_grad)
        sums1.append(sum1)
        sums_mine.append(sum_mine[0])
        sums_other.append(sum_other[0])
        return row_grad

    gate = joint
    for s in range(slots):
        mine, received, here, there, r_here, r_there, weights, weights_rem = saved[s]
        d_here, d_there = attend_back(
            s, mine, received, after(d_ctx_mine[s], gate), d_ctx_got, here, there, r_here, r_there, weights, weights_rem
        )
        d_mine.append(d_here)
        d_other.append(swap_axis(d_there, "core"))
        gate = (d_here,)
        if s == 0:
            sums[3] = after(sums[3], d_here)
            gate = (d_here, sums[3])
        elif s == 1:
            sums = add_chips(ids[0], after(sums, d_here), chips, rows)
            gate = sums
            terms = send_chips(sums)
            gate = (gate, [sums[i] for i in range(chips)])
        if s == 2:
            gate = complete(0, (d_here, terms, got_result[2]))
    got_rows.append(swap_owner(row_grads[0], chips))
    sent_qkv = grad_qkv_part(ids[0], chips, d_mine, after(d_other, gate), normed, None)
    gate = complete(1, sent_qkv)
    got_rows.append(swap_owner(row_grads[1], chips))
    part_qkv = grad_qkv_part(
        ids[0], chips, d_mine, d_other, normed, after(swap_axis(sent_qkv, "core"), (gate, got_rows[0])),
        (sent_qkv.shape[2], 0, []),
    )
    qkv_rows = part_qkv[0].shape[1]
    qkv_terms = send_sums([part.reshape(-1, cols) for part in part_qkv])
    complete(2, (part_qkv, got_rows[1]))
    total1 = sum(sums1)
    total_mine, total_other = sum(sums_mine), sum(sums_other)
    grad_bq = in_order(core, total_mine[:inner], total_other[:inner])
    grad_bv = in_order(core, total_mine[2 * inner :], total_other[2 * inner :])
    lines = jnp.concatenate(
        [jnp.stack([total1[0], early[0], total1[1], grad_bq, grad_bv, early[2], early[1], early[3]]), early[4:]]
    )
    lines = lines + swap_axis(lines, "core")
    shape = lines.shape
    lines = sum(send_sums([lines] * 4))
    got_rows.append(swap_owner(after(row_grads[2], lines), chips))
    sums = add_chips(ids[0], qkv_terms, chips, qkv_rows)
    under = as_lines(lines, cols)
    sends = [jnp.concatenate([sums[i], under]) for i in range(chips)]
    qkv_terms = send_chips(sends)
    total = sum(term.astype(F32) for term in after(terms, sends))
    chunks = rows_down // rows_out
    down = total[:rows_down].reshape(chunks, 2, -1, cols).transpose(1, 0, 2, 3).reshape(2, -1, cols)
    up = total[rows_down : rows_down + rows_up].reshape(2, -1, cols)
    out = total[rows_down + rows_up :].reshape(2, -1, cols)
    mine, other = settle(total, (down, up, out), core)
    whole_rows = in_order(core, mine, other, 1)
    n_down, n_up = rows_down // 2, rows_up // 2
    own_down = in_order(core, mine[:n_down].reshape(chunks, -1, cols), other[:n_down].reshape(chunks, -1, cols))
    grad_down = own_down.transpose(0, 2, 1).reshape(2 * chunks * cols, -1)
    grad_up = whole_rows[n_down : n_down + n_up].T
    grad_out = whole_rows[n_down + n_up :].T

    outs = jnp.stack([jnp.where(swap == 1, after(got_result[s], sends), result[s]) for s in range(slots)])
    input_grad = jnp.stack([jnp.where(swap == 1, after(got_rows[s], sends), row_grads[s]) for s in range(slots)]).astype(F32)
    qkv_terms = after(qkv_terms, input_grad)
    lines = sum(from_lines(term[qkv_rows:], shape) for term in qkv_terms)
    columns = own_half(lines[:8], x, 1)
    hidden_part = own_half(lines[8:], x).reshape(-1)
    total = sum(term[:qkv_rows].astype(F32) for term in qkv_terms)
    mine, other = settle(total, (total.reshape(2, -1, cols),), core)
    grad_qkv = in_order(core, mine, other, 1).T
    return (outs, input_grad, columns[:2], columns[2:], hidden_part, grad_qkv, grad_out, grad_up, grad_down)


def solution(mesh):
    in_specs = (
        P("rep", "grp", None),
        P("rep"),
        P("rep", "grp", None),
        P(None, "grp"),
        P(None, "grp"),
        P("grp"),
        P("grp", None),
        P("grp", None),
        P("grp", None),
        P("grp", None),
    )
    out_specs = (
        P("rep", "grp", None),
        P("rep", "grp", None),
        P(None, "grp"),
        P(None, "grp"),
        P("grp"),
        P("grp", "rep"),
        P("grp", "rep"),
        P("grp", "rep"),
        P("grp", "rep"),
    )
    if mesh.shape["grp"] != 2 or mesh.shape["rep"] != 16:
        return jax.shard_map(plain_body, mesh=mesh, in_specs=in_specs, out_specs=out_specs, check_vma=False)
    chips = mesh.shape["rep"] // 4
    split = Mesh(mesh.devices.reshape(chips, 2, 2, 2), AXES)
    rep = lambda spec: P(*[AXES[:3] if axis == "rep" else axis for axis in spec])
    return jax.shard_map(
        functools.partial(body, chips),
        mesh=split,
        in_specs=tuple(rep(spec) for spec in in_specs),
        out_specs=tuple(rep(spec) for spec in out_specs),
        check_vma=False,
    )
```

```python
import functools

import jax
import jax.numpy as jnp
from jax import lax
from jax.experimental import pallas as pl
from jax.experimental.pallas import tpu as pltpu
from jax.sharding import Mesh
from jax.sharding import PartitionSpec as P

H = 16
HD = 64
EPSILON = 1e-06

F32 = jnp.float32
BF = jnp.bfloat16
LOG2E = 1.4426950408889634
SCALE = HD ** -0.5
AXES = ("z", "mid", "core", "grp")
BQ = 512
TK = 224
COST = 5 * 10**10
LIMIT = 56.0


def dot(a, b, dims):
    return lax.dot_general(a, b, (dims, ((), ())), preferred_element_type=F32)


def nt(a, b):
    return dot(a, b, ((1,), (1,)))


def nn(a, b):
    return dot(a, b, ((1,), (0,)))


def tn(a, b):
    return dot(a, b, ((0,), (0,)))


def pair_mask(a):
    lane = lax.broadcasted_iota(jnp.int32, (1, 128), 1)
    return (lane < HD) if a == 0 else (lane >= HD)

def norm_peak(x, np_):
    inner = x.shape[1]
    r = lax.broadcasted_iota(jnp.int32, (inner, 128), 0)
    c = lax.broadcasted_iota(jnp.int32, (inner, 128), 1)
    ones = jnp.where(r // HD == c, 1.0, 0.0).astype(BF)
    xf = x.astype(F32)
    return jnp.max(nn((xf * xf).astype(BF), ones), axis=0, keepdims=True)

def attend_kernel(own, rec, oo, orr, ro, rr, p_out, prem_out, q_s, k_s, vt_s, o_s, r_s, fast, *, nb, np_, rem):
    half = own.shape[0]
    inner = own.shape[1] // 3
    full = 2 * half
    t = pl.program_id(0)
    last = np_ * nb

    @pl.when(t == 0)
    def _():
        q_s[:half] = own[:, :inner]
        q_s[half:] = rec[:, :inner]
        k_s[:half] = own[:, inner:2 * inner]
        k_s[half:] = rec[:, inner:2 * inner]
        row = lax.broadcasted_iota(jnp.int32, (128, 1), 0)
        for p in range(np_):
            cols = slice(2 * inner + p * 128, 2 * inner + (p + 1) * 128)
            vt = jnp.concatenate([own[:, cols], rec[:, cols]], axis=0).T
            for a in range(2):
                mine = (row < HD) if a == 0 else (row >= HD)
                vt_s[2 * p + a] = jnp.where(mine, vt, 1.0).astype(BF)
        peak = jnp.max(norm_peak(q_s[...], np_) * norm_peak(k_s[...], np_))
        fast[0] = (peak * (1.1 * SCALE * SCALE) < LIMIT * LIMIT).astype(jnp.int32)

    def store(o, rows, cols):
        oa, ob = o
        ra = 1.0 / oa[HD:]
        rb = 1.0 / ob[:HD]
        o_s[rows, cols] = jnp.concatenate([oa[:HD] * ra, ob[HD:] * rb], axis=0).T.astype(BF)
        r_s[rows, cols] = jnp.concatenate([ra, rb], axis=0).T

    def main(quick):
        p = t // nb
        b = t % nb
        rows = pl.ds(pl.multiple_of(b * BQ, BQ), BQ)
        cols = pl.ds(pl.multiple_of(p * 128, 128), 128)
        q = q_s[rows, cols]
        def weights(a):
            qa = jnp.where(pair_mask(a), q, 0.0).astype(BF)
            if quick:
                for j in range(full // TK):
                    tile = slice(j * TK, (j + 1) * TK)
                    s = nt(k_s[tile, cols], qa)
                    p_out[0, a, tile] = jnp.exp2(s * (LOG2E * SCALE)).astype(BF)
            else:
                s = nt(k_s[:, cols], qa)
                m = jnp.max(s, axis=0, keepdims=True)
                p_out[0, a] = jnp.exp2((s - m) * (LOG2E * SCALE)).astype(BF)
        weights(0)
        weights(1)
        oa = nn(vt_s[2 * p], p_out[0, 0])
        ob = nn(vt_s[2 * p + 1], p_out[0, 1])
        store((oa, ob), rows, cols)

    @pl.when((t < last) & (fast[0] == 1))
    def _():
        main(True)

    @pl.when((t < last) & (fast[0] == 0))
    def _():
        main(False)

    @pl.when(t == last)
    def _():
        if rem:
            lane = lax.broadcasted_iota(jnp.int32, (1, 256), 1)
            for u in range(np_ // 2):
                q = q_s[nb * BQ:, u * 256:(u + 1) * 256]
                qd = jnp.concatenate([jnp.where(lane // HD == h, q, 0.0).astype(BF) for h in range(4)], axis=0)
                s = nt(k_s[:, u * 256:(u + 1) * 256], qd)
                m = jnp.max(s, axis=0, keepdims=True)
                prem_out[u] = jnp.exp2((s - m) * (LOG2E * SCALE)).astype(BF)
                for v in range(2):
                    oa = nn(vt_s[4 * u + 2 * v], prem_out[u])
                    ob = nn(vt_s[4 * u + 2 * v + 1], prem_out[u])
                    ra = 1.0 / oa[HD:]
                    rb = 1.0 / ob[:HD]
                    x = jnp.concatenate([oa[:HD] * ra, ob[HD:] * rb], axis=0).T
                    r = jnp.concatenate([ra, rb], axis=0).T
                    ha, hb = 2 * v, 2 * v + 1
                    pick = lambda y: jnp.where(pair_mask(0), y[ha * rem:(ha + 1) * rem], y[hb * rem:(hb + 1) * rem])
                    cols = slice((2 * u + v) * 128, (2 * u + v + 1) * 128)
                    o_s[nb * BQ:, cols] = pick(x).astype(BF)
                    r_s[nb * BQ:, cols] = pick(r)
        oo[...] = o_s[:half]
        orr[...] = o_s[half:]
        ro[...] = r_s[:half]
        rr[...] = r_s[half:]

def attend(own, rec):
    half, w = own.shape
    inner = w // 3
    np_ = inner // 128
    full = 2 * half
    nb = full // BQ
    rem = full - nb * BQ
    last = np_ * nb
    whole = lambda shape: pl.BlockSpec(shape, lambda t: (0,) * len(shape))
    return pl.pallas_call(
        functools.partial(attend_kernel, nb=nb, np_=np_, rem=rem),
        grid=(last + 1,),
        in_specs=[whole((half, w))] * 2,
        out_specs=[whole((half, inner))] * 4 + [pl.BlockSpec((1, 2, full, BQ), lambda t: (jnp.minimum(t, last - 1), 0, 0, 0)), whole((np_ // 2, full, 4 * rem))],
        out_shape=[jax.ShapeDtypeStruct((half, inner), BF)] * 2 + [jax.ShapeDtypeStruct((half, inner), F32)] * 2
        + [jax.ShapeDtypeStruct((last, 2, full, BQ), BF), jax.ShapeDtypeStruct((np_ // 2, full, 4 * rem), BF)],
        scratch_shapes=[
            pltpu.VMEM((full, inner), BF), pltpu.VMEM((full, inner), BF), pltpu.VMEM((2 * np_, 128, full), BF),
            pltpu.VMEM((full, inner), BF), pltpu.VMEM((full, inner), F32), pltpu.SMEM((1,), jnp.int32)],
        cost_estimate=pl.CostEstimate(flops=0, bytes_accessed=0, transcendentals=0),
        compiler_params=pltpu.CompilerParams(vmem_limit_bytes=60 * 1024 * 1024),
    )(own, rec)


def attend_back_kernel(own, rec, do_o, do_r, o_o, o_r, r_o, r_r, e, erem, out_o, out_r,
               q_s, k_s, v_s, kt_s, do_s, pr_s, ds_s, dq_s, dk_s, dv_s, *, nb, np_, rem):
    half = own.shape[0]
    inner = own.shape[1] // 3
    full = 2 * half
    t = pl.program_id(0)
    last = np_ * nb

    @pl.when(t == 0)
    def _():
        for lo, src, d, o, r in ((0, own, do_o, o_o, r_o), (half, rec, do_r, o_r, r_r)):
            rows = slice(lo, lo + half)
            q_s[rows] = src[:, :inner]
            k_s[rows] = src[:, inner:2 * inner]
            v_s[rows] = src[:, 2 * inner:]
            dn = (d[...].astype(F32) * r[...]).astype(BF)
            do_s[rows] = dn
            pr_s[rows] = dn.astype(F32) * o[...].astype(F32)
        for p in range(np_):
            kt_s[p * 128:(p + 1) * 128] = k_s[:, p * 128:(p + 1) * 128].T
        dk_s[...] = jnp.zeros_like(dk_s)
        dv_s[...] = jnp.zeros_like(dv_s)

    @pl.when(t < last)
    def _():
        p = t // nb
        b = t % nb
        rows = pl.ds(pl.multiple_of(b * BQ, BQ), BQ)
        cols = pl.ds(pl.multiple_of(p * 128, 128), 128)
        q = q_s[rows, cols]
        dn = do_s[rows, cols]
        prod = pr_s[rows, cols].T
        qs, dns = [], []
        for a in range(2):
            qs.append(jnp.where(pair_mask(a), q, 0.0).astype(BF))
            dns.append(jnp.where(pair_mask(a), dn, 0.0).astype(BF))
        for a in range(2):
            delta = jnp.sum(prod[a * HD:(a + 1) * HD], axis=0, keepdims=True)
            for j in range(full // TK):
                tile = slice(j * TK, (j + 1) * TK)
                dp = nt(v_s[tile, cols], dns[a])
                ds_s[a, tile] = (e[0, a, tile].astype(F32) * (dp - delta)).astype(BF)
        for j in range(full // TK):
            tile = slice(j * TK, (j + 1) * TK)
            dv_s[tile, cols] += nn(e[0, 0, tile], dns[0]) + nn(e[0, 1, tile], dns[1])
        dqt = []
        for a in range(2):
            dqt.append(nn(kt_s[pl.ds(pl.multiple_of(p * 128, 128), 128)], ds_s[a])[a * HD:(a + 1) * HD])
        dq_s[rows, cols] = (jnp.concatenate(dqt, axis=0) * SCALE).T.astype(BF)
        for j in range(full // TK):
            tile = slice(j * TK, (j + 1) * TK)
            dk_s[tile, cols] += nn(ds_s[0, tile], qs[0]) + nn(ds_s[1, tile], qs[1])

    @pl.when(t == last)
    def _():
        if rem:
            lane = lax.broadcasted_iota(jnp.int32, (1, 256), 1)
            def spread(x):
                return jnp.concatenate([jnp.where(lane // HD == h, x, 0.0).astype(x.dtype) for h in range(4)], axis=0)
            for u in range(np_ // 2):
                cols = slice(u * 256, (u + 1) * 256)
                qd = spread(q_s[nb * BQ:, cols])
                dd = spread(do_s[nb * BQ:, cols])
                delta = jnp.sum(spread(pr_s[nb * BQ:, cols]).T, axis=0, keepdims=True)
                dp = nt(v_s[:, cols], dd)
                ds = (erem[u].astype(F32) * (dp - delta)).astype(BF)
                dv_s[:, cols] += nn(erem[u], dd)
                dk_s[:, cols] += nn(ds, qd)
                x = nn(kt_s[cols], ds).T * SCALE
                dq = x[:rem]
                for h in range(1, 4):
                    dq = jnp.where(lane // HD == h, x[h * rem:(h + 1) * rem], dq)
                dq_s[nb * BQ:, cols] = dq.astype(BF)
        for lo, dst in ((0, out_o), (half, out_r)):
            rows = slice(lo, lo + half)
            dst[:, :inner] = dq_s[rows]
            dst[:, inner:2 * inner] = (dk_s[rows] * SCALE).astype(BF)
            dst[:, 2 * inner:] = dv_s[rows].astype(BF)

def attend_back(slot, own, rec, do_o, do_r, o_o, o_r, r_o, r_r, e, erem):
    half, w = own.shape
    inner = w // 3
    np_ = inner // 128
    full = 2 * half
    nb = full // BQ
    rem = full - nb * BQ
    last = np_ * nb
    whole = lambda shape, **kw: pl.BlockSpec(shape, lambda t: (0,) * len(shape), **kw)
    one = dict(pipeline_mode=pl.Buffered(1))
    return pl.pallas_call(
        functools.partial(attend_back_kernel, nb=nb, np_=np_, rem=rem),
        grid=(last + 1,),
        in_specs=[whole((half, w), **one)] * 2
        + [whole((half, inner), **one), pl.BlockSpec((None, half, inner), lambda t: (slot, 0, 0), **one)]
        + [whole((half, inner), **one)] * 4
        + [pl.BlockSpec((1, 2, full, BQ), lambda t: (jnp.minimum(t, last - 1), 0, 0, 0)), whole(erem.shape, **one)],
        out_specs=[whole((half, w), **one)] * 2,
        out_shape=[jax.ShapeDtypeStruct((half, w), BF)] * 2,
        scratch_shapes=[
            pltpu.VMEM((full, inner), BF), pltpu.VMEM((full, inner), BF), pltpu.VMEM((full, inner), BF),
            pltpu.VMEM((inner, full), BF), pltpu.VMEM((full, inner), BF), pltpu.VMEM((full, inner), F32),
            pltpu.VMEM((2, full, BQ), BF), pltpu.VMEM((full, inner), BF),
            pltpu.VMEM((full, inner), F32), pltpu.VMEM((full, inner), F32)],
        cost_estimate=pl.CostEstimate(flops=COST, bytes_accessed=0, transcendentals=0),
        compiler_params=pltpu.CompilerParams(vmem_limit_bytes=62 * 1024 * 1024),
    )(own, rec, do_o, do_r, o_o, o_r, r_o, r_r, e, erem)


def matmul(left, right):
    return jnp.dot(left, right, preferred_element_type=jnp.float32)


def layer_norm(values, gain, shift):
    centred = values - jnp.mean(values, -1, keepdims=True)
    spread = jnp.mean(centred * centred, -1, keepdims=True)
    inverse = lax.rsqrt(spread + EPSILON)
    scaled = centred * inverse
    return (scaled, inverse, scaled * gain + shift)


def norm_back(scaled, inverse, gain, incoming):
    weighted = incoming * gain
    first = jnp.mean(weighted, -1, keepdims=True)
    second = jnp.mean(weighted * scaled, -1, keepdims=True)
    return inverse * (weighted - first - scaled * second)


def fetch_weights(shards):
    return (
        lax.all_gather(shards[0], "grp", axis=0, tiled=True),
        lax.all_gather(shards[1], "grp", axis=0, tiled=True),
        lax.all_gather(shards[2], "grp", axis=0, tiled=True),
        lax.all_gather(shards[3], "grp", axis=0, tiled=True),
        lax.all_gather(shards[4], "grp", axis=1, tiled=True),
        lax.all_gather(shards[5], "grp", axis=1, tiled=True),
        lax.all_gather(shards[6], "grp", axis=0, tiled=True),
    )


def shard_grads(weight_grads):
    return (
        lax.psum_scatter(weight_grads[0], "grp", scatter_dimension=1, tiled=True),
        lax.psum_scatter(weight_grads[1], "grp", scatter_dimension=1, tiled=True),
        lax.psum_scatter(weight_grads[2], "grp", scatter_dimension=0, tiled=True),
        lax.psum_scatter(weight_grads[3], "grp", scatter_dimension=0, tiled=True),
        lax.psum_scatter(weight_grads[4], "grp", scatter_dimension=0, tiled=True),
        lax.psum_scatter(weight_grads[5], "grp", scatter_dimension=0, tiled=True),
        lax.psum_scatter(weight_grads[6], "grp", scatter_dimension=0, tiled=True),
    )


def raw_scores(query, keys):
    rows = query.shape[0]
    length = keys.shape[0]
    return jnp.einsum(
        "qhd,khd->hqk",
        query.reshape(rows, H, HD),
        keys.reshape(length, H, HD),
        preferred_element_type=jnp.float32,
    ) * HD ** (-0.5)


def score_probs(query, keys):
    return jax.nn.softmax(raw_scores(query, keys), axis=-1)


def forward_pass(row_block, gathered):
    qkv_weight, out_weight, up_weight, down_weight, gains, biases, hidden_bias = gathered
    gain_f = gains.astype(jnp.float32)
    bias_f = biases.astype(jnp.float32)
    rows = row_block.shape[0]
    model_width = row_block.shape[1]
    inputs = row_block.astype(jnp.float32)
    scaled1, inverse1, normed = layer_norm(inputs, gain_f[0], bias_f[0])
    normed = normed.astype(jnp.bfloat16)
    shift = jnp.concatenate([bias_f[1], jnp.zeros_like(bias_f[1]), bias_f[2]])
    qkv = (matmul(normed, qkv_weight) + shift).astype(jnp.bfloat16)
    query = qkv[:, :model_width]
    key_part = qkv[:, model_width : 2 * model_width]
    value_part = qkv[:, 2 * model_width :]
    keys, values = (
        lax.all_gather(key_part, "grp", axis=0, tiled=True),
        lax.all_gather(value_part, "grp", axis=0, tiled=True),
    )
    length = keys.shape[0]
    probs = score_probs(query, keys)
    context = (
        jnp.einsum(
            "hqk,khd->qhd",
            probs.astype(jnp.bfloat16),
            values.reshape(length, H, HD),
            preferred_element_type=jnp.float32,
        )
        .reshape(rows, model_width)
        .astype(jnp.bfloat16)
    )
    hidden = inputs + matmul(context, out_weight) + bias_f[3]
    scaled2, inverse2, normed2 = layer_norm(hidden, gain_f[1], bias_f[4])
    normed2 = normed2.astype(jnp.bfloat16)
    pre = matmul(normed2, up_weight) + hidden_bias.astype(jnp.float32)
    active = jax.nn.gelu(pre, approximate=False).astype(jnp.bfloat16)
    result = hidden + matmul(active, down_weight) + bias_f[5]
    saved = (
        scaled1,
        inverse1,
        normed,
        query,
        keys,
        values,
        context,
        scaled2,
        inverse2,
        normed2,
        pre,
        active,
    )
    return (result, saved)


def backward_pass(incoming, weight, saved, gathered):
    qkv_weight, out_weight, up_weight, down_weight, gains, biases, hidden_bias = gathered
    gain_f = gains.astype(jnp.float32)
    (
        scaled1,
        inverse1,
        normed,
        query,
        keys,
        values,
        context,
        scaled2,
        inverse2,
        normed2,
        pre,
        active,
    ) = saved
    rows = query.shape[0]
    model_width = query.shape[1]
    length = keys.shape[0]
    d_out = incoming * weight.astype(jnp.bfloat16)
    d_out_f = d_out.astype(jnp.float32)
    grad_down = jnp.einsum("rf,rd->fd", active, d_out, preferred_element_type=jnp.float32)
    grad_b2 = jnp.sum(d_out_f, 0)
    d_act = jnp.einsum("rd,fd->rf", d_out, down_weight, preferred_element_type=jnp.float32)
    unused, gelu_pull = jax.vjp(lambda inputs: jax.nn.gelu(inputs, approximate=False), pre)
    d_pre = gelu_pull(d_act)[0].astype(jnp.bfloat16)
    grad_up = jnp.einsum("rd,rf->df", normed2, d_pre, preferred_element_type=jnp.float32)
    grad_hidden_bias = jnp.sum(d_pre.astype(jnp.float32), 0)
    d_norm2 = jnp.einsum("rf,df->rd", d_pre, up_weight, preferred_element_type=jnp.float32)
    d_hidden = d_out_f + norm_back(scaled2, inverse2, gain_f[1], d_norm2)
    grad_g2 = jnp.sum(d_norm2 * scaled2, 0)
    grad_beta2 = jnp.sum(d_norm2, 0)
    d_branch = d_hidden.astype(jnp.bfloat16)
    grad_out = jnp.einsum("rd,re->de", context, d_branch, preferred_element_type=jnp.float32)
    grad_bo = jnp.sum(d_branch.astype(jnp.float32), 0)
    d_context = jnp.einsum(
        "re,de->rd", d_branch, out_weight, preferred_element_type=jnp.float32
    ).astype(jnp.bfloat16)
    scores = raw_scores(query, keys)
    probs = jax.nn.softmax(scores, axis=-1)
    context_heads = d_context.reshape(rows, H, HD)
    d_probs = jnp.einsum(
        "qhd,khd->hqk",
        context_heads,
        values.reshape(length, H, HD),
        preferred_element_type=jnp.float32,
    )
    delta = jnp.sum(probs * d_probs, -1)
    d_scores = (probs * (d_probs - delta[..., None])).astype(jnp.bfloat16)
    d_query = (
        jnp.einsum(
            "hqk,khd->qhd",
            d_scores,
            keys.reshape(length, H, HD),
            preferred_element_type=jnp.float32,
        )
        * HD ** (-0.5)
    ).reshape(rows, model_width)
    d_value = jnp.einsum(
        "hqk,qhd->khd",
        probs.astype(jnp.bfloat16),
        context_heads,
        preferred_element_type=jnp.float32,
    ).reshape(length, model_width)
    d_key = (
        jnp.einsum(
            "hqk,qhd->khd", d_scores, query.reshape(rows, H, HD), preferred_element_type=jnp.float32
        )
        * HD ** (-0.5)
    ).reshape(length, model_width)
    d_key, d_value = (
        lax.psum_scatter(d_key, "grp", scatter_dimension=0, tiled=True),
        lax.psum_scatter(d_value, "grp", scatter_dimension=0, tiled=True),
    )
    d_qkv = jnp.concatenate(
        [d_query.astype(jnp.bfloat16), d_key.astype(jnp.bfloat16), d_value.astype(jnp.bfloat16)], 1
    )
    grad_qkv = jnp.einsum("rd,re->de", normed, d_qkv, preferred_element_type=jnp.float32)
    d_qkv_f = d_qkv.astype(jnp.float32)
    grad_bq = jnp.sum(d_qkv_f[:, :model_width], 0)
    grad_bv = jnp.sum(d_qkv_f[:, 2 * model_width :], 0)
    d_norm1 = jnp.einsum("re,de->rd", d_qkv, qkv_weight, preferred_element_type=jnp.float32)
    row_grad = d_hidden + norm_back(scaled1, inverse1, gain_f[0], d_norm1)
    grad_g1 = jnp.sum(d_norm1 * scaled1, 0)
    grad_beta1 = jnp.sum(d_norm1, 0)
    grad_gains = jnp.stack([grad_g1, grad_g2])
    grad_biases = jnp.stack([grad_beta1, grad_bq, grad_bv, grad_bo, grad_beta2, grad_b2])
    weight_grads = (
        grad_gains,
        grad_biases,
        grad_hidden_bias,
        grad_qkv,
        grad_out,
        grad_up,
        grad_down,
    )
    return (row_grad, weight_grads)


def plain_body(clips, clip_count, cotangent, norm_gain, bias_d, bias_ff, w_qkv, w_o, w_up, w_down):
    shards = (w_qkv, w_o, w_up, w_down, norm_gain, bias_d, bias_ff)
    number = clips.shape[0]
    outputs = []
    records = []
    actives = []
    for slot_index in range(number):
        gathered = fetch_weights(shards)
        active = (clip_count[0] > slot_index).astype(jnp.float32)
        result, saved = forward_pass(clips[slot_index], gathered)
        outputs.append((result * active).astype(jnp.bfloat16))
        records.append(saved)
        actives.append(active)
    row_grads = [None] * number
    totals = None
    for slot_index in reversed(range(number)):
        gathered = fetch_weights(shards)
        row_grad, weight_grads = backward_pass(
            cotangent[slot_index], actives[slot_index], records[slot_index], gathered
        )
        row_grads[slot_index] = row_grad
        totals = (
            weight_grads
            if totals is None
            else jax.tree.map(lambda left, right: left + right, totals, weight_grads)
        )
    totals = shard_grads(totals)
    small_sums = lax.psum((totals[0], totals[1], totals[2]), "rep")
    matrix_sums = (
        lax.psum_scatter(totals[3], "rep", scatter_dimension=1, tiled=True),
        lax.psum_scatter(totals[4], "rep", scatter_dimension=1, tiled=True),
        lax.psum_scatter(totals[5], "rep", scatter_dimension=1, tiled=True),
        lax.psum_scatter(totals[6], "rep", scatter_dimension=1, tiled=True),
    )
    return (jnp.stack(outputs), jnp.stack(row_grads)) + tuple(small_sums) + tuple(matrix_sums)


def row_stats(values):
    centred = values - jnp.mean(values, -1, keepdims=True)
    inverse = lax.rsqrt(jnp.mean(centred * centred, -1, keepdims=True) + EPSILON)
    return centred * inverse, inverse


def whole(shape, **kw):
    return pl.BlockSpec(shape, lambda *_: (0,) * len(shape), **kw)


def call(kernel, ids, grid, in_specs, out_specs, out_shape, args, scratch=(), flops=0, limit=60, aliases=()):
    return pl.pallas_call(
        kernel,
        grid_spec=pltpu.PrefetchScalarGridSpec(
            num_scalar_prefetch=1, grid=grid, in_specs=in_specs, out_specs=out_specs, scratch_shapes=list(scratch)
        ),
        out_shape=out_shape,
        cost_estimate=pl.CostEstimate(flops=int(flops), bytes_accessed=0, transcendentals=0),
        input_output_aliases=dict(aliases),
        compiler_params=pltpu.CompilerParams(vmem_limit_bytes=limit * 1024 * 1024),
    )(ids, *args)


def slot_of(shape, s):
    return pl.BlockSpec((None,) + shape, lambda *_: (s,) + (0,) * len(shape))


def piece_places(ids):
    y, core = ids[4], ids[0]
    return (2 * y + core, 2 * (1 - y) + core, 2 * y + 1 - core, 2 * (1 - y) + 1 - core)


def lay_pieces(ids, target, pieces):
    size = target.shape[0] // len(pieces)
    for piece, place in zip(pieces, piece_places(ids)):
        target[pl.ds(pl.multiple_of(place * size, size), size)] = piece[...]


def by_rows(ids, x, near, far):
    size = near.shape[0]
    own = pl.ds(pl.multiple_of(ids[3] * size, size), size)
    across = pl.ds(pl.multiple_of((1 - ids[3]) * size, size), size)
    return nn(x[:, own], near[...]) + nn(x[:, across], far[...])


def project_other_kernel(ids, mine, got, gain, shift, near, p0, p1, p2, p3, bias, block, normed, out, far_s):
    @pl.when(pl.program_id(0) == 0)
    def _():
        x = jnp.where(ids[1] == 1, got[...], mine[...])
        block[...] = x
        hat, unused = row_stats(x.astype(F32))
        normed[...] = (hat * gain[...] + shift[...]).astype(BF)

    lay_pieces(ids, far_s, (p0, p1, p2, p3))
    out[...] = (by_rows(ids, normed, near, far_s) + bias[...]).astype(BF)


def project_other(ids, mine, mine_slot, got, got_slot, gain, shift, near, far, bias):
    rows, width = mine.shape[1:]
    inner = width // 2
    columns = lambda i, ids: (0, 2 * i + 1 - ids[0])
    return call(
        project_other_kernel,
        ids,
        (3,),
        [
            slot_of((rows, width), mine_slot),
            slot_of((rows, width), got_slot),
            whole((1, width)),
            whole((1, width)),
            pl.BlockSpec((inner, inner), columns),
        ]
        + [pl.BlockSpec((inner // 4, inner), columns)] * 4
        + [pl.BlockSpec((1, inner), columns)],
        [whole((rows, width)), whole((rows, width)), pl.BlockSpec((rows, inner), lambda i, ids: (0, i))],
        [
            jax.ShapeDtypeStruct((rows, width), BF),
            jax.ShapeDtypeStruct((rows, width), BF),
            jax.ShapeDtypeStruct((rows, 3 * inner), BF),
        ],
        (mine, got, gain, shift, near, *far, bias),
        scratch=[pltpu.VMEM((inner, inner), BF)],
    )


def project_mine_kernel(ids, normed, near, p0, p1, p2, p3, bias, out, far_s):
    lay_pieces(ids, far_s, (p0, p1, p2, p3))
    out[...] = (by_rows(ids, normed, near, far_s) + bias[...]).astype(BF)


def project_mine(ids, normed, near, far, bias):
    rows, width = normed.shape
    inner = width // 2
    columns = lambda i, ids: (0, 2 * i + ids[0])
    return call(
        project_mine_kernel,
        ids,
        (3,),
        [whole((rows, width)), pl.BlockSpec((inner, inner), columns)]
        + [pl.BlockSpec((inner // 4, inner), columns)] * 4
        + [pl.BlockSpec((1, inner), columns)],
        pl.BlockSpec((rows, inner), lambda i, ids: (0, i)),
        jax.ShapeDtypeStruct((rows, 3 * inner), BF),
        (normed, near, *far, bias),
        scratch=[pltpu.VMEM((inner, inner), BF)],
    )


def feed_kernel(
    ids, block, ctx_mine, ctx_other, cot_mine, cot_got, out_near, o0, o1, o2, o3, up_near, u0, u1, u2, u3,
    down_near, d0, d1, d2, d3, gain, biases, bias_hidden, *rest,
):
    (
        active, d_pre, normed2, d_out, result, d_branch, d_ctx_mine, d_ctx_other, sums, sum_hidden,
        hidden_s, total_s, d_norm_s, up_far, w_down,
    ) = rest[-15:]
    j = pl.program_id(0)
    half = pl.num_programs(0) // 2
    inner = ctx_mine.shape[1]
    live = ids[2].astype(F32)
    own = pl.ds(pl.multiple_of(ids[3] * inner, inner), inner)
    across = pl.ds(pl.multiple_of((1 - ids[3]) * inner, inner), inner)
    lay_pieces(ids, up_far, (u0, u1, u2, u3))

    out_far = w_down.at[:inner]

    straight = ids[0] == ids[3]

    @pl.when(j == 0)
    def _():
        lay_pieces(ids, out_far, (o0, o1, o2, o3))
        w_mine = jnp.where(straight, out_near[...], out_far[...])
        w_other = jnp.where(straight, out_far[...], out_near[...])
        hidden = block[...].astype(F32) + (nn(ctx_mine[...], w_mine) + nn(ctx_other[...], w_other))
        hidden = hidden + biases[3:4]
        hidden_s[...] = hidden
        hat, unused = row_stats(hidden)
        normed2[...] = (hat * gain[1:2] + biases[4:5]).astype(BF)
        d = (jnp.where(ids[1] == 1, cot_got[...], cot_mine[...]).astype(F32) * live).astype(BF)
        d_out[...] = d

    @pl.when(j < half)
    def _():
        w_down[...] = down_near[...]

    @pl.when(j >= half)
    def _():
        here = ids[4] == j - half
        size = d0.shape[0]
        w_down[pl.ds(pl.multiple_of(ids[0] * size, size), size)] = jnp.where(here, d0[...], d1[...])
        w_down[pl.ds(pl.multiple_of((1 - ids[0]) * size, size), size)] = jnp.where(here, d2[...], d3[...])

    rows = block.shape[0]
    parts = (slice(0, rows // 32 * 16), slice(rows // 32 * 16, rows))

    def begin(part):
        pre = nn(normed2[part, own], up_near[...]) + nn(normed2[part, across], up_far[...])
        return pre, nt(d_out[part], w_down[...])

    def middle(part, pre, d_act):
        pre = pre + bias_hidden[...]
        phi = 0.5 + 0.5 * lax.erf(pre * 0.7071067811865476)
        act = (pre * phi).astype(BF)
        active[part] = act
        slope = phi + pre * (jnp.exp2(pre * pre * (-0.5 * LOG2E)) * 0.3989422804014327)
        dp = d_act * slope
        total = jnp.sum(dp, 0, keepdims=True)
        dp = dp.astype(BF)
        d_pre[part] = dp
        return act, dp, total

    def end(part, act, dp):
        total_s[part] += nn(act, w_down[...])
        d_norm_s[part, own] += nt(dp, up_near[...])
        d_norm_s[part, across] += nt(dp, up_far[...])

    @pl.when(j == 0)
    def _():
        total_s[...] = jnp.zeros_like(total_s)
        d_norm_s[...] = jnp.zeros_like(d_norm_s)

    first, second = parts
    begun = begin(first)
    begun_second = begin(second)
    act, dp, total = middle(first, *begun)
    end(first, act, dp)
    act, dp, total_second = middle(second, *begun_second)
    end(second, act, dp)
    sum_hidden[...] = jnp.broadcast_to(total + total_second, sum_hidden.shape)

    @pl.when(j == pl.num_programs(0) - 1)
    def _():
        hidden = hidden_s[...]
        result[...] = ((hidden + total_s[...] + biases[5:6]) * live).astype(BF)
        hat, inverse = row_stats(hidden)
        d_norm = d_norm_s[...]
        weighted = d_norm * gain[1:2]
        first = jnp.mean(weighted, -1, keepdims=True)
        second = jnp.mean(weighted * hat, -1, keepdims=True)
        d = d_out[...].astype(F32)
        branch = (d + inverse * (weighted - first - hat * second)).astype(BF)
        d_branch[...] = branch
        sums[...] = jnp.concatenate(
            [
                jnp.sum(d_norm * hat, 0, keepdims=True),
                jnp.sum(d_norm, 0, keepdims=True),
                jnp.sum(branch.astype(F32), 0, keepdims=True),
                jnp.sum(d, 0, keepdims=True),
                jnp.zeros((4, d.shape[1]), F32),
            ],
            0,
        )
        lay_pieces(ids, out_far, (o0, o1, o2, o3))
        w_mine = jnp.where(straight, out_near[...], out_far[...])
        w_other = jnp.where(straight, out_far[...], out_near[...])
        d_ctx_mine[...] = nt(branch, w_mine).astype(BF)
        d_ctx_other[...] = nt(branch, w_other).astype(BF)


def feed(ids, slot, slots, block, ctx_mine, ctx_other, cot_mine, cot_got, got_slot, w_out, w_up, w_down, far, far_down, gain, biases, bias_hidden, before):
    rows, width = block.shape
    inner = width // 2
    ff = w_up.shape[1]
    chunk = width
    steps = ff // chunk
    one = dict(pipeline_mode=pl.Buffered(1))
    full = whole((rows, width), **one)
    part = whole((rows, inner), **one)
    place = lambda j, ids: (0, (ids[3] * (steps // 2) + j) % steps)
    columns = pl.BlockSpec((rows, chunk), place)
    one_slot = lambda shape, at=slot: pl.BlockSpec((None,) + shape, lambda *_: (at, 0, 0), **one)
    wide = jax.ShapeDtypeStruct((rows, width), BF)
    args = (
        block, ctx_mine, ctx_other, cot_mine, cot_got, w_out, *far, w_up, *far, w_down, *far_down, gain, biases, bias_hidden,
    )
    return call(
        feed_kernel,
        ids,
        (steps,),
        [full, part, part, one_slot((rows, width)), one_slot((rows, width), got_slot), whole((inner, width), **one)]
        + [pl.BlockSpec((inner // 4, width), lambda j, ids: (steps, 0), **one)] * 4
        + [pl.BlockSpec((inner, chunk), place)]
        + [pl.BlockSpec((inner // 4, chunk), lambda j, ids: (place(j, ids)[1], 0))] * 4
        + [pl.BlockSpec((chunk, width), lambda j, ids: (jnp.minimum(j, steps // 2 - 1), 0), **one)]
        + [whole((ff // 8, width), **one)] * 4
        + [whole(gain.shape), whole(biases.shape), pl.BlockSpec((1, chunk), place)]
        + [pl.BlockSpec(memory_space=pl.ANY)] * len(before),
        [
            columns, columns, full, full, full, full, part, one_slot((rows, inner)),
            whole((8, width)),
            pl.BlockSpec((8, chunk), place),
        ],
        [
            jax.ShapeDtypeStruct((rows, ff), BF), jax.ShapeDtypeStruct((rows, ff), BF),
            wide, wide, wide, wide,
            jax.ShapeDtypeStruct((rows, inner), BF), jax.ShapeDtypeStruct((slots, rows, inner), BF),
            jax.ShapeDtypeStruct((8, width), F32), jax.ShapeDtypeStruct((8, ff), F32),
        ],
        args + tuple(before),
        scratch=[pltpu.VMEM((rows, width), F32)] * 3
        + [pltpu.VMEM((inner, chunk), BF), pltpu.VMEM((chunk, width), BF)],
        flops=COST,
        limit=62,
        aliases=[(1 + len(args), 7)] if before else (),
    )


def outer_sum(left, right):
    return tn(jnp.concatenate(left), jnp.concatenate(right))


def put_block(ids, outs, rec, piece, x, y, z, rows):
    place = 2 * (x != ids[3]).astype(jnp.int32) + (y != ids[4]).astype(jnp.int32)
    if rec is None:
        outs[0][place, z, rows] = piece.astype(BF)
        return
    for i, out in enumerate(outs):

        @pl.when(place == i)
        def _(i=i, out=out):
            out[z, rows] = (piece + rec[i, z, rows].astype(F32)).astype(BF)


def split_refs(refs, counts):
    parts, at = [], 0
    for count in counts:
        parts.append(refs[at : at + count])
        at += count
    rest = refs[at:]
    return parts + ([None, rest] if len(rest) == 1 else [rest[0], rest[-4:]])


def grad_down_kernel(ids, *refs, slots):
    left, right, rec, outs = split_refs(refs, (slots, slots))
    step = pl.program_id(0)
    x = jnp.where(step == 0, 1 - ids[3], ids[3])
    total = outer_sum([a[...] for a in left], [b[...] for b in right])
    chips, rows, cols = outs[0].shape[-3:]
    parts = total.shape[1] // cols
    rows = rows // parts
    for z in range(chips):
        for y in range(2):
            at = (2 * z + y) * rows
            for part in range(parts):
                piece = total[at : at + rows, part * cols : (part + 1) * cols]
                put_block(ids, outs, rec, piece, x, jnp.int32(y), z, slice(part * rows, (part + 1) * rows))


def grad_up_kernel(ids, *refs, slots):
    left, first, last, rec, outs = split_refs(refs, (slots, slots, slots))
    z = pl.program_id(0)
    right = [jnp.concatenate([a[...], b[...]], 1) for a, b in zip(first, last)]
    total = outer_sum([a[...] for a in left], right)
    rows, cols = outs[0].shape[-2:]
    for x in range(2):
        for y in range(2):
            piece = total[y * rows : (y + 1) * rows, x * cols : (x + 1) * cols]
            put_block(ids, outs, rec, piece, jnp.int32(x), jnp.int32(y), z, slice(0, rows))


def grad_out_kernel(ids, *refs, slots):
    left, mine, other, rec, outs = split_refs(refs, (slots, slots, slots))
    right = [jnp.concatenate([a[...], b[...]], 1) for a, b in zip(mine, other)]
    total = outer_sum([a[...] for a in left], right)
    chips, rows, cols = outs[0].shape[-3:]
    for near in range(2):
        x = ids[0] if near == 0 else 1 - ids[0]
        for z in range(chips):
            for y in range(2):
                at = (2 * z + y) * rows
                piece = total[at : at + rows, near * cols : (near + 1) * cols]
                put_block(ids, outs, rec, piece, x, jnp.int32(y), z, slice(0, rows))


def grad_qkv_kernel(ids, *refs, slots, steps):
    mine, other, first, last, rec, outs = split_refs(refs, (slots, slots, slots, slots))
    right = [jnp.concatenate([a[...], b[...]], 1) for a, b in zip(first, last)]
    near = outer_sum([a[...] for a in mine], right)
    far = outer_sum([a[...] for a in other], right)
    total = jnp.concatenate([jnp.where(ids[0] == 0, near, far), jnp.where(ids[0] == 0, far, near)])
    chips, rows, cols = outs[0].shape[-3:]
    span = total.shape[0]
    for step in range(steps):

        @pl.when(pl.program_id(0) == step)
        def _(step=step):
            for block in range(2 * chips):
                begin = max(block * rows, step * span)
                end = min((block + 1) * rows, (step + 1) * span)
                if begin >= end:
                    continue
                for x in range(2):
                    piece = total[begin - step * span : end - step * span, x * cols : (x + 1) * cols]
                    put_block(
                        ids, outs, rec, piece, jnp.int32(x), jnp.int32(block % 2), block // 2,
                        slice(begin - block * rows, end - block * rows),
                    )


def grad_call(kernel, ids, grid, groups, shape, rec, flops, joint=None, **kw):
    specs, args = [], []
    for arrays, block, index in groups:
        specs += [pl.BlockSpec(block, index)] * len(arrays)
        args += arrays
    if rec is None:
        out_specs, out_shapes, aliases = whole(shape, pipeline_mode=pl.Buffered(1)), jax.ShapeDtypeStruct(shape, BF), ()
    else:
        specs.append(whole(shape, pipeline_mode=pl.Buffered(1)))
        args.append(rec)
        all_rows, at, arrays = joint
        out_specs = [pl.BlockSpec(shape[1:], lambda *_: (0, at, 0), pipeline_mode=pl.Buffered(1))] * 4
        out_shapes = [jax.ShapeDtypeStruct((shape[1], all_rows, shape[3]), BF)] * 4
        aliases = [(1 + len(args) + i, i) for i in range(len(arrays))]
        specs += [pl.BlockSpec(memory_space=pl.ANY)] * len(arrays)
        args += arrays
    return call(
        functools.partial(kernel, slots=len(groups[0][0]), **kw),
        ids, grid, specs, out_specs, out_shapes, tuple(args), flops=flops, aliases=aliases,
    )


def column_half(ids, rec):
    return 1 - ids[0] if rec is None else ids[0]


def grad_down_part(ids, chips, d_out, active, rec, joint=None):
    rows, width = d_out[0].shape
    ff = active[0].shape[1]
    cols = ff // 4
    parts = 4 * cols // width
    block = lambda i, ids: (0, 2 * jnp.where(i == 0, 1 - ids[3], ids[3]) + column_half(ids, rec))
    groups = [(d_out, (rows, width), lambda i, ids: (0, 0)), (active, (rows, cols), block)]
    shape = (4, chips, parts * width // (2 * chips), cols // parts)
    return grad_call(grad_down_kernel, ids, (2,), groups, shape, rec, COST // 2, joint)


def grad_up_part(ids, chips, d_pre, normed, rec, joint=None):
    rows, width = normed[0].shape
    ff = d_pre[0].shape[1]
    cols = width // 4
    groups = [
        (d_pre, (rows, ff // chips), lambda i, ids: (0, i)),
        (normed, (rows, cols), lambda i, ids: (0, column_half(ids, rec))),
        (normed, (rows, cols), lambda i, ids: (0, 2 + column_half(ids, rec))),
    ]
    return grad_call(grad_up_kernel, ids, (chips,), groups, (4, chips, ff // (2 * chips), cols), rec, COST // 2, joint)


def grad_out_part(ids, chips, d_branch, mine, other, rec, joint=None):
    rows, width = d_branch[0].shape
    cols = width // 4
    half = lambda i, ids: (0, column_half(ids, rec))
    groups = [(d_branch, (rows, width), lambda i, ids: (0, 0)), (mine, (rows, cols), half), (other, (rows, cols), half)]
    return grad_call(grad_out_kernel, ids, (1,), groups, (4, chips, width // (2 * chips), cols), rec, COST // 2, joint)


def grad_qkv_part(ids, chips, mine, other, normed, rec, joint=None):
    rows, width = normed[0].shape
    cols = width // 4
    columns = lambda i, ids: (0, i)
    groups = [
        (mine, (rows, width // 2), columns),
        (other, (rows, width // 2), columns),
        (normed, (rows, cols), lambda i, ids: (0, column_half(ids, rec))),
        (normed, (rows, cols), lambda i, ids: (0, 2 + column_half(ids, rec))),
    ]
    return grad_call(
        grad_qkv_kernel, ids, (3,), groups, (4, chips, 3 * width // (2 * chips), cols), rec, COST // 2, joint, steps=3
    )


def add_kernel(ids, *refs):
    refs[-1][...] = sum(term[...].astype(F32) for term in refs[:-1]).astype(BF)


def add_chips(ids, terms, chips, rows):
    cols = terms[0].shape[1]
    return call(
        add_kernel,
        ids,
        (chips,),
        [pl.BlockSpec((rows, cols), lambda i, ids: (ids[5] ^ i, 0))] * len(terms),
        pl.BlockSpec((None, rows, cols), lambda i, ids: (i, 0, 0)),
        jax.ShapeDtypeStruct((chips, rows, cols), BF),
        tuple(terms),
    )


def finish_kernel(
    ids, d_mine, d_other, mine_near, m0, m1, m2, m3, other_near, o0, o1, o2, o3, block, d_hidden, gain,
    row_grad, sums, sum_mine, sum_other, total_s, mine_far, other_far,
):
    i = pl.program_id(0)
    size = mine_near.shape[0]
    lay_pieces(ids, mine_far, (m0, m1, m2, m3))
    lay_pieces(ids, other_far, (o0, o1, o2, o3))
    own = pl.ds(pl.multiple_of(ids[3] * size, size), size)
    across = pl.ds(pl.multiple_of((1 - ids[3]) * size, size), size)
    term = nt(d_mine[...], mine_near[...]) + nt(d_other[...], other_near[...])
    term_far = nt(d_mine[...], mine_far[...]) + nt(d_other[...], other_far[...])
    sum_mine[...] = jnp.broadcast_to(jnp.sum(d_mine[...].astype(F32), 0, keepdims=True), sum_mine.shape)
    sum_other[...] = jnp.broadcast_to(jnp.sum(d_other[...].astype(F32), 0, keepdims=True), sum_other.shape)

    @pl.when(i == 0)
    def _():
        total_s[:, own] = term
        total_s[:, across] = term_far

    @pl.when(i > 0)
    def _():
        total_s[:, own] += term
        total_s[:, across] += term_far

    @pl.when(i == pl.num_programs(0) - 1)
    def _():
        hat, inverse = row_stats(block[...].astype(F32))
        d_norm = total_s[...]
        weighted = d_norm * gain[0:1]
        first = jnp.mean(weighted, -1, keepdims=True)
        second = jnp.mean(weighted * hat, -1, keepdims=True)
        row_grad[...] = (d_hidden[...].astype(F32) + inverse * (weighted - first - hat * second)).astype(BF)
        sums[...] = jnp.concatenate(
            [jnp.sum(d_norm * hat, 0, keepdims=True), jnp.sum(d_norm, 0, keepdims=True), jnp.zeros((6, d_norm.shape[1]), F32)], 0
        )


def finish(ids, d_mine, d_other, near, far, block, d_hidden, gain):
    rows, width = block.shape
    inner = width // 2
    full = whole((rows, width))
    part = pl.BlockSpec((rows, inner), lambda i, ids: (0, i))
    row = pl.BlockSpec((8, inner), lambda i, ids: (0, i))
    mine = lambda i, ids: (0, 2 * i + ids[0])
    other = lambda i, ids: (0, 2 * i + 1 - ids[0])
    return call(
        finish_kernel,
        ids,
        (3,),
        [
            part, part,
            pl.BlockSpec((inner, inner), mine), *[pl.BlockSpec((inner // 4, inner), mine)] * 4,
            pl.BlockSpec((inner, inner), other), *[pl.BlockSpec((inner // 4, inner), other)] * 4,
            full, full, whole(gain.shape),
        ],
        [full, whole((8, width)), row, row],
        [
            jax.ShapeDtypeStruct((rows, width), BF), jax.ShapeDtypeStruct((8, width), F32),
            jax.ShapeDtypeStruct((8, 3 * inner), F32), jax.ShapeDtypeStruct((8, 3 * inner), F32),
        ],
        (d_mine, d_other, near, *far, near, *far, block, d_hidden, gain),
        scratch=[pltpu.VMEM((rows, width), F32)] + [pltpu.VMEM((inner, inner), BF)] * 2,
        flops=COST,
    )


def swap_axis(x, axis, step=1):
    size = lax.axis_size(axis)
    return lax.ppermute(x, axis, [(i, i ^ step) for i in range(size)])


def swap_across(x):
    return lax.ppermute(x, ("mid", "grp"), [(0, 3), (1, 2), (2, 1), (3, 0)])


def swap_owner(x, chips):
    pairs = []
    for k in range(2 * chips):
        pairs += [(4 * k + 1, 4 * k + 2), (4 * k + 2, 4 * k + 1)]
    return lax.ppermute(x, AXES, pairs)


def after(values, first):
    return lax.optimization_barrier((values, first))[0]


def in_order(index, mine, other, axis=0):
    return jnp.concatenate([jnp.where(index == 0, mine, other), jnp.where(index == 0, other, mine)], axis)


def own_half(x, index, axis=0):
    size = x.shape[axis] // 2
    return lax.dynamic_slice_in_dim(x, index * size, size, axis)


def send_piece(piece):
    return swap_axis(piece, "grp")


def own_piece(shard):
    place = 2 * lax.axis_index("mid") + lax.axis_index("core")
    part = shard.shape[0] // 4
    return lax.dynamic_slice_in_dim(shard, place * part, part, 0)


def as_lines(x, cols):
    parts = []
    for _ in range(2):
        part = lax.reduce_precision(x, 8, 7)
        parts.append(part.astype(BF))
        x = x - part
    return jnp.concatenate(parts).reshape(-1, cols)


def from_lines(lines, shape):
    return lines.astype(F32).reshape((2,) + shape).sum(0)


def send_sums(part):
    return [part[0], swap_axis(part[1], "mid"), swap_axis(part[2], "grp"), swap_across(part[3])]


def send_chips(part):
    return [part[0]] + [swap_axis(part[i], "z", i) for i in range(1, lax.axis_size("z"))]


def settle(total, parts, core):
    mine = jnp.concatenate([lax.dynamic_index_in_dim(part, core, 0, False) for part in parts])
    other = jnp.concatenate([lax.dynamic_index_in_dim(part, 1 - core, 0, False) for part in parts])
    return mine, swap_axis(other, "core")


def body(chips, clips, clip_count, cotangent, norm_gain, bias_d, bias_ff, w_qkv, w_o, w_up, w_down):
    core, x, y, z = (lax.axis_index(axis) for axis in ("core", "grp", "mid", "z"))
    slots, half, width = clips.shape
    inner = width // 2
    ff = w_up.shape[1]
    swap = (core != x).astype(jnp.int32)

    qkv_piece = own_piece(w_qkv)
    small = jnp.concatenate([norm_gain.reshape(-1), bias_d.reshape(-1), bias_ff]).reshape(-1, 128)
    qkv_0 = send_piece(qkv_piece)
    got_small = swap_axis(after(small, qkv_piece), "grp")
    got_first = swap_owner(after(clips[:1], qkv_piece), chips)
    other_count = swap_axis(clip_count, "core")
    qkv_1 = swap_axis(qkv_0, "mid")
    qkv_2 = swap_axis(qkv_0, "core")
    rest = after(clips[1:], qkv_0)
    got_rest = swap_owner(rest, chips)
    piece = own_piece(w_up).reshape(-1, ff // width, width).transpose(1, 0, 2).reshape(-1, width)
    piece = jnp.concatenate([piece, own_piece(w_o)])
    down_piece = own_piece(w_down)
    qkv_3 = swap_axis(qkv_1, "core")
    qkv_far = (qkv_0, qkv_1, qkv_2, qkv_3)
    piece, down_piece = after((piece, down_piece), qkv_1)
    far_0 = send_piece(piece)
    down_0 = send_piece(down_piece)

    pair = in_order(x, small[None], got_small[None]).reshape(2, -1).astype(F32)
    gains = pair[:, : 2 * inner].reshape(2, 2, inner).transpose(1, 0, 2).reshape(2, width)
    biases = pair[:, 2 * inner : 8 * inner].reshape(2, 6, inner).transpose(1, 0, 2).reshape(6, width)
    bias_hidden = pair[:, 8 * inner :].reshape(1, -1)
    count = jnp.where(swap == 1, other_count, clip_count)[0]
    qkv_bias = jnp.concatenate([biases[1], jnp.zeros_like(biases[1]), biases[2]])[None]
    ids = [jnp.stack([core, swap, (count > s).astype(jnp.int32), x, y, z]).astype(jnp.int32) for s in range(slots)]

    cot_first, cot_others = after((cotangent[:1], cotangent[1:]), qkv_0)
    got_first = after(got_first, (rest, piece, down_piece, cot_first, cot_others))
    blocks, normed, saved, ctx_mine, ctx_other = [], [], [], [], []
    for s in range(slots):
        got, slot = (got_first, 0) if s == 0 else (got_rest, s - 1)
        block, norm, other = project_other(ids[s], clips, s, got, slot, gains[0:1], biases[0:1], w_qkv, qkv_far, qkv_bias)
        received = swap_axis(other, "core")
        mine = project_mine(ids[s], norm, w_qkv, qkv_far, qkv_bias)
        here, there, r_here, r_there, weights, weights_rem = attend(mine, received)
        saved.append((mine, received, here, there, r_here, r_there, weights, weights_rem))
        ctx_mine.append(here)
        ctx_other.append(swap_axis(there, "core"))
        blocks.append(block)
        normed.append(norm)
        if s == 0:
            down_0 = after(down_0, here)
            down_1 = swap_axis(down_0, "mid")
            down_2 = swap_axis(down_0, "core")
            got_rest = after(got_rest, (here, down_0))
        elif s == 1:
            down_1, far_0 = after((down_1, far_0), here)
            down_3 = swap_axis(down_1, "core")
            far_1 = swap_axis(far_0, "mid")
            far_2 = swap_axis(far_0, "core")
            got_rest = after(got_rest, (here, down_1, far_0))
        elif s == 2:
            far_1 = after(far_1, here)
            far_3 = swap_axis(far_1, "core")
    far = (far_0, far_1, far_2, far_3)
    far_down = (down_0, down_1, down_2, down_3)

    others = swap_owner(after(cot_others, here), chips)
    got_cot = [(swap_owner(cot_first, chips), 0)] + [(others, s - 1) for s in range(1, slots)]
    fed, got_result = [], []
    before = ()
    for s in range(slots):
        if s == 2:
            got_cot[s] = (after(others, got_result[0]), s - 1)
        fed.append(
            feed(
                ids[s], s, slots, blocks[s], ctx_mine[s], ctx_other[s], cotangent, *got_cot[s], w_o, w_up, w_down, far, far_down,
                gains, biases, bias_hidden, before,
            )
        )
        before = (fed[-1][7],)
        got_result.append(swap_owner(fed[-1][4], chips))
    active, d_pre, normed2, d_out, result, d_branch, d_ctx_mine, d_ctx_other, sums2, sums_hidden = map(list, zip(*fed))
    d_ctx_got = swap_axis(d_ctx_other[-1], "core")

    sent_down = grad_down_part(ids[0], chips, after(d_out, got_result[1]), active, None)
    sent_up = grad_up_part(ids[0], chips, d_pre, normed2, None)
    sent_out = grad_out_part(ids[0], chips, d_branch, ctx_mine, ctx_other, None)
    rows_down, rows_up, rows_out = (part.shape[2] for part in (sent_down, sent_up, sent_out))
    rows = rows_down + rows_up + rows_out
    joint = grad_down_part(ids[0], chips, d_out, active, swap_axis(sent_down, "core"), (rows, 0, []))
    joint = grad_up_part(
        ids[0], chips, d_pre, normed2, swap_axis(sent_up, "core"),
        (rows, rows_down // rows_up, joint),
    )
    joint = grad_out_part(
        ids[0], chips, d_branch, ctx_mine, ctx_other, swap_axis(sent_out, "core"),
        (rows, (rows_down + rows_up) // rows_out, joint),
    )
    cols = joint[0].shape[-1]
    sums = send_sums([part.reshape(-1, cols) for part in joint])
    early = jnp.concatenate([sum(sums2)[:4], sum(sums_hidden)[0].reshape(-1, width)])

    got_rows = []
    d_mine, d_other, row_grads, sums1, sums_mine, sums_other = [], [], [], [], [], []

    def complete(s, first):
        row_grad, sum1, sum_mine, sum_other = finish(
            ids[s], d_mine[s], after(d_other[s], first), w_qkv, qkv_far, blocks[s], d_branch[s], gains
        )
        row_grads.append(row_grad)
        sums1.append(sum1)
        sums_mine.append(sum_mine[0])
        sums_other.append(sum_other[0])
        return row_grad

    gate = joint
    for s in range(slots):
        mine, received, here, there, r_here, r_there, weights, weights_rem = saved[s]
        d_here, d_there = attend_back(
            s, mine, received, after(d_ctx_mine[s], gate), d_ctx_got, here, there, r_here, r_there, weights, weights_rem
        )
        d_mine.append(d_here)
        d_other.append(swap_axis(d_there, "core"))
        gate = (d_here,)
        if s == 0:
            sums[3] = after(sums[3], d_here)
            gate = (d_here, sums[3])
        elif s == 1:
            sums = add_chips(ids[0], after(sums, d_here), chips, rows)
            gate = sums
            terms = send_chips(sums)
            gate = (gate, [sums[i] for i in range(chips)])
        if s == 2:
            gate = complete(0, (d_here, terms, got_result[2]))
    got_rows.append(swap_owner(row_grads[0], chips))
    sent_qkv = grad_qkv_part(ids[0], chips, d_mine, after(d_other, gate), normed, None)
    gate = complete(1, sent_qkv)
    got_rows.append(swap_owner(row_grads[1], chips))
    part_qkv = grad_qkv_part(
        ids[0], chips, d_mine, d_other, normed, after(swap_axis(sent_qkv, "core"), (gate, got_rows[0])),
        (sent_qkv.shape[2], 0, []),
    )
    qkv_rows = part_qkv[0].shape[1]
    qkv_terms = send_sums([part.reshape(-1, cols) for part in part_qkv])
    complete(2, (part_qkv, got_rows[1]))
    total1 = sum(sums1)
    total_mine, total_other = sum(sums_mine), sum(sums_other)
    grad_bq = in_order(core, total_mine[:inner], total_other[:inner])
    grad_bv = in_order(core, total_mine[2 * inner :], total_other[2 * inner :])
    lines = jnp.concatenate(
        [jnp.stack([total1[0], early[0], total1[1], grad_bq, grad_bv, early[2], early[1], early[3]]), early[4:]]
    )
    lines = lines + swap_axis(lines, "core")
    shape = lines.shape
    lines = sum(send_sums([lines] * 4))
    got_rows.append(swap_owner(after(row_grads[2], lines), chips))
    sums = add_chips(ids[0], qkv_terms, chips, qkv_rows)
    under = as_lines(lines, cols)
    sends = [jnp.concatenate([sums[i], under]) for i in range(chips)]
    qkv_terms = send_chips(sends)
    total = sum(term.astype(F32) for term in after(terms, sends))
    chunks = rows_down // rows_out
    down = total[:rows_down].reshape(chunks, 2, -1, cols).transpose(1, 0, 2, 3).reshape(2, -1, cols)
    up = total[rows_down : rows_down + rows_up].reshape(2, -1, cols)
    out = total[rows_down + rows_up :].reshape(2, -1, cols)
    mine, other = settle(total, (down, up, out), core)
    whole_rows = in_order(core, mine, other, 1)
    n_down, n_up = rows_down // 2, rows_up // 2
    own_down = in_order(core, mine[:n_down].reshape(chunks, -1, cols), other[:n_down].reshape(chunks, -1, cols))
    grad_down = own_down.transpose(0, 2, 1).reshape(2 * chunks * cols, -1)
    grad_up = whole_rows[n_down : n_down + n_up].T
    grad_out = whole_rows[n_down + n_up :].T

    outs = jnp.stack([jnp.where(swap == 1, after(got_result[s], sends), result[s]) for s in range(slots)])
    input_grad = jnp.stack([jnp.where(swap == 1, after(got_rows[s], sends), row_grads[s]) for s in range(slots)]).astype(F32)
    qkv_terms = after(qkv_terms, input_grad)
    lines = sum(from_lines(term[qkv_rows:], shape) for term in qkv_terms)
    columns = own_half(lines[:8], x, 1)
    hidden_part = own_half(lines[8:], x).reshape(-1)
    total = sum(term[:qkv_rows].astype(F32) for term in qkv_terms)
    mine, other = settle(total, (total.reshape(2, -1, cols),), core)
    grad_qkv = in_order(core, mine, other, 1).T
    return (outs, input_grad, columns[:2], columns[2:], hidden_part, grad_qkv, grad_out, grad_up, grad_down)


def solution(mesh):
    in_specs = (
        P("rep", "grp", None),
        P("rep"),
        P("rep", "grp", None),
        P(None, "grp"),
        P(None, "grp"),
        P("grp"),
        P("grp", None),
        P("grp", None),
        P("grp", None),
        P("grp", None),
    )
    out_specs = (
        P("rep", "grp", None),
        P("rep", "grp", None),
        P(None, "grp"),
        P(None, "grp"),
        P("grp"),
        P("grp", "rep"),
        P("grp", "rep"),
        P("grp", "rep"),
        P("grp", "rep"),
    )
    if mesh.shape["grp"] != 2 or mesh.shape["rep"] != 16:
        return jax.shard_map(plain_body, mesh=mesh, in_specs=in_specs, out_specs=out_specs, check_vma=False)
    chips = mesh.shape["rep"] // 4
    split = Mesh(mesh.devices.reshape(chips, 2, 2, 2), AXES)
    rep = lambda spec: P(*[AXES[:3] if axis == "rep" else axis for axis in spec])
    return jax.shard_map(
        functools.partial(body, chips),
        mesh=split,
        in_specs=tuple(rep(spec) for spec in in_specs),
        out_specs=tuple(rep(spec) for spec in out_specs),
        check_vma=False,
    )
```
